256 devices in a mesh: dp: 32 (over y_hi, z, core), mp: 8 (over x, y_lo).
Axes of the slice: x: 4, y: 4 (y_hi: 2, y_lo: 2; y = y_hi * 2 + y_lo), z: 8, core: 2. Of those that a mesh axis runs over, the one named last changes fastest.
Arguments:
- features: bfloat16 [32768, 4096], P('dp'), may hold values from -13 to 13
- out_grads: bfloat16 [32768, 4096], P('dp', 'mp'), may hold values from -6 to 6
- counts: int32 [32], P('dp'), may hold values from 341 to 1024, as said below
- factor_old: float32 [8, 32, 2, 512, 512], P('mp', 'dp'), may hold values from -1 to 3, as said below
- inverse_old: float32 [8, 32, 2, 512, 512], P('mp', 'dp'), may hold values from -1 to 3, as said below
- old_owner: int32 [8, 2], replicated, may hold values from 0 to 31, as said below
- new_owner: int32 [8, 2], replicated, may hold values from 0 to 31, as said below
Outputs:
- factor_new: float32 [8, 32, 512, 512], P('mp', 'dp')
- inverse_new: float32 [8, 32, 512, 512], P('mp', 'dp')
- update: float32 [4096, 4096], P('dp', 'mp')
The draws below stay inside these ranges and needn't reach their ends.
Inputs may be any that keep to these rules, and one draw needn't show every extreme that they name: `counts`: some dp index has all 1024 rows valid. `factor_old`: Symmetric. `inverse_old`: Symmetric. `old_owner`: A dp index holds at most both blocks of one mp index; in every draw some mp index has both blocks at one dp index. `new_owner`: the two blocks of one mp index have different new owners.
All inputs are finite; a program needn't handle non-finite values.
Results may differ from the reference program's by a relative error of at most 0.0057.
Values may be sent and summed in bfloat16 or wider, within the bound.
No kernel may reach another device: no remote copies, remote signals or barrier semaphores. Data moves between devices by JAX's collectives and lax.ppermute only.
A program may use at most 128 MiB of HBM per device.

```python
import math
import jax
import jax.numpy as jnp
from jax import lax

BLOCK = 512
TOK_DEV = 1024
DA = 4096
FFW = 4096
TOKENS = 32768
N_DP = 32
N_MP = 8


def diagonal_scales(key):
    return jnp.exp(jax.random.uniform(key, (N_MP, N_DP, 2, BLOCK), jnp.float32, math.log(0.5), math.log(2.0)))


def symmetric_noise(noise, spread):
    return spread / math.sqrt(2.0 * BLOCK) * (noise + jnp.swapaxes(noise, -1, -2))


def place_value(orders, row_pick, value, position):
    column_ids = jnp.arange(orders.shape[1], dtype=jnp.int32)[None, :]
    row_ids = jnp.arange(orders.shape[0], dtype=jnp.int32)[:, None]
    current = orders[:, position][:, None]
    placed = jnp.where(orders == value, current, jnp.where(column_ids == position, value, orders))
    return jnp.where(row_ids == row_pick, placed, orders)


def draw_features(key, part):
    key = jax.random.fold_in(key, 1)
    first_key, second_key, third_key = jax.random.split(key, 3)
    row_scale = jnp.exp(jax.random.uniform(second_key, (TOKENS, 1), jnp.float32, math.log(0.4), math.log(1.6)))
    col_scale = jnp.exp(jax.random.uniform(third_key, (1, DA), jnp.float32, math.log(0.4), math.log(1.6)))
    values = jnp.clip(jax.random.normal(first_key, (TOKENS, DA), jnp.float32), -5.0, 5.0) * row_scale
    return (values * col_scale).astype(jnp.bfloat16)


def draw_counts(key, part):
    key = jax.random.fold_in(key, 2)
    index_list = jnp.arange(N_DP, dtype=jnp.int32)
    base_rows = TOK_DEV * (N_DP - 1 + 2 * index_list) // (3 * (N_DP - 1))
    jitter = jax.random.randint(key, (N_DP,), 0, TOK_DEV // 8 + 1, dtype=jnp.int32)
    counted = jnp.minimum(base_rows + jitter, TOK_DEV)
    return jnp.where(index_list == N_DP - 1, TOK_DEV, counted).astype(jnp.int32)


def draw_factor_old(key, part):
    scales = diagonal_scales(key)
    key = jax.random.fold_in(key, 3)
    shape_full = (N_MP, N_DP, 2, BLOCK, BLOCK)
    noise = jnp.clip(jax.random.normal(key, shape_full, jnp.float32), -5.0, 5.0)
    identity = jnp.eye(BLOCK, dtype=jnp.float32)
    return symmetric_noise(noise, 0.2) + identity * scales[..., :, None]


def draw_inverse_old(key, part):
    scales = diagonal_scales(key)
    key = jax.random.fold_in(key, 4)
    noise_key, ratio_key = jax.random.split(key)
    shape_full = (N_MP, N_DP, 2, BLOCK, BLOCK)
    ratio = jnp.exp(jax.random.uniform(ratio_key, (N_MP, N_DP, 2, BLOCK), jnp.float32, math.log(0.8), math.log(1.25)))
    noise = jnp.clip(jax.random.normal(noise_key, shape_full, jnp.float32), -5.0, 5.0)
    identity = jnp.eye(BLOCK, dtype=jnp.float32)
    return symmetric_noise(noise, 0.15) + identity * (ratio / scales)[..., :, None]


def draw_old_owner(key, part):
    key = jax.random.fold_in(key, 5)
    perm_key, share_key, force_key = jax.random.split(key, 3)
    orders = jax.vmap(lambda sub_key: jax.random.permutation(sub_key, N_DP))(jax.random.split(perm_key, N_MP)).astype(jnp.int32)
    shared = jax.random.randint(share_key, (N_MP,), 0, 2, dtype=jnp.int32)
    forced = jax.random.randint(force_key, (), 0, N_MP, dtype=jnp.int32)
    orders = place_value(orders, forced, N_DP - 1, 0)
    shared = jnp.where(jnp.arange(N_MP, dtype=jnp.int32) == forced, 1, shared)
    second = jnp.where(shared == 1, orders[:, 0], orders[:, 1])
    return jnp.stack([orders[:, 0], second], axis=1).astype(jnp.int32)


def draw_new_owner(key, part):
    key = jax.random.fold_in(key, 6)
    perm_key, force_key = jax.random.split(key)
    orders = jax.vmap(lambda sub_key: jax.random.permutation(sub_key, N_DP))(jax.random.split(perm_key, N_MP)).astype(jnp.int32)
    forced = jax.random.randint(force_key, (), 0, N_MP, dtype=jnp.int32)
    orders = place_value(orders, forced, N_DP - 1, 0)
    orders = place_value(orders, forced, 0, 1)
    return orders[:, :2].astype(jnp.int32)


def block_levels(own_key, shape, cuts, smallest, largest):
    gain = 1.0
    for axis_at, blocks in cuts:
        draws = jax.random.uniform(jax.random.fold_in(jax.random.fold_in(own_key, 6), axis_at), (blocks,), jnp.float32, smallest / len(cuts), largest / len(cuts))
        gain = gain * jnp.repeat(jnp.exp(draws), shape[axis_at] // blocks).reshape((-1,) + (1,) * (len(shape) - 1 - axis_at))
    return gain


def normal_values(own_key, dims, width, bound, cuts=(), kind=jnp.bfloat16):
    array = width * jax.random.normal(own_key, dims, jnp.float32)
    if cuts:
        array = array * block_levels(own_key, dims, cuts, -0.22, 0.18)
    return jnp.clip(array, -bound, bound).astype(kind)


def setup_inputs(seed: int = 0) -> dict:
    streams_of = jax.random.split(jax.random.key(seed), 8)
    features = draw_features(jax.random.fold_in(streams_of[7], 71), 0)
    out_grads = normal_values(streams_of[1], (TOKENS, FFW), 1.0, 6.0, ((0, 32), (1, 8)))
    counts = draw_counts(jax.random.fold_in(streams_of[7], 71), 0)
    factor_old = draw_factor_old(jax.random.fold_in(streams_of[7], 71), 0)
    inverse_old = draw_inverse_old(jax.random.fold_in(streams_of[7], 71), 0)
    old_owner = draw_old_owner(jax.random.fold_in(streams_of[7], 71), 0)
    new_owner = draw_new_owner(jax.random.fold_in(streams_of[7], 71), 0)
    return {"features": features, "out_grads": out_grads, "counts": counts, "factor_old": factor_old, "inverse_old": inverse_old, "old_owner": old_owner, "new_owner": new_owner}


DECAY = 0.9
DAMPING = 0.01

def refresh(stale_factor, stale_inverse, covariance, token_total):
    block_width = stale_factor.shape[0]
    factor = DECAY * stale_factor + (1.0 - DECAY) * covariance / token_total
    damped = factor + DAMPING * jnp.eye(block_width, dtype=jnp.float32)
    inner_prod = jnp.dot(damped, stale_inverse, precision=lax.Precision.HIGHEST)
    inverse = 2.0 * stale_inverse - jnp.dot(stale_inverse, inner_prod, precision=lax.Precision.HIGHEST)
    return (factor, inverse)

def reference(features, out_grads, counts, factor_old, inverse_old, old_owner, new_owner):
    position = jnp.arange(TOKENS, dtype=jnp.int32)
    valid_rows = position % TOK_DEV < counts[position // TOK_DEV]
    token_total = jnp.sum(counts).astype(jnp.float32)
    kept_features = jnp.where(valid_rows[:, None], features, jnp.zeros_like(features))
    kept_grads = jnp.where(valid_rows[:, None], out_grads, jnp.zeros_like(out_grads))
    columns = jnp.arange(N_MP, dtype=jnp.int32)

    def feature_block(column):
        col_start = (column * BLOCK).astype(jnp.int32)
        masked = lax.dynamic_slice_in_dim(kept_features, col_start, BLOCK, 1).astype(jnp.float32)
        plain = lax.dynamic_slice_in_dim(features, col_start, BLOCK, 1).astype(jnp.float32)
        return jnp.dot(masked.T, plain, preferred_element_type=jnp.float32)

    def hidden_block(column):
        col_start = (column * BLOCK).astype(jnp.int32)
        masked = lax.dynamic_slice_in_dim(kept_grads, col_start, BLOCK, 1).astype(jnp.float32)
        plain = lax.dynamic_slice_in_dim(out_grads, col_start, BLOCK, 1).astype(jnp.float32)
        return jnp.dot(masked.T, plain, preferred_element_type=jnp.float32)
    covariances = jnp.stack([lax.map(feature_block, columns), lax.map(hidden_block, columns)], axis=1)
    shared_slot = (old_owner[:, 1] == old_owner[:, 0]).astype(jnp.int32)
    slot_index = jnp.stack([jnp.zeros_like(shared_slot), shared_slot], axis=1)
    stale_factor = factor_old[columns[:, None], old_owner, slot_index]
    stale_inverse = inverse_old[columns[:, None], old_owner, slot_index]
    inner_map = jax.vmap(refresh, in_axes=(0, 0, 0, None))
    fresh_factor, fresh_inverse = jax.vmap(inner_map, in_axes=(0, 0, 0, None))(stale_factor, stale_inverse, covariances, token_total)
    blank_blocks = jnp.zeros((N_MP, N_DP, BLOCK, BLOCK), jnp.float32)
    factor_out = blank_blocks.at[columns[:, None], new_owner].set(fresh_factor)
    inverse_out = blank_blocks.at[columns[:, None], new_owner].set(fresh_inverse)
    rounded_inv = fresh_inverse.astype(jnp.bfloat16)
    gradient = jnp.dot(kept_features.astype(jnp.float32).T, out_grads.astype(jnp.float32), preferred_element_type=jnp.float32)
    grad_round = gradient.astype(jnp.bfloat16)
    left_blocks = rounded_inv[:, 0].astype(jnp.float32)
    right_blocks = rounded_inv[:, 1].astype(jnp.float32)
    half_step = jnp.einsum('cik,ckf->cif', left_blocks, grad_round.reshape(N_MP, BLOCK, FFW).astype(jnp.float32))
    half_step = half_step.reshape(DA, FFW).astype(jnp.bfloat16)
    result = jnp.einsum('ach,chj->acj', half_step.reshape(DA, N_MP, BLOCK).astype(jnp.float32), right_blocks).reshape(DA, FFW)
    curvature = jnp.sum(result * grad_round.astype(jnp.float32))
    clip_scale = jnp.minimum(1.0, jnp.sqrt(DA * FFW / jnp.abs(curvature)))
    return (factor_out, inverse_out, clip_scale * result)
```

```python
import jax
import jax.numpy as jnp
import numpy as np
from jax import lax
from jax.sharding import PartitionSpec as P

DECAY = 0.9
DAMPING = 0.01
TILE = 128
BF16 = jnp.bfloat16
F32 = jnp.float32


def contract_rows(first_rows, second_rows):
    return lax.dot_general(
        first_rows, second_rows, (((0,), (0,)), ((), ())), preferred_element_type=F32
    )


def upper_pairs(tiles):
    return [(a, b) for a in range(tiles) for b in range(a, tiles)]


def pack_upper(block):
    tiles = block.shape[0] // TILE
    return jnp.concatenate(
        [
            block[a * TILE : (a + 1) * TILE, b * TILE : (b + 1) * TILE]
            for a, b in upper_pairs(tiles)
        ],
        axis=0,
    )


def unpack_upper(packed, width):
    tiles = width // TILE
    at = {pair: n for n, pair in enumerate(upper_pairs(tiles))}

    def tile(a, b):
        n = at[(min(a, b), max(a, b))]
        piece = packed[n * TILE : (n + 1) * TILE]
        return piece if a <= b else piece.T

    return jnp.concatenate(
        [jnp.concatenate([tile(a, b) for b in range(tiles)], axis=1) for a in range(tiles)], axis=0
    )


def split_words(value):
    high = lax.reduce_precision(value, 8, 7)
    return high.astype(BF16), (value - high).astype(BF16)


def local(features, out_grads, counts, factor_old, inverse_old, old_owner, new_owner):
    width = out_grads.shape[1]
    tok_rows = features.shape[0]
    feature_count = features.shape[1]
    column = lax.axis_index("mp")
    member = lax.axis_index("dp")
    members = lax.axis_size("dp")
    columns = lax.axis_size("mp")
    chips = members // 2
    core = member % 2
    swap = [(i, i ^ 1) for i in range(members)]
    same_core = [[2 * q + c for q in range(chips)] for c in range(2)]

    def pair_split(parts):
        paired = parts.reshape((chips, 2) + parts.shape[1:])
        mine = lax.dynamic_index_in_dim(paired, core, 1, keepdims=False)
        other = lax.dynamic_index_in_dim(paired, 1 - core, 1, keepdims=False)
        return mine, lax.ppermute(other, "dp", swap)

    def across_chips(parts):
        return lax.all_to_all(parts, "dp", 0, 0, tiled=True, axis_index_groups=same_core)

    def reduce_scatter(parts):
        mine, received = pair_split(parts)
        pair_sum = (mine.astype(F32) + received.astype(F32)).astype(BF16)
        return jnp.sum(across_chips(pair_sum).astype(F32), axis=0)

    stale_owner = lax.dynamic_index_in_dim(old_owner, column, 0, keepdims=False)
    fresh_owner = lax.dynamic_index_in_dim(new_owner, column, 0, keepdims=False)
    shared_slot = (stale_owner[1] == stale_owner[0]).astype(jnp.int32)

    stale = [
        held[0, 0, 0] if k == 0 else lax.dynamic_index_in_dim(held[0, 0], shared_slot, 0, keepdims=False)
        for held in (factor_old, inverse_old)
        for k in range(2)
    ]
    eye = jnp.eye(width, dtype=F32)
    share = width * (width + TILE) // 2 // TILE // members
    diagonals = jnp.stack([jnp.sum(block * eye, axis=0) for block in stale])
    diag_high, diag_low = split_words(diagonals.reshape(-1, TILE))
    diag_rows = jnp.concatenate([diag_high, diag_low], axis=0)
    packed = jnp.stack(
        [pack_upper((block * (1.0 - eye)).astype(BF16)).reshape(members, share, TILE) for block in stale],
        axis=1,
    ).reshape(members, 4 * share, TILE)
    packed = jnp.concatenate(
        [packed, jnp.broadcast_to(diag_rows, (members,) + diag_rows.shape)], axis=1
    )
    lanes = width // TILE
    row_kind = np.concatenate(
        [np.repeat([0, 1, 0, 1], share), np.tile(np.repeat([0, 1, 0, 1], lanes), 2)]
    )[:, None]
    owner_core = stale_owner % 2
    owner_chip = stale_owner // 2
    mine, received = pair_split(packed)
    from_mine = jnp.where(row_kind == 0, owner_core[0] == core, owner_core[1] == core)
    chosen = across_chips(jnp.where(from_mine, mine, received))
    scattered = jnp.where(
        row_kind == 0,
        lax.dynamic_index_in_dim(chosen, owner_chip[0], 0, keepdims=False),
        lax.dynamic_index_in_dim(chosen, owner_chip[1], 0, keepdims=False),
    )
    diag_rows = scattered[4 * share :].astype(F32)
    diagonals = (diag_rows[: 4 * lanes] + diag_rows[4 * lanes :]).reshape(4, width)
    factor_share = scattered[: 2 * share].astype(F32)
    inverse_share = scattered[2 * share : 4 * share]

    valid_rows = (jnp.arange(tok_rows, dtype=jnp.int32) < counts[0])[:, None]
    grads_kept = jnp.where(valid_rows, out_grads, jnp.zeros_like(out_grads))
    own_block = lax.dynamic_slice_in_dim(features, column * width, width, 1)
    block_kept = jnp.where(valid_rows, own_block, jnp.zeros_like(own_block))
    covariances = [contract_rows(block_kept, own_block), contract_rows(grads_kept, out_grads)]
    digits = jnp.concatenate(
        [jnp.full((4, TILE), (counts[0] >> (3 * d)) & 7).astype(BF16) for d in range(4)], axis=0
    )
    cov_parts = jnp.concatenate(
        [pack_upper(cov.astype(BF16)).reshape(members, share, TILE) for cov in covariances]
        + [jnp.broadcast_to(digits, (members,) + digits.shape)],
        axis=1,
    )
    cov_share = reduce_scatter(cov_parts)
    total = sum(cov_share[2 * share + 4 * d, 0] * float(8**d) for d in range(4))
    factor_share = DECAY * factor_share + (1.0 - DECAY) * cov_share[: 2 * share] / total

    shares = jnp.concatenate([factor_share.astype(BF16), inverse_share], axis=0)
    gathered = across_chips(jnp.broadcast_to(shares, (chips,) + shares.shape))
    gathered_other = lax.ppermute(gathered, "dp", swap)
    gathered = jnp.where(
        core == 0,
        jnp.stack([gathered, gathered_other], axis=1),
        jnp.stack([gathered_other, gathered], axis=1),
    )
    gathered = gathered.reshape(members, 4, share, TILE).transpose(1, 0, 2, 3)
    gathered = gathered.reshape(4, members * share, TILE).astype(F32)
    factors = [unpack_upper(gathered[k], width) + DECAY * eye * diagonals[k] for k in range(2)]
    stales = [unpack_upper(gathered[2 + k], width) + eye * diagonals[2 + k] for k in range(2)]
    inverses = []
    for factor, inverse in zip(factors, stales):
        inner = jnp.dot(factor + DAMPING * eye, inverse, precision=lax.Precision.HIGHEST)
        inverses.append(
            2.0 * inverse - jnp.dot(inverse, inner, precision=lax.Precision.HIGHEST)
        )
    keeps = [member == fresh_owner[k] for k in range(2)]
    factor_out = jnp.where(keeps[0], factors[0], jnp.where(keeps[1], factors[1], 0.0))
    inverse_out = jnp.where(keeps[0], inverses[0], jnp.where(keeps[1], inverses[1], 0.0))
    right_inverse = inverses[1].astype(BF16)

    holders = members // columns
    share_rows = feature_count // members
    left_rows = lax.dynamic_slice_in_dim(
        inverses[0].astype(BF16), (member % holders) * share_rows, share_rows, 0
    )
    left_rows = lax.all_to_all(
        jnp.broadcast_to(left_rows, (columns,) + left_rows.shape), "mp", 0, 0, tiled=True
    )
    left_rows = lax.dynamic_index_in_dim(left_rows, member // holders, 0, keepdims=False)

    grad_parts = contract_rows(features, grads_kept).astype(BF16)
    grad_rows = reduce_scatter(grad_parts.reshape(members, share_rows, width)).astype(BF16)
    neighbours = [[holders * c + r for r in range(holders)] for c in range(columns)]
    grad_block = lax.all_gather(
        grad_rows, "dp", axis=0, tiled=True, axis_index_groups=neighbours
    )
    half = jnp.dot(left_rows, grad_block, preferred_element_type=F32).astype(BF16)
    result = jnp.dot(half, right_inverse, preferred_element_type=F32)

    curvature = jnp.full((8, TILE), jnp.sum(result * grad_rows.astype(F32)))
    curvature = curvature + lax.ppermute(curvature, "dp", swap)
    curvature = jnp.sum(across_chips(jnp.broadcast_to(curvature, (chips, 8, TILE))), axis=0)
    curvature = lax.all_to_all(
        jnp.broadcast_to(curvature, (columns, 8, TILE)), "mp", 0, 0, tiled=True
    )
    curvature = jnp.sum(curvature, axis=0)[0, 0]
    entries = float(feature_count * width * columns)
    clip_scale = jnp.minimum(1.0, jnp.sqrt(entries / jnp.abs(curvature)))
    return (factor_out[None, None], inverse_out[None, None], clip_scale * result)


def solution(mesh):
    return jax.shard_map(
        local,
        mesh=mesh,
        in_specs=(
            P("dp", None),
            P("dp", "mp"),
            P("dp"),
            P("mp", "dp", None, None, None),
            P("mp", "dp", None, None, None),
            P(),
            P(),
        ),
        out_specs=(P("mp", "dp", None, None), P("mp", "dp", None, None), P("dp", "mp")),
        check_vma=False,
    )
```

```python
import jax
import jax.numpy as jnp
from jax import lax
from jax.experimental import pallas as pl
from jax.experimental.pallas import tpu as pltpu
from jax.sharding import PartitionSpec as P

DECAY = 0.9
DAMPING = 0.01
TILE = 128
ROWS = 16
VMEM_BYTES = 48 * 1024 * 1024
BF16 = jnp.bfloat16
F32 = jnp.float32
HIGHEST = lax.Precision.HIGHEST
PARAMS = pltpu.CompilerParams(vmem_limit_bytes=VMEM_BYTES)
SCALARS = pl.BlockSpec(memory_space=pltpu.SMEM)
WHOLE = pl.BlockSpec(memory_space=pltpu.VMEM)


def upper_pairs(tiles):
    return [(a, b) for a in range(tiles) for b in range(a, tiles)]


def diagonal_mask():
    rows = lax.broadcasted_iota(jnp.int32, (TILE, TILE), 0)
    return rows == lax.broadcasted_iota(jnp.int32, (TILE, TILE), 1)


def tile_of(a, b):
    return (slice(a * TILE, (a + 1) * TILE), slice(b * TILE, (b + 1) * TILE))


def pack_old(scalars, factors, inverses, keep, send, packed, diag):
    core, shared = scalars[0], scalars[1]
    tiles = factors.shape[1] // TILE
    on_diagonal = diagonal_mask()
    for which, held in enumerate((factors, inverses)):
        for kind in range(2):
            slot = 0 if kind == 0 else shared
            for n, (a, b) in enumerate(upper_pairs(tiles)):
                piece = held[(slot,) + tile_of(a, b)]
                if a == b:
                    row = (which * 2 + kind) * tiles + a
                    diag[row : row + 1, :] = jnp.sum(
                        jnp.where(on_diagonal, piece, 0.0), axis=0, keepdims=True
                    )
                    piece = jnp.where(on_diagonal, 0.0, piece)
                packed[kind, which, n * TILE : (n + 1) * TILE, :] = piece.astype(BF16)
    high = diag[...].astype(BF16)
    low = (diag[...] - high.astype(F32)).astype(BF16)
    words = jnp.concatenate([high, low], axis=0)
    chips = keep.shape[0]
    share = (keep.shape[1] - words.shape[0]) // 2
    for q in range(chips):
        kind, pair = divmod(q, chips // 2)
        for ref, parity in ((keep, core), (send, 1 - core)):
            start = pl.multiple_of((2 * pair + parity) * share, ROWS)
            for which in range(2):
                ref[q, which * share : (which + 1) * share, :] = packed[
                    kind, which, pl.ds(start, share), :
                ]
            ref[q, 2 * share :, :] = words


def covariance_parts(scalars, own, grads, keep, send, kept, packed):
    core, count = scalars[0], scalars[1]
    rows, width = own.shape
    tiles = width // TILE
    valid = lax.broadcasted_iota(jnp.int32, (rows, width), 0) < count
    for kind, block in enumerate((own, grads)):
        masked = jnp.where(valid, block[...].astype(F32), 0.0)
        kept[...] = masked.T.astype(BF16)
        for n, (a, b) in enumerate(upper_pairs(tiles)):
            if b % 2 == 0 and a % 2 == 0:
                square = jnp.dot(
                    kept[a * TILE : (a + 2) * TILE, :],
                    block[:, b * TILE : (b + 2) * TILE],
                    preferred_element_type=F32,
                ).astype(BF16)
                for i in range(2):
                    for j in range(2):
                        if a + i <= b + j:
                            at = upper_pairs(tiles).index((a + i, b + j))
                            packed[kind, at * TILE : (at + 1) * TILE, :] = square[tile_of(i, j)]
    quarter = lax.broadcasted_iota(jnp.int32, (ROWS, TILE), 0) // 4
    digits = lax.shift_right_logical(jnp.full((ROWS, TILE), count), 3 * quarter) & 7
    digits = digits.astype(F32).astype(BF16)
    chips = keep.shape[0]
    share = keep.shape[1] - ROWS
    for q in range(chips):
        kind, pair = divmod(q, chips // 2)
        for ref, parity in ((keep, core), (send, 1 - core)):
            start = pl.multiple_of((2 * pair + parity) * share, ROWS)
            ref[q, :share, :] = packed[kind, pl.ds(start, share), :]
            ref[q, share:, :] = digits


def gradient_parts(scalars, features, grads, keep, send, turned, product):
    core, count = scalars[0], scalars[1]

    @pl.when(pl.program_id(0) == 0)
    def _():
        valid = lax.broadcasted_iota(jnp.int32, grads.shape, 0) < count
        turned[...] = jnp.where(valid, grads[...].astype(F32), 0.0).T.astype(BF16)

    product[...] = jnp.dot(turned[...], features[...], preferred_element_type=F32).astype(BF16)
    for ref, parity in ((keep, core), (send, 1 - core)):
        start = pl.multiple_of(parity * TILE, TILE)
        ref[0] = product[:, pl.ds(start, TILE)]


def unpack(mine, other, core, kind, packed):
    chips = mine.shape[0]
    share = mine.shape[1] // 2
    for pair in range(chips // 2):
        q = kind * (chips // 2) + pair
        for ref, parity in ((mine, core), (other, 1 - core)):
            start = pl.multiple_of((2 * pair + parity) * share, ROWS)
            for which in range(2):
                packed[which, pl.ds(start, share), :] = ref[
                    q, which * share : (which + 1) * share, :
                ]


def spread(packed, which, diag, row, scale, block):
    tiles = block.shape[0] // TILE
    on_diagonal = diagonal_mask()
    for n, (a, b) in enumerate(upper_pairs(tiles)):
        piece = packed[which, n * TILE : (n + 1) * TILE, :].astype(F32)
        if a == b:
            piece = piece + jnp.where(on_diagonal, scale * diag[row + a : row + a + 1, :], 0.0)
        else:
            block[tile_of(b, a)] = piece.T
        block[tile_of(a, b)] = piece


def load_blocks(mine, other, core, kind, packed, diag, factor, inverse):
    tiles = factor.shape[0] // TILE
    unpack(mine, other, core, kind, packed)
    spread(packed, 0, diag, kind * tiles, DECAY, factor)
    spread(packed, 1, diag, (2 + kind) * tiles, 1.0, inverse)


def refine(factor, inverse, part):
    inner = jnp.dot(factor[...], part, precision=HIGHEST, preferred_element_type=F32)
    inner = inner + DAMPING * part
    return 2.0 * part - jnp.dot(inverse[...], inner, precision=HIGHEST, preferred_element_type=F32)


def left_columns(scalars, mine, other, diag, left, packed, factor, inverse):
    core, place = scalars[0], scalars[1]
    load_blocks(mine, other, core, 0, packed, diag, factor, inverse)
    start = pl.multiple_of(place * TILE, TILE)
    left[...] = refine(factor, inverse, inverse[:, pl.ds(start, TILE)]).astype(BF16)


def new_blocks(scalars, mine, other, diag, right, factor_out, inverse_out, packed, factor, inverse):
    core, first, second = scalars[0], scalars[2], scalars[3]
    load_blocks(mine, other, core, 1, packed, diag, factor, inverse)
    fresh = refine(factor, inverse, inverse[...])
    right[...] = fresh.astype(BF16)

    @pl.when(second == 1)
    def _():
        factor_out[...] = factor[...]
        inverse_out[...] = fresh

    @pl.when(second == 0)
    def _():
        factor_out[...] = jnp.zeros_like(factor_out)
        inverse_out[...] = jnp.zeros_like(inverse_out)

    @pl.when(first == 1)
    def _():
        load_blocks(mine, other, core, 0, packed, diag, factor, inverse)
        factor_out[...] = factor[...]
        inverse_out[...] = refine(factor, inverse, inverse[...])


def precondition(scalars, grad, lefts, right, result, curvature):
    own, block = scalars[0], scalars[1]
    left = lefts[block]
    half = sum(
        jnp.dot(grad[p], left[p * TILE : (p + 1) * TILE, :], preferred_element_type=F32)
        for p in range(grad.shape[0])
    )
    product = jnp.dot(half.T.astype(BF16), right[...], preferred_element_type=F32)
    result[...] = product
    curvature[...] = jnp.full(curvature.shape, jnp.sum(product * grad[own].astype(F32).T))


def local(features, out_grads, counts, factor_old, inverse_old, old_owner, new_owner):
    tok_rows, width = out_grads.shape
    feature_count = features.shape[1]
    column = lax.axis_index("mp")
    member = lax.axis_index("dp")
    members = lax.axis_size("dp")
    columns = lax.axis_size("mp")
    chips = members // 2
    core = member % 2
    swap = [(i, i ^ 1) for i in range(members)]
    same_core = [[2 * q + c for q in range(chips)] for c in range(2)]
    packed_rows = width * (width + TILE) // 2 // TILE
    share = 2 * packed_rows // members
    lanes = width // TILE
    shape = jax.ShapeDtypeStruct

    def across_chips(parts):
        return lax.all_to_all(parts, "dp", 0, 0, tiled=True, axis_index_groups=same_core)

    def pair_sum(keep, send):
        received = lax.ppermute(send, "dp", swap)
        return (keep.astype(F32) + received.astype(F32)).astype(BF16)

    stale_owner = lax.dynamic_index_in_dim(old_owner, column, 0, keepdims=False)
    fresh_owner = lax.dynamic_index_in_dim(new_owner, column, 0, keepdims=False)
    shared_slot = (stale_owner[1] == stale_owner[0]).astype(jnp.int32)

    message = shape((chips, 2 * share + 8 * lanes, TILE), BF16)
    keep, send = pl.pallas_call(
        pack_old,
        out_shape=(message, message),
        in_specs=[SCALARS, WHOLE, WHOLE],
        out_specs=(WHOLE, WHOLE),
        scratch_shapes=[
            pltpu.VMEM((2, 2, packed_rows, TILE), BF16),
            pltpu.VMEM((4 * lanes, TILE), F32),
        ],
        compiler_params=PARAMS,
        name="pack_old",
    )(jnp.stack([core, shared_slot]), factor_old[0, 0], inverse_old[0, 0])
    received = lax.ppermute(send, "dp", swap)
    row = lax.broadcasted_iota(jnp.int32, message.shape, 1) - 2 * share
    chip = lax.broadcasted_iota(jnp.int32, message.shape, 0)
    row_kind = jnp.where(row < 0, chip // (chips // 2), (row // lanes) % 2)
    owner_core = jnp.where(row_kind == 0, stale_owner[0] % 2, stale_owner[1] % 2)
    chosen = across_chips(jnp.where(owner_core == core, keep, received))
    from_first = lax.dynamic_index_in_dim(chosen, stale_owner[0] // 2, 0, keepdims=False)
    from_second = lax.dynamic_index_in_dim(chosen, stale_owner[1] // 2, 0, keepdims=False)
    own_kind = member // chips
    scattered = jnp.where(own_kind == 0, from_first, from_second)
    row = lax.broadcasted_iota(jnp.int32, (8 * lanes, TILE), 0)
    words = jnp.where((row // lanes) % 2 == 0, from_first[2 * share :], from_second[2 * share :])
    words = words.astype(F32)
    diag = words[: 4 * lanes] + words[4 * lanes :]

    message = shape((chips, share + ROWS, TILE), BF16)
    grads_spec = pl.BlockSpec((tok_rows, width), lambda i, s: (0, 0))
    message_spec = pl.BlockSpec(message.shape, lambda i, s: (0, 0, 0))
    keep, send = pl.pallas_call(
        covariance_parts,
        out_shape=(message, message),
        grid_spec=pltpu.PrefetchScalarGridSpec(
            num_scalar_prefetch=1,
            grid=(1,),
            in_specs=[pl.BlockSpec((tok_rows, width), lambda i, s: (0, s[2])), grads_spec],
            out_specs=(message_spec, message_spec),
            scratch_shapes=[
                pltpu.VMEM((width, tok_rows), BF16),
                pltpu.VMEM((2, packed_rows, TILE), BF16),
            ],
        ),
        compiler_params=PARAMS,
        name="covariance_parts",
    )(jnp.stack([core, counts[0], column]), features, out_grads)
    cov_share = jnp.sum(across_chips(pair_sum(keep, send)).astype(F32), axis=0)
    total = sum(cov_share[share + 4 * d, 0] * float(8**d) for d in range(4))
    factor_share = DECAY * scattered[:share].astype(F32) + (1.0 - DECAY) * cov_share[:share] / total

    shares = jnp.concatenate([factor_share.astype(BF16), scattered[share : 2 * share]], axis=0)
    mine = across_chips(jnp.broadcast_to(shares, (chips,) + shares.shape))
    other = lax.ppermute(mine, "dp", swap)
    holders = members // columns
    place = member % holders
    scalars = jnp.stack(
        [core, place, (member == fresh_owner[0]).astype(jnp.int32), (member == fresh_owner[1]).astype(jnp.int32)]
    )
    unpacked = [
        pltpu.VMEM((2, packed_rows, TILE), BF16),
        pltpu.VMEM((width, width), F32),
        pltpu.VMEM((width, width), F32),
    ]
    left = pl.pallas_call(
        left_columns,
        out_shape=shape((width, TILE), BF16),
        in_specs=[SCALARS, WHOLE, WHOLE, WHOLE],
        out_specs=WHOLE,
        scratch_shapes=unpacked,
        compiler_params=PARAMS,
        name="left_columns",
    )(scalars, mine, other, diag)
    lefts = lax.all_to_all(
        jnp.broadcast_to(left, (columns,) + left.shape), "mp", 0, 0, tiled=True
    )
    right, factor_out, inverse_out = pl.pallas_call(
        new_blocks,
        out_shape=(
            shape((width, width), BF16),
            shape((width, width), F32),
            shape((width, width), F32),
        ),
        in_specs=[SCALARS, WHOLE, WHOLE, WHOLE],
        out_specs=(WHOLE, WHOLE, WHOLE),
        scratch_shapes=unpacked,
        compiler_params=PARAMS,
        name="new_blocks",
    )(scalars, mine, other, diag)

    message = shape((chips, width, TILE), BF16)
    message_spec = pl.BlockSpec((1, width, TILE), lambda i, s: (i, 0, 0))
    keep, send = pl.pallas_call(
        gradient_parts,
        out_shape=(message, message),
        grid_spec=pltpu.PrefetchScalarGridSpec(
            num_scalar_prefetch=1,
            grid=(chips,),
            in_specs=[pl.BlockSpec((tok_rows, 2 * TILE), lambda i, s: (0, i)), grads_spec],
            out_specs=(message_spec, message_spec),
            scratch_shapes=[
                pltpu.VMEM((width, tok_rows), BF16),
                pltpu.VMEM((width, 2 * TILE), BF16),
            ],
        ),
        compiler_params=PARAMS,
        name="gradient_parts",
    )(jnp.stack([core, counts[0]]), features, out_grads)
    grad = jnp.sum(across_chips(pair_sum(keep, send)).astype(F32), axis=0).astype(BF16)
    neighbours = [[holders * c + r for r in range(holders)] for c in range(columns)]
    grads = lax.all_gather(grad, "dp", axis=0, axis_index_groups=neighbours)

    result, curvature = pl.pallas_call(
        precondition,
        out_shape=(shape((TILE, width), F32), shape((8, TILE), F32)),
        in_specs=[SCALARS, WHOLE, WHOLE, WHOLE],
        out_specs=(WHOLE, WHOLE),
        compiler_params=PARAMS,
        name="precondition",
    )(jnp.stack([place, member // holders]), grads, lefts, right)

    curvature = curvature + lax.ppermute(curvature, "dp", swap)
    curvature = jnp.sum(across_chips(jnp.broadcast_to(curvature, (chips, 8, TILE))), axis=0)
    curvature = lax.all_to_all(
        jnp.broadcast_to(curvature, (columns, 8, TILE)), "mp", 0, 0, tiled=True
    )
    curvature = jnp.sum(curvature, axis=0)[0, 0]
    entries = float(feature_count * width * columns)
    clip_scale = jnp.minimum(1.0, jnp.sqrt(entries / jnp.abs(curvature)))
    return (factor_out[None, None], inverse_out[None, None], clip_scale * result)


def solution(mesh):
    return jax.shard_map(
        local,
        mesh=mesh,
        in_specs=(
            P("dp", None),
            P("dp", "mp"),
            P("dp"),
            P("mp", "dp", None, None, None),
            P("mp", "dp", None, None, None),
            P(),
            P(),
        ),
        out_specs=(P("mp", "dp", None, None), P("mp", "dp", None, None), P("dp", "mp")),
        check_vma=False,
    )
```

```python
import jax
import jax.numpy as jnp
from jax import lax
from jax.experimental import pallas as pl
from jax.experimental.pallas import tpu as pltpu
from jax.sharding import PartitionSpec as P

DECAY = 0.9
DAMPING = 0.01
TILE = 128
ROWS = 16
VMEM_BYTES = 48 * 1024 * 1024
BF16 = jnp.bfloat16
F32 = jnp.float32
HIGHEST = lax.Precision.HIGHEST
PARAMS = pltpu.CompilerParams(vmem_limit_bytes=VMEM_BYTES)
SCALARS = pl.BlockSpec(memory_space=pltpu.SMEM)
WHOLE = pl.BlockSpec(memory_space=pltpu.VMEM)


def upper_pairs(tiles):
    return [(a, b) for a in range(tiles) for b in range(a, tiles)]


def diagonal_mask():
    rows = lax.broadcasted_iota(jnp.int32, (TILE, TILE), 0)
    return rows == lax.broadcasted_iota(jnp.int32, (TILE, TILE), 1)


def tile_of(a, b):
    return (slice(a * TILE, (a + 1) * TILE), slice(b * TILE, (b + 1) * TILE))


def pack_old(scalars, factors, inverses, keep, send, packed, diag):
    core, shared, flip = scalars[0], scalars[1], scalars[2]
    tiles = factors.shape[1] // TILE
    on_diagonal = diagonal_mask()
    for which, held in enumerate((factors, inverses)):
        for kind in range(2):
            slot = 0 if kind == 0 else shared
            for n, (a, b) in enumerate(upper_pairs(tiles)):
                piece = held[(slot,) + tile_of(a, b)]
                if a == b:
                    row = (which * 2 + kind) * tiles + a
                    diag[row : row + 1, :] = jnp.sum(
                        jnp.where(on_diagonal, piece, 0.0), axis=0, keepdims=True
                    )
                    piece = jnp.where(on_diagonal, 0.0, piece)
                packed[kind, which, n * TILE : (n + 1) * TILE, :] = piece.astype(BF16)
    high = diag[...].astype(BF16)
    low = (diag[...] - high.astype(F32)).astype(BF16)
    words = jnp.concatenate([high, low], axis=0)
    chips = keep.shape[0]
    share = (keep.shape[1] - words.shape[0]) // 2
    for q in range(chips):
        plane, pair = divmod(q, chips // 2)
        kind = flip if plane == 0 else 1 - flip
        for ref, parity in ((keep, core), (send, 1 - core)):
            start = pl.multiple_of((2 * pair + parity) * share, ROWS)
            for which in range(2):
                ref[q, which * share : (which + 1) * share, :] = packed[
                    kind, which, pl.ds(start, share), :
                ]
            ref[q, 2 * share :, :] = words


def covariance_parts(scalars, own, grads, keep, send, kept, packed):
    core, count, flip = scalars[0], scalars[1], scalars[3]
    rows, width = own.shape
    tiles = width // TILE
    valid = lax.broadcasted_iota(jnp.int32, (rows, width), 0) < count
    for kind, block in enumerate((own, grads)):
        masked = jnp.where(valid, block[...].astype(F32), 0.0)
        kept[...] = masked.T.astype(BF16)
        for n, (a, b) in enumerate(upper_pairs(tiles)):
            if b % 2 == 0 and a % 2 == 0:
                square = jnp.dot(
                    kept[a * TILE : (a + 2) * TILE, :],
                    block[:, b * TILE : (b + 2) * TILE],
                    preferred_element_type=F32,
                ).astype(BF16)
                for i in range(2):
                    for j in range(2):
                        if a + i <= b + j:
                            at = upper_pairs(tiles).index((a + i, b + j))
                            packed[kind, at * TILE : (at + 1) * TILE, :] = square[tile_of(i, j)]
    quarter = lax.broadcasted_iota(jnp.int32, (ROWS, TILE), 0) // 4
    digits = lax.shift_right_logical(jnp.full((ROWS, TILE), count), 3 * quarter) & 7
    digits = digits.astype(F32).astype(BF16)
    chips = keep.shape[0]
    share = keep.shape[1] - ROWS
    for q in range(chips):
        plane, pair = divmod(q, chips // 2)
        kind = flip if plane == 0 else 1 - flip
        for ref, parity in ((keep, core), (send, 1 - core)):
            start = pl.multiple_of((2 * pair + parity) * share, ROWS)
            ref[q, :share, :] = packed[kind, pl.ds(start, share), :]
            ref[q, share:, :] = digits


def gradient_parts(scalars, features, grads, keep, send, turned, product):
    core, count = scalars[0], scalars[1]

    @pl.when(pl.program_id(0) == 0)
    def _():
        valid = lax.broadcasted_iota(jnp.int32, grads.shape, 0) < count
        turned[...] = jnp.where(valid, grads[...].astype(F32), 0.0).T.astype(BF16)

    product[...] = jnp.dot(turned[...], features[...], preferred_element_type=F32).astype(BF16)
    for q in range(keep.shape[0]):
        for ref, parity in ((keep, core), (send, 1 - core)):
            start = pl.multiple_of((2 * q + parity) * TILE, TILE)
            ref[q] = product[:, pl.ds(start, TILE)]


def unpack(mine, other, core, packed):
    share = mine.shape[1] // 2
    for pair in range(mine.shape[0]):
        for ref, parity in ((mine, core), (other, 1 - core)):
            start = pl.multiple_of((2 * pair + parity) * share, ROWS)
            for which in range(2):
                packed[which, pl.ds(start, share), :] = ref[
                    pair, which * share : (which + 1) * share, :
                ]


def spread(packed, which, diag, row, scale, block):
    tiles = block.shape[0] // TILE
    on_diagonal = diagonal_mask()
    for n, (a, b) in enumerate(upper_pairs(tiles)):
        piece = packed[which, n * TILE : (n + 1) * TILE, :].astype(F32)
        if a == b:
            piece = piece + jnp.where(on_diagonal, scale * diag[row + a : row + a + 1, :], 0.0)
        else:
            block[tile_of(b, a)] = piece.T
        block[tile_of(a, b)] = piece


def fill_blocks(kind, packed, diag, factor, inverse):
    tiles = factor.shape[0] // TILE
    spread(packed, 0, diag, kind * tiles, DECAY, factor)
    spread(packed, 1, diag, (2 + kind) * tiles, 1.0, inverse)


def refine(factor, inverse, part):
    inner = jnp.dot(factor[...], part, precision=HIGHEST, preferred_element_type=F32)
    inner = inner + DAMPING * part
    return 2.0 * part - jnp.dot(inverse[...], inner, precision=HIGHEST, preferred_element_type=F32)


def left_columns(scalars, mine, other, diag, left, packed, factor, inverse):
    core, place = scalars[0], scalars[1]
    unpack(mine, other, core, packed)
    fill_blocks(0, packed, diag, factor, inverse)
    start = pl.multiple_of(place * TILE, TILE)
    left[...] = refine(factor, inverse, inverse[:, pl.ds(start, TILE)]).astype(BF16)


def new_blocks(
    scalars, mine, other, far_mine, far_other, diag, right, factor_out, inverse_out, packed, factor, inverse
):
    core, first, second, own_kind = scalars[0], scalars[2], scalars[3], scalars[4]

    def load_blocks(kind):
        @pl.when(own_kind == kind)
        def _():
            unpack(mine, other, core, packed)

        @pl.when(own_kind != kind)
        def _():
            unpack(far_mine, far_other, core, packed)

        fill_blocks(kind, packed, diag, factor, inverse)

    load_blocks(1)
    fresh = refine(factor, inverse, inverse[...])
    right[...] = fresh.astype(BF16)

    @pl.when(second == 1)
    def _():
        factor_out[...] = factor[...]
        inverse_out[...] = fresh

    @pl.when(second == 0)
    def _():
        factor_out[...] = jnp.zeros_like(factor_out)
        inverse_out[...] = jnp.zeros_like(inverse_out)

    @pl.when(first == 1)
    def _():
        load_blocks(0)
        factor_out[...] = factor[...]
        inverse_out[...] = refine(factor, inverse, inverse[...])


def precondition(scalars, grad, left, right, result, curvature):
    own = scalars[0]
    half = sum(
        jnp.dot(grad[p], left[p * TILE : (p + 1) * TILE, :], preferred_element_type=F32)
        for p in range(grad.shape[0])
    )
    product = jnp.dot(half.T.astype(BF16), right[...], preferred_element_type=F32)
    result[...] = product
    curvature[...] = jnp.full(curvature.shape, jnp.sum(product * grad[own].astype(F32).T))


def local(features, out_grads, counts, factor_old, inverse_old, old_owner, new_owner):
    tok_rows, width = out_grads.shape
    feature_count = features.shape[1]
    column = lax.axis_index("mp")
    member = lax.axis_index("dp")
    members = lax.axis_size("dp")
    columns = lax.axis_size("mp")
    chips = members // 2
    ring = chips // 2
    core = member % 2
    plane = member // chips
    core_swap = [(i, i ^ 1) for i in range(members)]
    plane_swap = [(i, (i + chips) % members) for i in range(members)]
    rings = [[y * chips + 2 * z + c for z in range(ring)] for y in range(2) for c in range(2)]
    packed_rows = width * (width + TILE) // 2 // TILE
    share = 2 * packed_rows // members
    lanes = width // TILE
    holders = members // columns
    place = member % holders
    shape = jax.ShapeDtypeStruct

    def across_ring(parts):
        return lax.all_to_all(parts, "dp", 0, 0, tiled=True, axis_index_groups=rings)

    def swap_cores(send):
        return lax.ppermute(send, "dp", core_swap)

    def swap_planes(send):
        return lax.ppermute(send, "dp", plane_swap)

    def plane_of(parts, which):
        return lax.dynamic_slice_in_dim(parts, which * ring, ring, 0)

    def sum_planes(keep, received):
        def pair(which):
            return plane_of(keep, which).astype(F32) + plane_of(received, which).astype(F32)

        arrived = swap_planes(pair(1 - plane).astype(BF16))
        return (pair(plane) + arrived.astype(F32)).astype(BF16)

    stale_owner = lax.dynamic_index_in_dim(old_owner, column, 0, keepdims=False)
    fresh_owner = lax.dynamic_index_in_dim(new_owner, column, 0, keepdims=False)
    shared_slot = (stale_owner[1] == stale_owner[0]).astype(jnp.int32)
    flip = column // (columns // 2)
    own_kind = plane ^ flip

    message = shape((chips, 2 * share + 8 * lanes, TILE), BF16)
    keep, send = pl.pallas_call(
        pack_old,
        out_shape=(message, message),
        in_specs=[SCALARS, WHOLE, WHOLE],
        out_specs=(WHOLE, WHOLE),
        scratch_shapes=[
            pltpu.VMEM((2, 2, packed_rows, TILE), BF16),
            pltpu.VMEM((4 * lanes, TILE), F32),
        ],
        compiler_params=PARAMS,
        name="pack_old",
    )(jnp.stack([core, shared_slot, flip]), factor_old[0, 0], inverse_old[0, 0])
    row = lax.broadcasted_iota(jnp.int32, message.shape, 1) - 2 * share
    chip = lax.broadcasted_iota(jnp.int32, message.shape, 0)

    def from_owner(kinds, place_of_owner, here, one, two):
        owner = jnp.where(kinds == 0, place_of_owner[0], place_of_owner[1])
        return jnp.where(owner == here, one, two)

    kinds = jnp.where(row < 0, (chip // ring) ^ flip, (row // lanes) % 2)
    chosen = from_owner(kinds, stale_owner % 2, core, keep, swap_cores(send))
    arrived = swap_planes(plane_of(chosen, 1 - plane))
    kinds = plane_of(kinds, plane)
    chosen = from_owner(kinds, stale_owner // chips, plane, plane_of(chosen, plane), arrived)

    message = shape((chips, share + ROWS, TILE), BF16)
    grads_spec = pl.BlockSpec((tok_rows, width), lambda i, s: (0, 0))
    message_spec = pl.BlockSpec(message.shape, lambda i, s: (0, 0, 0))
    keep, send = pl.pallas_call(
        covariance_parts,
        out_shape=(message, message),
        grid_spec=pltpu.PrefetchScalarGridSpec(
            num_scalar_prefetch=1,
            grid=(1,),
            in_specs=[pl.BlockSpec((tok_rows, width), lambda i, s: (0, s[2])), grads_spec],
            out_specs=(message_spec, message_spec),
            scratch_shapes=[
                pltpu.VMEM((width, tok_rows), BF16),
                pltpu.VMEM((2, packed_rows, TILE), BF16),
            ],
        ),
        compiler_params=PARAMS,
        name="covariance_parts",
    )(jnp.stack([core, counts[0], column, flip]), features, out_grads)
    covariances = sum_planes(keep, swap_cores(send))

    arrived = across_ring(jnp.concatenate([chosen, covariances], axis=1))
    owner_at = (stale_owner // 2) % ring
    from_first = lax.dynamic_index_in_dim(arrived, owner_at[0], 0, keepdims=False)
    from_second = lax.dynamic_index_in_dim(arrived, owner_at[1], 0, keepdims=False)
    scattered = jnp.where(own_kind == 0, from_first, from_second)
    at = slice(2 * share, 2 * share + 8 * lanes)
    row = lax.broadcasted_iota(jnp.int32, (8 * lanes, TILE), 0)
    words = jnp.where((row // lanes) % 2 == 0, from_first[at], from_second[at]).astype(F32)
    diag = words[: 4 * lanes] + words[4 * lanes :]
    cov_share = jnp.sum(arrived[:, 2 * share + 8 * lanes :].astype(F32), axis=0)
    total = sum(cov_share[share + 4 * d, 0] * float(8**d) for d in range(4))
    factor_share = DECAY * scattered[:share].astype(F32) + (1.0 - DECAY) * cov_share[:share] / total

    shares = jnp.concatenate([factor_share.astype(BF16), scattered[share : 2 * share]], axis=0)
    mine = across_ring(jnp.broadcast_to(shares, (ring,) + shares.shape))
    other = swap_cores(mine)
    far_mine = swap_planes(mine)
    far_other = swap_cores(far_mine)
    scalars = jnp.stack(
        [
            core,
            place,
            (member == fresh_owner[0]).astype(jnp.int32),
            (member == fresh_owner[1]).astype(jnp.int32),
            own_kind,
        ]
    )
    unpacked = [
        pltpu.VMEM((2, packed_rows, TILE), BF16),
        pltpu.VMEM((width, width), F32),
        pltpu.VMEM((width, width), F32),
    ]
    left = pl.pallas_call(
        left_columns,
        out_shape=shape((width, TILE), BF16),
        in_specs=[SCALARS, WHOLE, WHOLE, WHOLE],
        out_specs=WHOLE,
        scratch_shapes=unpacked,
        compiler_params=PARAMS,
        name="left_columns",
    )(scalars, mine, other, diag)
    gates = [(i, i // holders) for i in range(members)]
    near = lax.ppermute(
        left, ("dp", "mp"), [(i * columns + g, i * columns + (g ^ 1)) for i, g in gates]
    )
    gate = member // holders
    left = jnp.where(column == gate, left, near)
    left = jnp.where(
        column // 2 == gate // 2,
        left,
        sum(
            lax.ppermute(
                left,
                ("dp", "mp"),
                [
                    (i * columns + g, i * columns + (g + 2 * step) % columns)
                    for i, at in gates
                    for g in (at, at ^ 1)
                ],
            )
            for step in range(1, columns // 2)
        ),
    )
    right, factor_out, inverse_out = pl.pallas_call(
        new_blocks,
        out_shape=(
            shape((width, width), BF16),
            shape((width, width), F32),
            shape((width, width), F32),
        ),
        in_specs=[SCALARS, WHOLE, WHOLE, WHOLE, WHOLE, WHOLE],
        out_specs=(WHOLE, WHOLE, WHOLE),
        scratch_shapes=unpacked,
        compiler_params=PARAMS,
        name="new_blocks",
    )(scalars, mine, other, far_mine, far_other, diag)

    message = shape((chips, width, TILE), BF16)
    step = 8
    message_spec = pl.BlockSpec((step // 2, width, TILE), lambda i, s: (i, 0, 0))
    keep, send = pl.pallas_call(
        gradient_parts,
        out_shape=(message, message),
        grid_spec=pltpu.PrefetchScalarGridSpec(
            num_scalar_prefetch=1,
            grid=(members // step,),
            in_specs=[pl.BlockSpec((tok_rows, step * TILE), lambda i, s: (0, i)), grads_spec],
            out_specs=(message_spec, message_spec),
            scratch_shapes=[
                pltpu.VMEM((width, tok_rows), BF16),
                pltpu.VMEM((width, step * TILE), BF16),
            ],
        ),
        compiler_params=PARAMS,
        name="gradient_parts",
    )(jnp.stack([core, counts[0]]), features, out_grads)
    grad = across_ring(sum_planes(keep, swap_cores(send)))
    grad = jnp.sum(grad.astype(F32), axis=0).astype(BF16)
    neighbours = [[holders * c + r for r in range(holders)] for c in range(columns)]
    grads = lax.all_gather(grad, "dp", axis=0, axis_index_groups=neighbours)

    result, curvature = pl.pallas_call(
        precondition,
        out_shape=(shape((TILE, width), F32), shape((8, TILE), F32)),
        in_specs=[SCALARS, WHOLE, WHOLE, WHOLE],
        out_specs=(WHOLE, WHOLE),
        compiler_params=PARAMS,
        name="precondition",
    )(place[None], grads, left, right)

    curvature = curvature + swap_cores(curvature)
    curvature = curvature + swap_planes(curvature)
    curvature = jnp.sum(across_ring(jnp.broadcast_to(curvature, (ring, 8, TILE))), axis=0)
    curvature = lax.all_to_all(
        jnp.broadcast_to(curvature, (columns, 8, TILE)), "mp", 0, 0, tiled=True
    )
    curvature = jnp.sum(curvature, axis=0)[0, 0]
    entries = float(feature_count * width * columns)
    clip_scale = jnp.minimum(1.0, jnp.sqrt(entries / jnp.abs(curvature)))
    return (factor_out[None, None], inverse_out[None, None], clip_scale * result)


def solution(mesh):
    return jax.shard_map(
        local,
        mesh=mesh,
        in_specs=(
            P("dp", None),
            P("dp", "mp"),
            P("dp"),
            P("mp", "dp", None, None, None),
            P("mp", "dp", None, None, None),
            P(),
            P(),
        ),
        out_specs=(P("mp", "dp", None, None), P("mp", "dp", None, None), P("dp", "mp")),
        check_vma=False,
    )
```

```python
import jax
import jax.numpy as jnp
from jax import lax
from jax.experimental import pallas as pl
from jax.experimental.pallas import tpu as pltpu
from jax.sharding import PartitionSpec as P

DECAY = 0.9
DAMPING = 0.01
TILE = 128
ROWS = 16
VMEM_BYTES = 48 * 1024 * 1024
BF16 = jnp.bfloat16
F32 = jnp.float32
PARAMS = pltpu.CompilerParams(vmem_limit_bytes=VMEM_BYTES)
SCALARS = pl.BlockSpec(memory_space=pltpu.SMEM)
WHOLE = pl.BlockSpec(memory_space=pltpu.VMEM)


def upper_pairs(tiles):
    return [(a, b) for a in range(tiles) for b in range(a, tiles)]


def diagonal_mask():
    rows = lax.broadcasted_iota(jnp.int32, (TILE, TILE), 0)
    return rows == lax.broadcasted_iota(jnp.int32, (TILE, TILE), 1)


def tile_of(a, b):
    return (slice(a * TILE, (a + 1) * TILE), slice(b * TILE, (b + 1) * TILE))


def pack_old(scalars, factors, inverses, keep, send, packed, diag):
    core, shared, flip = scalars[0], scalars[1], scalars[2]
    tiles = factors.shape[1] // TILE
    on_diagonal = diagonal_mask()
    for which, held in enumerate((factors, inverses)):
        for kind in range(2):
            slot = 0 if kind == 0 else shared
            for n, (a, b) in enumerate(upper_pairs(tiles)):
                piece = held[(slot,) + tile_of(a, b)]
                if a == b:
                    row = (which * 2 + kind) * tiles + a
                    diag[row : row + 1, :] = jnp.sum(
                        jnp.where(on_diagonal, piece, 0.0), axis=0, keepdims=True
                    )
                    piece = jnp.where(on_diagonal, 0.0, piece)
                packed[kind, which, n * TILE : (n + 1) * TILE, :] = piece.astype(BF16)
    high = diag[...].astype(BF16)
    low = (diag[...] - high.astype(F32)).astype(BF16)
    words = jnp.concatenate([high, low], axis=0)
    chips = keep.shape[0]
    share = (keep.shape[1] - words.shape[0]) // 2
    for q in range(chips):
        plane, pair = divmod(q, chips // 2)
        kind = flip if plane == 0 else 1 - flip
        for ref, parity in ((keep, core), (send, 1 - core)):
            start = pl.multiple_of((2 * pair + parity) * share, ROWS)
            for which in range(2):
                ref[q, which * share : (which + 1) * share, :] = packed[
                    kind, which, pl.ds(start, share), :
                ]
            ref[q, 2 * share :, :] = words


def covariance_parts(scalars, own, grads, keep, send, turned, kept, packed):
    core, count, flip = scalars[0], scalars[1], scalars[3]
    rows, width = own.shape
    tiles = width // TILE
    valid = lax.broadcasted_iota(jnp.int32, (rows, width), 0) < count
    for kind, (block, left) in enumerate(((own, kept), (grads, turned))):
        left[...] = jnp.where(valid, block[...].astype(F32), 0.0).T.astype(BF16)
        for a, b in upper_pairs(tiles // 2):
            square = jnp.dot(
                left[2 * a * TILE : 2 * (a + 1) * TILE, :],
                block[:, 2 * b * TILE : 2 * (b + 1) * TILE],
                preferred_element_type=F32,
            ).astype(BF16)
            for i in range(2):
                for j in range(2):
                    if 2 * a + i <= 2 * b + j:
                        at = upper_pairs(tiles).index((2 * a + i, 2 * b + j))
                        packed[kind, at * TILE : (at + 1) * TILE, :] = square[tile_of(i, j)]
    quarter = lax.broadcasted_iota(jnp.int32, (ROWS, TILE), 0) // 4
    digits = lax.shift_right_logical(jnp.full((ROWS, TILE), count), 3 * quarter) & 7
    digits = digits.astype(F32).astype(BF16)
    chips = keep.shape[0]
    share = keep.shape[1] - ROWS
    for q in range(chips):
        plane, pair = divmod(q, chips // 2)
        kind = flip if plane == 0 else 1 - flip
        for ref, parity in ((keep, core), (send, 1 - core)):
            start = pl.multiple_of((2 * pair + parity) * share, ROWS)
            ref[q, :share, :] = packed[kind, pl.ds(start, share), :]
            ref[q, share:, :] = digits


def merge_words(first_flag, second_flag, one, two):
    lanes = one.shape[0] // 8
    kinds = (lax.broadcasted_iota(jnp.int32, one.shape, 0) // lanes) % 2
    flags = jnp.where(kinds == 0, first_flag, second_flag)
    return jnp.where(flags == 1, one.astype(F32), two.astype(F32))


def choose_core(scalars, keep, received, near, far):
    first, second, plane, own_kind = scalars[0], scalars[1], scalars[2], scalars[3]
    ring, rows = near.shape[0], near.shape[1]
    data = rows // 6 * 5
    words = merge_words(first, second, keep[0, data:, :], received[0, data:, :]).astype(BF16)
    for ref, at, kind in ((near, plane, own_kind), (far, 1 - plane, 1 - own_kind)):
        flag = jnp.where(kind == 0, first, second)

        @pl.when(flag == 1)
        def _():
            ref[:, :data, :] = keep[pl.ds(at * ring, ring), :data, :]

        @pl.when(flag == 0)
        def _():
            ref[:, :data, :] = received[pl.ds(at * ring, ring), :data, :]

        for z in range(ring):
            ref[z, data:, :] = words


def add_core(scalars, keep, received, near, far):
    plane = scalars[2]
    ring = near.shape[0]
    for ref, at in ((near, plane), (far, 1 - plane)):
        chips = pl.ds(at * ring, ring)
        total = keep[chips].astype(F32) + received[chips].astype(F32)
        ref[...] = total.astype(ref.dtype)


def join_planes(scalars, near, arrived, near_sum, arrived_sum, out):
    first, second, own_kind = scalars[4], scalars[5], scalars[3]
    ring, rows = near.shape[0], near.shape[1]
    data = rows // 6 * 5
    flag = jnp.where(own_kind == 0, first, second)

    @pl.when(flag == 1)
    def _():
        out[:, :data, :] = near[:, :data, :]

    @pl.when(flag == 0)
    def _():
        out[:, :data, :] = arrived[:, :data, :]

    words = merge_words(first, second, near[0, data:, :], arrived[0, data:, :]).astype(BF16)
    for z in range(ring):
        out[z, data:rows, :] = words
    out[:, rows:, :] = (near_sum[...] + arrived_sum[...].astype(F32)).astype(BF16)


def make_shares(scalars, arrived, shares, diag):
    own_kind, first, second = scalars[3], scalars[6], scalars[7]
    ring, rows = shares.shape[0], shares.shape[1]
    share = rows // 2
    words = rows // 5 + rows
    owner = jnp.where(own_kind == 0, first, second)
    both = merge_words(1, 0, arrived[first, rows:words, :], arrived[second, rows:words, :])
    diag[...] = both[: diag.shape[0]] + both[diag.shape[0] :]
    summed = sum(arrived[z, words:, :].astype(F32) for z in range(ring))
    total = sum(summed[share + 4 * d : share + 4 * d + 1, :] * float(8**d) for d in range(4))
    factor = DECAY * arrived[owner, :share, :].astype(F32) + (1.0 - DECAY) * summed[:share] / total
    factor = factor.astype(BF16)
    inverse = arrived[owner, share:rows, :]
    for z in range(ring):
        shares[z, :share, :] = factor
        shares[z, share:, :] = inverse


def gradient_tiles(turned, tiles):
    block = jnp.concatenate([tile[...] for tile in tiles], axis=1)
    return jnp.dot(turned[...], block, preferred_element_type=F32)


def gradient_send(scalars, turned, *refs):
    tiles, send = refs[:4], refs[-1]
    product = gradient_tiles(turned, tiles)
    for n in range(4):
        send[n] = product[:, n * TILE : (n + 1) * TILE].astype(send.dtype)


def gradient_add(scalars, turned, *refs):
    tiles, received, out = refs[:4], refs[4], refs[-1]
    product = gradient_tiles(turned, tiles)
    for n in range(4):
        total = product[:, n * TILE : (n + 1) * TILE] + received[n].astype(F32)
        out[n] = total.astype(out.dtype)


def unpack(mine, other, core, packed):
    share = mine.shape[1] // 2
    for pair in range(mine.shape[0]):
        for ref, parity in ((mine, core), (other, 1 - core)):
            start = pl.multiple_of((2 * pair + parity) * share, ROWS)
            for which in range(2):
                packed[which, pl.ds(start, share), :] = ref[
                    pair, which * share : (which + 1) * share, :
                ]


def spread(packed, which, diag, row, scale, high, low):
    tiles = high.shape[0] // TILE
    on_diagonal = diagonal_mask()
    for n, (a, b) in enumerate(upper_pairs(tiles)):
        piece = packed[which, n * TILE : (n + 1) * TILE, :].astype(F32)
        if a == b:
            exact = piece + jnp.where(on_diagonal, scale * diag[row + a : row + a + 1, :], 0.0)
            rounded = exact.astype(BF16)
            high[tile_of(a, a)] = rounded
            rest = jnp.sum(exact - rounded.astype(F32), axis=1, keepdims=True)
            low[a * TILE : (a + 1) * TILE, :] = jnp.broadcast_to(rest, (TILE, TILE))
        else:
            high[tile_of(a, b)] = packed[which, n * TILE : (n + 1) * TILE, :]
            high[tile_of(b, a)] = piece.T.astype(BF16)


def fill_blocks(kind, packed, diag, factor, factor_low, inverse, inverse_low):
    tiles = factor.shape[0] // TILE
    spread(packed, 0, diag, kind * tiles, DECAY, factor, factor_low)
    spread(packed, 1, diag, (2 + kind) * tiles, 1.0, inverse, inverse_low)


def times(high, low, right):
    width = right.shape[1]
    first = right.astype(BF16)
    second = (right - first.astype(F32)).astype(BF16)
    both = jnp.dot(high[...], jnp.concatenate([first, second], axis=1), preferred_element_type=F32)
    return both[:, :width] + both[:, width:] + low * right


def refine(factor, factor_low, inverse, inverse_low, part):
    inner = times(factor, factor_low[:, :1] + DAMPING, part)
    return 2.0 * part - times(inverse, inverse_low[:, :1], inner)


def exact_block(high, low):
    rows = lax.broadcasted_iota(jnp.int32, high.shape, 0)
    columns = lax.broadcasted_iota(jnp.int32, high.shape, 1)
    return high[...].astype(F32) + jnp.where(rows == columns, low[:, :1], 0.0)


def left_columns(scalars, mine, other, diag, left, packed, factor, factor_low, inverse, inverse_low):
    core, place = scalars[0], scalars[1]
    unpack(mine, other, core, packed)
    fill_blocks(0, packed, diag, factor, factor_low, inverse, inverse_low)
    start = pl.multiple_of(place * TILE, TILE)
    part = inverse[:, pl.ds(start, TILE)].astype(F32)
    rows = lax.broadcasted_iota(jnp.int32, part.shape, 0) - start
    part = part + jnp.where(
        rows == lax.broadcasted_iota(jnp.int32, part.shape, 1), inverse_low[...], 0.0
    )
    left[...] = refine(factor, factor_low, inverse, inverse_low, part).astype(BF16)


def new_blocks(
    scalars, mine, other, far_mine, far_other, diag, right, factor_out, inverse_out,
    packed, factor, factor_low, inverse, inverse_low,
):
    core, first, second, own_kind = scalars[0], scalars[2], scalars[3], scalars[4]
    blocks = (factor, factor_low, inverse, inverse_low)

    def load_blocks(kind):
        @pl.when(own_kind == kind)
        def _():
            unpack(mine, other, core, packed)

        @pl.when(own_kind != kind)
        def _():
            unpack(far_mine, far_other, core, packed)

        fill_blocks(kind, packed, diag, *blocks)

    load_blocks(1)
    fresh = refine(*blocks, exact_block(inverse, inverse_low))
    right[...] = fresh.astype(BF16)

    @pl.when(second == 1)
    def _():
        factor_out[...] = exact_block(factor, factor_low)
        inverse_out[...] = fresh

    @pl.when(second == 0)
    def _():
        factor_out[...] = jnp.zeros_like(factor_out)
        inverse_out[...] = jnp.zeros_like(inverse_out)

    @pl.when(first == 1)
    def _():
        load_blocks(0)
        factor_out[...] = exact_block(factor, factor_low)
        inverse_out[...] = refine(*blocks, exact_block(inverse, inverse_low))


def precondition(scalars, grad, left, right, result, curvature):
    own = scalars[0]
    half = sum(
        jnp.dot(grad[p], left[p * TILE : (p + 1) * TILE, :], preferred_element_type=F32)
        for p in range(grad.shape[0])
    )
    product = jnp.dot(half.T.astype(BF16), right[...], preferred_element_type=F32)
    result[...] = product
    curvature[...] = jnp.full(curvature.shape, jnp.sum(product * grad[own].astype(F32).T))


def local(features, out_grads, counts, factor_old, inverse_old, old_owner, new_owner):
    tok_rows, width = out_grads.shape
    feature_count = features.shape[1]
    column = lax.axis_index("mp")
    member = lax.axis_index("dp")
    members = lax.axis_size("dp")
    columns = lax.axis_size("mp")
    chips = members // 2
    ring = chips // 2
    core = member % 2
    plane = member // chips
    core_swap = [(i, i ^ 1) for i in range(members)]
    plane_swap = [(i, (i + chips) % members) for i in range(members)]
    rings = [[y * chips + 2 * z + c for z in range(ring)] for y in range(2) for c in range(2)]
    packed_rows = width * (width + TILE) // 2 // TILE
    share = 2 * packed_rows // members
    lanes = width // TILE
    holders = members // columns
    place = member % holders
    shape = jax.ShapeDtypeStruct

    def across_ring(parts):
        return lax.all_to_all(parts, "dp", 0, 0, tiled=True, axis_index_groups=rings)

    def swap_cores(send):
        return lax.ppermute(send, "dp", core_swap)

    def swap_planes(send):
        return lax.ppermute(send, "dp", plane_swap)

    stale_owner = lax.dynamic_index_in_dim(old_owner, column, 0, keepdims=False)
    fresh_owner = lax.dynamic_index_in_dim(new_owner, column, 0, keepdims=False)
    shared_slot = (stale_owner[1] == stale_owner[0]).astype(jnp.int32)
    flip = column // (columns // 2)
    own_kind = plane ^ flip

    message = shape((chips, 2 * share + 8 * lanes, TILE), BF16)
    keep, send = pl.pallas_call(
        pack_old,
        out_shape=(message, message),
        in_specs=[SCALARS, WHOLE, WHOLE],
        out_specs=(WHOLE, WHOLE),
        scratch_shapes=[
            pltpu.VMEM((2, 2, packed_rows, TILE), BF16),
            pltpu.VMEM((4 * lanes, TILE), F32),
        ],
        compiler_params=PARAMS,
        name="pack_old",
    )(jnp.stack([core, shared_slot, flip]), factor_old[0, 0], inverse_old[0, 0])
    owner_at = (stale_owner // 2) % ring
    scalars = jnp.concatenate(
        [
            (stale_owner % 2 == core).astype(jnp.int32),
            jnp.stack([plane, own_kind]),
            (stale_owner // chips == plane).astype(jnp.int32),
            owner_at,
        ]
    )
    half_message = shape((ring,) + message.shape[1:], BF16)
    near_old, far_old = pl.pallas_call(
        choose_core,
        out_shape=(half_message, half_message),
        in_specs=[SCALARS, WHOLE, WHOLE],
        out_specs=(WHOLE, WHOLE),
        compiler_params=PARAMS,
        name="choose_core",
    )(scalars, keep, swap_cores(send))
    arrived_old = swap_planes(far_old)

    message = shape((chips, share + ROWS, TILE), BF16)
    message_spec = pl.BlockSpec(message.shape, lambda i, s: (0, 0, 0))
    keep, send, turned = pl.pallas_call(
        covariance_parts,
        out_shape=(message, message, shape((width, tok_rows), BF16)),
        grid_spec=pltpu.PrefetchScalarGridSpec(
            num_scalar_prefetch=1,
            grid=(1,),
            in_specs=[
                pl.BlockSpec((tok_rows, width), lambda i, s: (0, s[2])),
                pl.BlockSpec((tok_rows, width), lambda i, s: (0, 0)),
            ],
            out_specs=(
                message_spec,
                message_spec,
                pl.BlockSpec((width, tok_rows), lambda i, s: (0, 0)),
            ),
            scratch_shapes=[
                pltpu.VMEM((width, tok_rows), BF16),
                pltpu.VMEM((2, packed_rows, TILE), BF16),
            ],
        ),
        compiler_params=PARAMS,
        name="covariance_parts",
    )(jnp.stack([core, counts[0], column, flip]), features, out_grads)
    half_shape = (ring,) + message.shape[1:]
    near_sum, far_sum = pl.pallas_call(
        add_core,
        out_shape=(shape(half_shape, F32), shape(half_shape, BF16)),
        in_specs=[SCALARS, WHOLE, WHOLE],
        out_specs=(WHOLE, WHOLE),
        compiler_params=PARAMS,
        name="add_core",
    )(scalars, keep, swap_cores(send))
    arrived_sum = swap_planes(far_sum)

    def gradient(kernel, tile_at, count, dtype, name, *others):
        def tile_spec(n):
            return pl.BlockSpec((tok_rows, TILE), lambda i, s: (0, 2 * tile_at(4 * i + n, s) + s[0]))

        message_spec = pl.BlockSpec((4, width, TILE), lambda i, s: (i, 0, 0))
        received_spec = pl.BlockSpec((4, width, TILE), lambda i, s: (tile_at(4 * i, s) // 4, 0, 0))
        other_specs = [received_spec] if len(others) == 1 else [pl.BlockSpec(memory_space=pl.ANY)] * 2
        parity = 1 - core if len(others) == 2 else core
        return pl.pallas_call(
            kernel,
            out_shape=shape((count, width, TILE), dtype),
            grid_spec=pltpu.PrefetchScalarGridSpec(
                num_scalar_prefetch=1,
                grid=(count // 4,),
                in_specs=[pl.BlockSpec((width, tok_rows), lambda i, s: (0, 0))]
                + [tile_spec(n) for n in range(4)]
                + other_specs,
                out_specs=message_spec,
            ),
            compiler_params=PARAMS,
            name=name,
        )(jnp.stack([parity, plane]), turned, features, features, features, features, *others)

    send = gradient(gradient_send, lambda q, s: q, chips, BF16, "gradient_send", far_old, far_sum)
    received = swap_cores(send)
    far_grad = gradient(
        gradient_add, lambda q, s: (1 - s[1]) * ring + q, ring, BF16, "gradient_far", received
    )
    arrived_grad = swap_planes(far_grad)
    near_grad = gradient(
        gradient_add, lambda q, s: s[1] * ring + q, ring, F32, "gradient_near", received
    )

    joined = pl.pallas_call(
        join_planes,
        out_shape=shape((ring, near_old.shape[1] + near_sum.shape[1], TILE), BF16),
        in_specs=[SCALARS] + [WHOLE] * 4,
        out_specs=WHOLE,
        compiler_params=PARAMS,
        name="join_planes",
    )(scalars, near_old, arrived_old, near_sum, arrived_sum)
    shares, diag = pl.pallas_call(
        make_shares,
        out_shape=(shape((ring, 2 * share, TILE), BF16), shape((4 * lanes, TILE), F32)),
        in_specs=[SCALARS, WHOLE],
        out_specs=(WHOLE, WHOLE),
        compiler_params=PARAMS,
        name="make_shares",
    )(scalars, across_ring(joined))

    mine = across_ring(shares)
    other = swap_cores(mine)
    far_mine = swap_planes(mine)
    far_other = swap_cores(far_mine)
    scalars = jnp.stack(
        [
            core,
            place,
            (member == fresh_owner[0]).astype(jnp.int32),
            (member == fresh_owner[1]).astype(jnp.int32),
            own_kind,
        ]
    )
    unpacked = [
        pltpu.VMEM((2, packed_rows, TILE), BF16),
        pltpu.VMEM((width, width), BF16),
        pltpu.VMEM((width, TILE), F32),
        pltpu.VMEM((width, width), BF16),
        pltpu.VMEM((width, TILE), F32),
    ]
    left = pl.pallas_call(
        left_columns,
        out_shape=shape((width, TILE), BF16),
        in_specs=[SCALARS, WHOLE, WHOLE, WHOLE],
        out_specs=WHOLE,
        scratch_shapes=unpacked,
        compiler_params=PARAMS,
        name="left_columns",
    )(scalars, mine, other, diag)
    gates = [(i, i // holders) for i in range(members)]
    near = lax.ppermute(
        left, ("dp", "mp"), [(i * columns + g, i * columns + (g ^ 1)) for i, g in gates]
    )
    gate = member // holders
    left = jnp.where(column == gate, left, near)
    left = jnp.where(
        column // 2 == gate // 2,
        left,
        sum(
            lax.ppermute(
                left,
                ("dp", "mp"),
                [
                    (i * columns + g, i * columns + (g + 2 * step) % columns)
                    for i, at in gates
                    for g in (at, at ^ 1)
                ],
            )
            for step in range(1, columns // 2)
        ),
    )
    right, factor_out, inverse_out = pl.pallas_call(
        new_blocks,
        out_shape=(
            shape((width, width), BF16),
            shape((width, width), F32),
            shape((width, width), F32),
        ),
        in_specs=[SCALARS, WHOLE, WHOLE, WHOLE, WHOLE, WHOLE],
        out_specs=(WHOLE, WHOLE, WHOLE),
        scratch_shapes=unpacked,
        compiler_params=PARAMS,
        name="new_blocks",
    )(scalars, mine, other, far_mine, far_other, diag)

    grad = across_ring((near_grad + arrived_grad.astype(F32)).astype(BF16))
    grad = jnp.sum(grad.astype(F32), axis=0).astype(BF16)
    neighbours = [[holders * c + r for r in range(holders)] for c in range(columns)]
    grads = lax.all_gather(grad, "dp", axis=0, axis_index_groups=neighbours)

    result, curvature = pl.pallas_call(
        precondition,
        out_shape=(shape((TILE, width), F32), shape((8, TILE), F32)),
        in_specs=[SCALARS, WHOLE, WHOLE, WHOLE],
        out_specs=(WHOLE, WHOLE),
        compiler_params=PARAMS,
        name="precondition",
    )(place[None], grads, left, right)

    curvature = lax.all_to_all(
        jnp.broadcast_to(curvature, (members, 8, TILE)), "dp", 0, 0, tiled=True
    )
    curvature = jnp.sum(curvature, axis=0)
    curvature = lax.all_to_all(
        jnp.broadcast_to(curvature, (columns, 8, TILE)), "mp", 0, 0, tiled=True
    )
    curvature = jnp.sum(curvature, axis=0)[0, 0]
    entries = float(feature_count * width * columns)
    clip_scale = jnp.minimum(1.0, jnp.sqrt(entries / jnp.abs(curvature)))
    return (factor_out[None, None], inverse_out[None, None], clip_scale * result)


def solution(mesh):
    return jax.shard_map(
        local,
        mesh=mesh,
        in_specs=(
            P("dp", None),
            P("dp", "mp"),
            P("dp"),
            P("mp", "dp", None, None, None),
            P("mp", "dp", None, None, None),
            P(),
            P(),
        ),
        out_specs=(P("mp", "dp", None, None), P("mp", "dp", None, None), P("dp", "mp")),
        check_vma=False,
    )
```

```python
import jax
import jax.numpy as jnp
from jax import lax
from jax.experimental import pallas as pl
from jax.experimental.pallas import tpu as pltpu
from jax.sharding import PartitionSpec as P

DECAY = 0.9
DAMPING = 0.01
TILE = 128
ROWS = 16
VMEM_BYTES = 48 * 1024 * 1024
BF16 = jnp.bfloat16
F32 = jnp.float32
PARAMS = pltpu.CompilerParams(vmem_limit_bytes=VMEM_BYTES)
SCALARS = pl.BlockSpec(memory_space=pltpu.SMEM)
WHOLE = pl.BlockSpec(memory_space=pltpu.VMEM)
ANYWHERE = pl.BlockSpec(memory_space=pltpu.HBM)


def upper_pairs(tiles):
    return [(a, b) for a in range(tiles) for b in range(a, tiles)]


def diagonal_mask():
    rows = lax.broadcasted_iota(jnp.int32, (TILE, TILE), 0)
    return rows == lax.broadcasted_iota(jnp.int32, (TILE, TILE), 1)


def tile_of(a, b):
    return (slice(a * TILE, (a + 1) * TILE), slice(b * TILE, (b + 1) * TILE))


class Facts:
    def __init__(self, old_owner=None, new_owner=None):
        member = lax.axis_index("dp")
        self.column = lax.axis_index("mp")
        chips = lax.axis_size("dp") // 2
        self.core = member & 1
        self.plane = jnp.where(member >= chips, 1, 0)
        self.place = member & (lax.axis_size("dp") // lax.axis_size("mp") - 1)
        self.flip = jnp.where(self.column >= lax.axis_size("mp") // 2, 1, 0)
        self.own_kind = self.plane ^ self.flip
        if old_owner is not None:
            owners = [old_owner[self.column, kind] for kind in range(2)]
            self.shared = jnp.where(owners[0] == owners[1], 1, 0)
            self.same_core = [jnp.where((o & 1) == self.core, 1, 0) for o in owners]
            self.same_plane = [
                jnp.where(jnp.where(o >= chips, 1, 0) == self.plane, 1, 0) for o in owners
            ]
            self.ring_at = [lax.shift_right_logical(o & (chips - 1), 1) for o in owners]
        if new_owner is not None:
            self.keeps = [
                jnp.where(new_owner[self.column, kind] == member, 1, 0) for kind in range(2)
            ]


def pack_old(owners, factors, inverses, keep, send, held, packed, diag, arrived):
    facts = Facts(owners)
    core, flip = facts.core, facts.flip
    tiles = held.shape[1] // TILE
    on_diagonal = diagonal_mask()
    loads = [
        pltpu.make_async_copy(
            source.at[facts.shared if kind else 0], held.at[which * 2 + kind], arrived.at[which * 2 + kind]
        )
        for which, source in enumerate((factors, inverses))
        for kind in range(2)
    ]
    for load in loads:
        load.start()
    for which in range(2):
        for kind in range(2):
            loads[which * 2 + kind].wait()
            for n, (a, b) in enumerate(upper_pairs(tiles)):
                piece = held[(which * 2 + kind,) + tile_of(a, b)]
                if a == b:
                    row = (which * 2 + kind) * tiles + a
                    diag[row : row + 1, :] = jnp.sum(
                        jnp.where(on_diagonal, piece, 0.0), axis=0, keepdims=True
                    )
                    piece = jnp.where(on_diagonal, 0.0, piece)
                packed[kind, which, n * TILE : (n + 1) * TILE, :] = piece.astype(BF16)
    high = diag[...].astype(BF16)
    low = (diag[...] - high.astype(F32)).astype(BF16)
    words = jnp.concatenate([high, low], axis=0)
    chips = keep.shape[0]
    share = (keep.shape[1] - words.shape[0]) // 2
    for q in range(chips):
        plane, pair = divmod(q, chips // 2)
        kind = flip if plane == 0 else 1 - flip
        for ref, parity in ((keep, core), (send, 1 - core)):
            start = pl.multiple_of((2 * pair + parity) * share, ROWS)
            for which in range(2):
                ref[q, which * share : (which + 1) * share, :] = packed[
                    kind, which, pl.ds(start, share), :
                ]
            ref[q, 2 * share :, :] = words


def covariance_parts(counts, features, out_grads, keep, send, turned, own, grads, kept, packed, arrived):
    facts = Facts()
    core, flip, count = facts.core, facts.flip, counts[0]
    rows, width = own.shape
    start = pl.multiple_of(facts.column * width, width)
    loads = [
        pltpu.make_async_copy(features.at[:, pl.ds(start, width)], own, arrived.at[0]),
        pltpu.make_async_copy(out_grads, grads, arrived.at[1]),
    ]
    for load in loads:
        load.start()
    tiles = width // TILE
    valid = lax.broadcasted_iota(jnp.int32, (rows, width), 0) < count
    for kind, (block, left) in enumerate(((own, kept), (grads, turned))):
        loads[kind].wait()
        left[...] = jnp.where(valid, block[...].astype(F32), 0.0).T.astype(BF16)
        for a, b in upper_pairs(tiles // 2):
            square = jnp.dot(
                left[2 * a * TILE : 2 * (a + 1) * TILE, :],
                block[:, 2 * b * TILE : 2 * (b + 1) * TILE],
                preferred_element_type=F32,
            ).astype(BF16)
            for i in range(2):
                for j in range(2):
                    if 2 * a + i <= 2 * b + j:
                        at = upper_pairs(tiles).index((2 * a + i, 2 * b + j))
                        packed[kind, at * TILE : (at + 1) * TILE, :] = square[tile_of(i, j)]
    quarter = lax.broadcasted_iota(jnp.int32, (ROWS, TILE), 0) // 4
    digits = lax.shift_right_logical(jnp.full((ROWS, TILE), count), 3 * quarter) & 7
    digits = digits.astype(F32).astype(BF16)
    chips = keep.shape[0]
    share = keep.shape[1] - ROWS
    for q in range(chips):
        plane, pair = divmod(q, chips // 2)
        kind = flip if plane == 0 else 1 - flip
        for ref, parity in ((keep, core), (send, 1 - core)):
            start = pl.multiple_of((2 * pair + parity) * share, ROWS)
            ref[q, :share, :] = packed[kind, pl.ds(start, share), :]
            ref[q, share:, :] = digits


def merge_words(first_flag, second_flag, one, two):
    lanes = one.shape[0] // 8
    kinds = (lax.broadcasted_iota(jnp.int32, one.shape, 0) // lanes) % 2
    flags = jnp.where(kinds == 0, first_flag, second_flag)
    return jnp.where(flags == 1, one.astype(F32), two.astype(F32))


def choose_core(owners, keep, received, near, far):
    facts = Facts(owners)
    first, second = facts.same_core
    plane, own_kind = facts.plane, facts.own_kind
    ring, rows = near.shape[0], near.shape[1]
    data = rows // 6 * 5
    words = merge_words(first, second, keep[0, data:, :], received[0, data:, :]).astype(BF16)
    for ref, at, kind in ((near, plane, own_kind), (far, 1 - plane, 1 - own_kind)):
        flag = jnp.where(kind == 0, first, second)

        @pl.when(flag == 1)
        def _():
            ref[:, :data, :] = keep[pl.ds(at * ring, ring), :data, :]

        @pl.when(flag == 0)
        def _():
            ref[:, :data, :] = received[pl.ds(at * ring, ring), :data, :]

        for z in range(ring):
            ref[z, data:, :] = words


def add_core(keep, received, near, far):
    plane = Facts().plane
    ring = near.shape[0]
    for ref, at in ((near, plane), (far, 1 - plane)):
        chips = pl.ds(at * ring, ring)
        total = keep[chips].astype(F32) + received[chips].astype(F32)
        ref[...] = total.astype(ref.dtype)


def join_planes(owners, near, arrived, near_sum, arrived_sum, unread, out, untouched):
    facts = Facts(owners)
    first, second = facts.same_plane
    own_kind = facts.own_kind
    ring, rows = near.shape[0], near.shape[1]
    data = rows // 6 * 5
    flag = jnp.where(own_kind == 0, first, second)

    @pl.when(flag == 1)
    def _():
        out[:, :data, :] = near[:, :data, :]

    @pl.when(flag == 0)
    def _():
        out[:, :data, :] = arrived[:, :data, :]

    words = merge_words(first, second, near[0, data:, :], arrived[0, data:, :]).astype(BF16)
    for z in range(ring):
        out[z, data:rows, :] = words
    out[:, rows:, :] = (near_sum[...] + arrived_sum[...].astype(F32)).astype(BF16)


def make_shares(owners, arrived, shares, diag):
    facts = Facts(owners)
    own_kind = facts.own_kind
    first, second = facts.ring_at
    ring, rows = shares.shape[0], shares.shape[1]
    share = rows // 2
    words = rows // 5 + rows
    owner = jnp.where(own_kind == 0, first, second)
    both = merge_words(1, 0, arrived[first, rows:words, :], arrived[second, rows:words, :])
    diag[...] = both[: diag.shape[0]] + both[diag.shape[0] :]
    summed = sum(arrived[z, words:, :].astype(F32) for z in range(ring))
    total = sum(summed[share + 4 * d : share + 4 * d + 1, :] * float(8**d) for d in range(4))
    factor = DECAY * arrived[owner, :share, :].astype(F32) + (1.0 - DECAY) * summed[:share] / total
    factor = factor.astype(BF16)
    inverse = arrived[owner, share:rows, :]
    for z in range(ring):
        shares[z, :share, :] = factor
        shares[z, share:, :] = inverse


def gradient_tiles(turned, tiles):
    block = jnp.concatenate([tile[...] for tile in tiles], axis=1)
    return jnp.dot(turned[...], block, preferred_element_type=F32)


def gradient_send(scalars, turned, *refs):
    tiles, send = refs[:4], refs[-1]
    product = gradient_tiles(turned, tiles)
    for n in range(4):
        send[n] = product[:, n * TILE : (n + 1) * TILE].astype(send.dtype)


def gradient_add(scalars, turned, *refs):
    tiles, received, out = refs[:4], refs[4], refs[-1]
    product = gradient_tiles(turned, tiles)
    for n in range(4):
        total = product[:, n * TILE : (n + 1) * TILE] + received[n].astype(F32)
        out[n] = total.astype(out.dtype)


def unpack(mine, other, core, packed):
    share = mine.shape[1] // 2
    for pair in range(mine.shape[0]):
        for ref, parity in ((mine, core), (other, 1 - core)):
            start = pl.multiple_of((2 * pair + parity) * share, ROWS)
            for which in range(2):
                packed[which, pl.ds(start, share), :] = ref[
                    pair, which * share : (which + 1) * share, :
                ]


def spread(packed, which, diag, row, scale, high, low):
    tiles = high.shape[0] // TILE
    on_diagonal = diagonal_mask()
    for n, (a, b) in enumerate(upper_pairs(tiles)):
        piece = packed[which, n * TILE : (n + 1) * TILE, :].astype(F32)
        if a == b:
            exact = piece + jnp.where(on_diagonal, scale * diag[row + a : row + a + 1, :], 0.0)
            rounded = exact.astype(BF16)
            high[tile_of(a, a)] = rounded
            rest = jnp.sum(exact - rounded.astype(F32), axis=1, keepdims=True)
            low[a * TILE : (a + 1) * TILE, :] = jnp.broadcast_to(rest, (TILE, TILE))
        else:
            high[tile_of(a, b)] = packed[which, n * TILE : (n + 1) * TILE, :]
            high[tile_of(b, a)] = piece.T.astype(BF16)


def fill_blocks(kind, packed, diag, factor, factor_low, inverse, inverse_low):
    tiles = factor.shape[0] // TILE
    spread(packed, 0, diag, kind * tiles, DECAY, factor, factor_low)
    spread(packed, 1, diag, (2 + kind) * tiles, 1.0, inverse, inverse_low)


def times(high, low, right):
    width = right.shape[1]
    first = right.astype(BF16)
    second = (right - first.astype(F32)).astype(BF16)
    both = jnp.dot(high[...], jnp.concatenate([first, second], axis=1), preferred_element_type=F32)
    return both[:, :width] + both[:, width:] + low * right


def refine(factor, factor_low, inverse, inverse_low, part):
    inner = times(factor, factor_low[:, :1] + DAMPING, part)
    return 2.0 * part - times(inverse, inverse_low[:, :1], inner)


def exact_block(high, low):
    rows = lax.broadcasted_iota(jnp.int32, high.shape, 0)
    columns = lax.broadcasted_iota(jnp.int32, high.shape, 1)
    return high[...].astype(F32) + jnp.where(rows == columns, low[:, :1], 0.0)


def left_columns(mine, other, diag, left, packed, factor, factor_low, inverse, inverse_low):
    facts = Facts()
    core, place = facts.core, facts.place
    unpack(mine, other, core, packed)
    fill_blocks(0, packed, diag, factor, factor_low, inverse, inverse_low)
    start = pl.multiple_of(place * TILE, TILE)
    part = inverse[:, pl.ds(start, TILE)].astype(F32)
    rows = lax.broadcasted_iota(jnp.int32, part.shape, 0) - start
    part = part + jnp.where(
        rows == lax.broadcasted_iota(jnp.int32, part.shape, 1), inverse_low[...], 0.0
    )
    left[...] = refine(factor, factor_low, inverse, inverse_low, part).astype(BF16)


def new_blocks(
    owners, mine, other, far_mine, far_other, diag, right, factor_out, inverse_out,
    packed, factor, factor_low, inverse, inverse_low,
):
    facts = Facts(new_owner=owners)
    core, own_kind = facts.core, facts.own_kind
    first, second = facts.keeps
    blocks = (factor, factor_low, inverse, inverse_low)

    def load_blocks(kind):
        @pl.when(own_kind == kind)
        def _():
            unpack(mine, other, core, packed)

        @pl.when(own_kind != kind)
        def _():
            unpack(far_mine, far_other, core, packed)

        fill_blocks(kind, packed, diag, *blocks)

    load_blocks(1)
    fresh = refine(*blocks, exact_block(inverse, inverse_low))
    right[...] = fresh.astype(BF16)

    @pl.when(second == 1)
    def _():
        factor_out[...] = exact_block(factor, factor_low)
        inverse_out[...] = fresh

    @pl.when(second == 0)
    def _():
        factor_out[...] = jnp.zeros_like(factor_out)
        inverse_out[...] = jnp.zeros_like(inverse_out)

    @pl.when(first == 1)
    def _():
        load_blocks(0)
        factor_out[...] = exact_block(factor, factor_low)
        inverse_out[...] = refine(*blocks, exact_block(inverse, inverse_low))


def precondition(grad, left, right, result, curvature):
    own = Facts().place
    half = sum(
        jnp.dot(grad[p], left[p * TILE : (p + 1) * TILE, :], preferred_element_type=F32)
        for p in range(grad.shape[0])
    )
    product = jnp.dot(half.T.astype(BF16), right[...], preferred_element_type=F32)
    result[...] = product
    curvature[...] = jnp.full(curvature.shape, jnp.sum(product * grad[own].astype(F32).T))


def kernel_call(body, out_shape, in_specs, scratch=(), out_specs=None, aliases=None, flops=0, moved=0):
    if out_specs is None:
        out_specs = (WHOLE,) * len(out_shape) if isinstance(out_shape, tuple) else WHOLE
    return pl.pallas_call(
        body,
        out_shape=out_shape,
        in_specs=in_specs,
        out_specs=out_specs,
        input_output_aliases=aliases or {},
        scratch_shapes=list(scratch),
        compiler_params=PARAMS,
        cost_estimate=pl.CostEstimate(flops=flops, bytes_accessed=moved, transcendentals=0),
        name=body.__name__,
    )


def local(features, out_grads, counts, factor_old, inverse_old, old_owner, new_owner):
    tok_rows, width = out_grads.shape
    feature_count = features.shape[1]
    column = lax.axis_index("mp")
    member = lax.axis_index("dp")
    members = lax.axis_size("dp")
    columns = lax.axis_size("mp")
    chips = members // 2
    ring = chips // 2
    core = member & 1
    core_swap = [(i, i ^ 1) for i in range(members)]
    plane_swap = [(i, (i + chips) % members) for i in range(members)]
    rings = [[y * chips + 2 * z + c for z in range(ring)] for y in range(2) for c in range(2)]
    packed_rows = width * (width + TILE) // 2 // TILE
    share = 2 * packed_rows // members
    lanes = width // TILE
    holders = members // columns
    shape = jax.ShapeDtypeStruct
    megabyte = 2 * width * width * 2

    def across_ring(parts):
        return lax.all_to_all(parts, "dp", 0, 0, tiled=True, axis_index_groups=rings)

    def swap_cores(send):
        return lax.ppermute(send, "dp", core_swap)

    def swap_planes(send):
        return lax.ppermute(send, "dp", plane_swap)

    message = shape((chips, 2 * share + 8 * lanes, TILE), BF16)
    keep, send = kernel_call(
        pack_old,
        (message, message),
        [SCALARS, ANYWHERE, ANYWHERE],
        [
            pltpu.VMEM((4, width, width), F32),
            pltpu.VMEM((2, 2, packed_rows, TILE), BF16),
            pltpu.VMEM((4 * lanes, TILE), F32),
            pltpu.SemaphoreType.DMA((4,)),
        ],
        moved=6 * megabyte,
    )(old_owner, factor_old[0, 0], inverse_old[0, 0])
    half_message = shape((ring,) + message.shape[1:], BF16)
    near_old, far_old = kernel_call(
        choose_core, (half_message, half_message), [SCALARS, WHOLE, WHOLE], moved=megabyte
    )(old_owner, keep, swap_cores(send))
    arrived_old = swap_planes(far_old)

    message = shape((chips, share + ROWS, TILE), BF16)
    keep, send, turned = kernel_call(
        covariance_parts,
        (message, message, shape((width, tok_rows), BF16)),
        [SCALARS, ANYWHERE, ANYWHERE],
        [
            pltpu.VMEM((tok_rows, width), BF16),
            pltpu.VMEM((tok_rows, width), BF16),
            pltpu.VMEM((width, tok_rows), BF16),
            pltpu.VMEM((2, packed_rows, TILE), BF16),
            pltpu.SemaphoreType.DMA((2,)),
        ],
        flops=4 * tok_rows * width * width,
        moved=6 * megabyte,
    )(counts, features, out_grads)
    half_shape = (ring,) + message.shape[1:]
    near_sum, far_sum = kernel_call(
        add_core, (shape(half_shape, F32), shape(half_shape, BF16)), [WHOLE, WHOLE], moved=megabyte
    )(keep, swap_cores(send))
    arrived_sum = swap_planes(far_sum)

    def gradient(body, tile_at, count, dtype, name, *others):
        def tile_spec(n):
            return pl.BlockSpec((tok_rows, TILE), lambda i, s: (0, 2 * tile_at(4 * i + n, s) + s[0]))

        message_spec = pl.BlockSpec((4, width, TILE), lambda i, s: (i, 0, 0))
        received_spec = pl.BlockSpec((4, width, TILE), lambda i, s: (tile_at(4 * i, s) // 4, 0, 0))
        other_specs = [received_spec] if len(others) == 1 else [ANYWHERE] * 2
        parity = 1 - core if len(others) == 2 else core
        return pl.pallas_call(
            body,
            out_shape=shape((count, width, TILE), dtype),
            grid_spec=pltpu.PrefetchScalarGridSpec(
                num_scalar_prefetch=1,
                grid=(count // 4,),
                in_specs=[pl.BlockSpec((width, tok_rows), lambda i, s: (0, 0))]
                + [tile_spec(n) for n in range(4)]
                + other_specs,
                out_specs=message_spec,
            ),
            compiler_params=PARAMS,
            cost_estimate=pl.CostEstimate(
                flops=2 * tok_rows * width * TILE * count,
                bytes_accessed=(count // 2) * megabyte,
                transcendentals=0,
            ),
            name=name,
        )(
            jnp.stack([parity, jnp.where(member >= chips, 1, 0)]),
            turned, features, features, features, features, *others,
        )

    send = gradient(gradient_send, lambda q, s: q, chips, BF16, "gradient_send", far_old, far_sum)
    joined, send = kernel_call(
        join_planes,
        (
            shape((ring, near_old.shape[1] + near_sum.shape[1], TILE), BF16),
            shape(send.shape, send.dtype),
        ),
        [SCALARS] + [WHOLE] * 4 + [ANYWHERE],
        out_specs=(WHOLE, ANYWHERE),
        aliases={5: 1},
        moved=megabyte,
    )(old_owner, near_old, arrived_old, near_sum, arrived_sum, send)
    received = swap_cores(send)
    far_grad = gradient(
        gradient_add, lambda q, s: (1 - s[1]) * ring + q, ring, BF16, "gradient_far", received
    )
    arrived_grad = swap_planes(far_grad)
    near_grad = gradient(
        gradient_add, lambda q, s: s[1] * ring + q, ring, F32, "gradient_near", received
    )

    shares, diag = kernel_call(
        make_shares,
        (shape((ring, 2 * share, TILE), BF16), shape((4 * lanes, TILE), F32)),
        [SCALARS, WHOLE],
        moved=megabyte,
    )(old_owner, across_ring(joined))

    mine = across_ring(shares)
    other = swap_cores(mine)
    far_mine = swap_planes(mine)
    far_other = swap_cores(far_mine)
    unpacked = [
        pltpu.VMEM((2, packed_rows, TILE), BF16),
        pltpu.VMEM((width, width), BF16),
        pltpu.VMEM((width, TILE), F32),
        pltpu.VMEM((width, width), BF16),
        pltpu.VMEM((width, TILE), F32),
    ]
    left = kernel_call(
        left_columns,
        shape((width, TILE), BF16),
        [WHOLE] * 3,
        unpacked,
        flops=8 * width * width * TILE,
        moved=2 * megabyte,
    )(mine, other, diag)
    gates = [(i, i // holders) for i in range(members)]
    near = lax.ppermute(
        left, ("dp", "mp"), [(i * columns + g, i * columns + (g ^ 1)) for i, g in gates]
    )
    gate = lax.shift_right_logical(member, holders.bit_length() - 1)
    left = jnp.where(column == gate, left, near)
    left = jnp.where(
        (column ^ gate) <= 1,
        left,
        sum(
            lax.ppermute(
                left,
                ("dp", "mp"),
                [
                    (i * columns + g, i * columns + (g + 2 * step) % columns)
                    for i, at in gates
                    for g in (at, at ^ 1)
                ],
            )
            for step in range(1, columns // 2)
        ),
    )
    square = shape((width, width), F32)
    right, factor_out, inverse_out = kernel_call(
        new_blocks,
        (shape((width, width), BF16), square, square),
        [SCALARS] + [WHOLE] * 5,
        unpacked,
        flops=8 * width * width * width,
        moved=6 * megabyte,
    )(new_owner, mine, other, far_mine, far_other, diag)

    grad = across_ring((near_grad + arrived_grad.astype(F32)).astype(BF16))
    grad = jnp.sum(grad.astype(F32), axis=0).astype(BF16)
    neighbours = [[holders * c + r for r in range(holders)] for c in range(columns)]
    grads = lax.all_gather(grad, "dp", axis=0, axis_index_groups=neighbours)
    result, curvature = kernel_call(
        precondition,
        (shape((TILE, width), F32), shape((8, TILE), F32)),
        [WHOLE] * 3,
        flops=4 * width * width * TILE,
        moved=megabyte,
    )(grads, left, right)

    planes = [[y * chips + i for i in range(chips)] for y in range(2)]
    curvature = lax.all_to_all(
        jnp.broadcast_to(curvature, (chips, 8, TILE)),
        "dp", 0, 0, tiled=True, axis_index_groups=planes,
    )
    curvature = jnp.sum(curvature, axis=0)
    rings = [
        [(y * chips + i) * columns + c for y in range(2) for c in range(columns)] for i in range(chips)
    ]
    curvature = lax.all_to_all(
        jnp.broadcast_to(curvature, (2 * columns, 8, TILE)),
        ("dp", "mp"), 0, 0, tiled=True, axis_index_groups=rings,
    )
    curvature = jnp.sum(curvature, axis=0)[0, 0]
    entries = float(feature_count * width * columns)
    clip_scale = jnp.minimum(1.0, jnp.sqrt(entries / jnp.abs(curvature)))
    return (factor_out[None, None], inverse_out[None, None], clip_scale * result)


def solution(mesh):
    return jax.shard_map(
        local,
        mesh=mesh,
        in_specs=(
            P("dp", None),
            P("dp", "mp"),
            P("dp"),
            P("mp", "dp", None, None, None),
            P("mp", "dp", None, None, None),
            P(),
            P(),
        ),
        out_specs=(P("mp", "dp", None, None), P("mp", "dp", None, None), P("dp", "mp")),
        check_vma=False,
    )
```

```python
import jax
import jax.numpy as jnp
from jax import lax
from jax.experimental import pallas as pl
from jax.experimental.pallas import tpu as pltpu
from jax.sharding import PartitionSpec as P

DECAY = 0.9
DAMPING = 0.01
TILE = 128
ROWS = 16
VMEM_BYTES = 48 * 1024 * 1024
BF16 = jnp.bfloat16
F32 = jnp.float32
PARAMS = pltpu.CompilerParams(vmem_limit_bytes=VMEM_BYTES)
SCALARS = pl.BlockSpec(memory_space=pltpu.SMEM)
WHOLE = pl.BlockSpec(memory_space=pltpu.VMEM)
ANYWHERE = pl.BlockSpec(memory_space=pltpu.HBM)


def upper_pairs(tiles):
    return [(a, b) for a in range(tiles) for b in range(a, tiles)]


def diagonal_mask():
    rows = lax.broadcasted_iota(jnp.int32, (TILE, TILE), 0)
    return rows == lax.broadcasted_iota(jnp.int32, (TILE, TILE), 1)


def tile_of(a, b):
    return (slice(a * TILE, (a + 1) * TILE), slice(b * TILE, (b + 1) * TILE))


class Facts:
    def __init__(self, old_owner=None, new_owner=None):
        member = lax.axis_index("dp")
        self.column = lax.axis_index("mp")
        chips = lax.axis_size("dp") // 2
        self.core = member & 1
        self.plane = jnp.where(member >= chips, 1, 0)
        self.ring = lax.shift_right_logical(member & (chips - 1), 1)
        self.place = member & (lax.axis_size("dp") // lax.axis_size("mp") - 1)
        self.flip = jnp.where(self.column >= lax.axis_size("mp") // 2, 1, 0)
        self.own_kind = self.plane ^ self.flip
        if old_owner is not None:
            owners = [old_owner[self.column, kind] for kind in range(2)]
            self.shared = jnp.where(owners[0] == owners[1], 1, 0)
            self.same_core = [jnp.where((o & 1) == self.core, 1, 0) for o in owners]
            self.same_plane = [
                jnp.where(jnp.where(o >= chips, 1, 0) == self.plane, 1, 0) for o in owners
            ]
            self.ring_at = [lax.shift_right_logical(o & (chips - 1), 1) for o in owners]
        if new_owner is not None:
            self.keeps = [
                jnp.where(new_owner[self.column, kind] == member, 1, 0) for kind in range(2)
            ]


def pack_old(owners, factors, inverses, unread, keep, send, held, packed, diag, arrived):
    facts = Facts(owners)
    core, flip = facts.core, facts.flip
    tiles = held.shape[1] // TILE
    on_diagonal = diagonal_mask()
    loads = [
        pltpu.make_async_copy(
            source.at[facts.shared if kind else 0], held.at[which * 2 + kind], arrived.at[which * 2 + kind]
        )
        for which, source in enumerate((factors, inverses))
        for kind in range(2)
    ]
    for load in loads:
        load.start()
    for which in range(2):
        for kind in range(2):
            loads[which * 2 + kind].wait()
            for n, (a, b) in enumerate(upper_pairs(tiles)):
                piece = held[(which * 2 + kind,) + tile_of(a, b)]
                if a == b:
                    row = (which * 2 + kind) * tiles + a
                    diag[row : row + 1, :] = jnp.sum(
                        jnp.where(on_diagonal, piece, 0.0), axis=0, keepdims=True
                    )
                    piece = jnp.where(on_diagonal, 0.0, piece)
                packed[kind, which, n * TILE : (n + 1) * TILE, :] = piece.astype(BF16)
    high = diag[...].astype(BF16)
    low = (diag[...] - high.astype(F32)).astype(BF16)
    words = jnp.concatenate([high, low], axis=0)
    chips = keep.shape[0]
    share = (keep.shape[1] - words.shape[0]) // 2
    for q in range(chips):
        plane, pair = divmod(q, chips // 2)
        kind = flip if plane == 0 else 1 - flip
        for ref, parity in ((keep, core), (send, 1 - core)):
            start = pl.multiple_of((2 * pair + parity) * share, ROWS)
            for which in range(2):
                ref[q, which * share : (which + 1) * share, :] = packed[
                    kind, which, pl.ds(start, share), :
                ]
            ref[q, 2 * share :, :] = words


def covariance_parts(counts, features, out_grads, keep, send, turned, own, grads, kept, packed, arrived):
    facts = Facts()
    core, flip, count = facts.core, facts.flip, counts[0]
    rows, width = own.shape
    start = pl.multiple_of(facts.column * width, width)
    loads = [
        pltpu.make_async_copy(features.at[:, pl.ds(start, width)], own, arrived.at[0]),
        pltpu.make_async_copy(out_grads, grads, arrived.at[1]),
    ]
    for load in loads:
        load.start()
    tiles = width // TILE
    valid = lax.broadcasted_iota(jnp.int32, (rows, width), 0) < count
    for kind, (block, left) in enumerate(((own, kept), (grads, turned))):
        loads[kind].wait()
        left[...] = jnp.where(valid, block[...].astype(F32), 0.0).T.astype(BF16)
        for a, b in upper_pairs(tiles // 2):
            square = jnp.dot(
                left[2 * a * TILE : 2 * (a + 1) * TILE, :],
                block[:, 2 * b * TILE : 2 * (b + 1) * TILE],
                preferred_element_type=F32,
            ).astype(BF16)
            for i in range(2):
                for j in range(2):
                    if 2 * a + i <= 2 * b + j:
                        at = upper_pairs(tiles).index((2 * a + i, 2 * b + j))
                        packed[kind, at * TILE : (at + 1) * TILE, :] = square[tile_of(i, j)]
    quarter = lax.broadcasted_iota(jnp.int32, (ROWS, TILE), 0) // 4
    digits = lax.shift_right_logical(jnp.full((ROWS, TILE), count), 3 * quarter) & 7
    digits = digits.astype(F32).astype(BF16)
    chips = keep.shape[0]
    share = keep.shape[1] - ROWS
    for q in range(chips):
        plane, pair = divmod(q, chips // 2)
        kind = flip if plane == 0 else 1 - flip
        for ref, parity in ((keep, core), (send, 1 - core)):
            start = pl.multiple_of((2 * pair + parity) * share, ROWS)
            ref[q, :share, :] = packed[kind, pl.ds(start, share), :]
            ref[q, share:, :] = digits


def merge_words(first_flag, second_flag, one, two):
    lanes = one.shape[0] // 8
    kinds = (lax.broadcasted_iota(jnp.int32, one.shape, 0) // lanes) % 2
    flags = jnp.where(kinds == 0, first_flag, second_flag)
    return jnp.where(flags == 1, one.astype(F32), two.astype(F32))


def choose_core(owners, keep, received, near, far):
    facts = Facts(owners)
    first, second = facts.same_core
    plane, own_kind = facts.plane, facts.own_kind
    ring, rows = near.shape[0], near.shape[1]
    data = rows // 6 * 5
    words = merge_words(first, second, keep[0, data:, :], received[0, data:, :]).astype(BF16)
    for ref, at, kind in ((near, plane, own_kind), (far, 1 - plane, 1 - own_kind)):
        flag = jnp.where(kind == 0, first, second)

        @pl.when(flag == 1)
        def _():
            ref[:, :data, :] = keep[pl.ds(at * ring, ring), :data, :]

        @pl.when(flag == 0)
        def _():
            ref[:, :data, :] = received[pl.ds(at * ring, ring), :data, :]

        for z in range(ring):
            ref[z, data:, :] = words


def add_core(keep, received, near, far):
    plane = Facts().plane
    ring = near.shape[0]
    for ref, at in ((near, plane), (far, 1 - plane)):
        chips = pl.ds(at * ring, ring)
        total = keep[chips].astype(F32) + received[chips].astype(F32)
        ref[...] = total.astype(ref.dtype)


def join_planes(owners, near, arrived, near_sum, arrived_sum, *outs):
    facts = Facts(owners)
    first, second = facts.same_plane
    flag = jnp.where(facts.own_kind == 0, first, second)
    ring, rows = near.shape[0], near.shape[1]
    data = rows // 6 * 5
    words = merge_words(first, second, near[0, data:, :], arrived[0, data:, :]).astype(BF16)
    for step, out in enumerate(outs):
        at = (facts.ring + step) & (ring - 1)

        @pl.when(flag == 1)
        def _():
            out[:data, :] = near[at, :data, :]

        @pl.when(flag == 0)
        def _():
            out[:data, :] = arrived[at, :data, :]

        out[data:rows, :] = words
        out[rows:, :] = (near_sum[at] + arrived_sum[at].astype(F32)).astype(BF16)


def make_shares(owners, *refs):
    pieces, shares, diag, arrived = refs[:-3], refs[-3], refs[-2], refs[-1]
    facts = Facts(owners)
    ring, rows = len(pieces), shares.shape[0]
    share = rows // 2
    words = rows // 5 + rows
    first, second = [(facts.ring - at) & (ring - 1) for at in facts.ring_at]
    for step, piece in enumerate(pieces):
        arrived[step] = piece[...]
    owner = jnp.where(facts.own_kind == 0, first, second)
    both = merge_words(1, 0, arrived[first, rows:words, :], arrived[second, rows:words, :])
    diag[...] = both[: diag.shape[0]] + both[diag.shape[0] :]
    summed = sum(piece[words:, :].astype(F32) for piece in pieces)
    total = sum(summed[share + 4 * d : share + 4 * d + 1, :] * float(8**d) for d in range(4))
    factor = DECAY * arrived[owner, :share, :].astype(F32) + (1.0 - DECAY) * summed[:share] / total
    shares[:share, :] = factor.astype(BF16)
    shares[share:, :] = arrived[owner, share:rows, :]


def collect(*refs):
    for step, piece in enumerate(refs[:-1]):
        refs[-1][step] = piece[...]


def add_planes(near, arrived, *outs):
    position = Facts().ring
    for step, out in enumerate(outs):
        at = (position + step) & (near.shape[0] - 1)
        out[...] = (near[at] + arrived[at].astype(F32)).astype(out.dtype)


def add_ring(*refs):
    refs[-1][...] = sum(piece[...].astype(F32) for piece in refs[:-1]).astype(BF16)


def gradient_tiles(turned, tiles):
    block = jnp.concatenate([tile[...] for tile in tiles], axis=1)
    return jnp.dot(turned[...], block, preferred_element_type=F32)


def gradient_send(scalars, turned, *refs):
    tiles, send = refs[:4], refs[-1]
    product = gradient_tiles(turned, tiles)
    for n in range(4):
        send[n] = product[:, n * TILE : (n + 1) * TILE].astype(send.dtype)


def gradient_add(scalars, turned, *refs):
    tiles, received = refs[:4], refs[4]
    out = refs[5 + (len(refs) - 6) // 2]
    product = gradient_tiles(turned, tiles)
    for n in range(4):
        total = product[:, n * TILE : (n + 1) * TILE] + received[n].astype(F32)
        out[n] = total.astype(out.dtype)


def unpack(mine, other, core, packed):
    share = mine.shape[1] // 2
    position = Facts().ring
    for step in range(mine.shape[0]):
        pair = (position - step) & (mine.shape[0] - 1)
        for ref, parity in ((mine, core), (other, 1 - core)):
            start = pl.multiple_of((2 * pair + parity) * share, ROWS)
            for which in range(2):
                packed[which, pl.ds(start, share), :] = ref[
                    step, which * share : (which + 1) * share, :
                ]


def spread(packed, which, diag, row, scale, high, low):
    tiles = high.shape[0] // TILE
    on_diagonal = diagonal_mask()
    for n, (a, b) in enumerate(upper_pairs(tiles)):
        piece = packed[which, n * TILE : (n + 1) * TILE, :].astype(F32)
        if a == b:
            exact = piece + jnp.where(on_diagonal, scale * diag[row + a : row + a + 1, :], 0.0)
            rounded = exact.astype(BF16)
            high[tile_of(a, a)] = rounded
            rest = jnp.sum(exact - rounded.astype(F32), axis=1, keepdims=True)
            low[a * TILE : (a + 1) * TILE, :] = jnp.broadcast_to(rest, (TILE, TILE))
        else:
            high[tile_of(a, b)] = packed[which, n * TILE : (n + 1) * TILE, :]
            high[tile_of(b, a)] = piece.T.astype(BF16)


def fill_blocks(kind, packed, diag, factor, factor_low, inverse, inverse_low):
    tiles = factor.shape[0] // TILE
    spread(packed, 0, diag, kind * tiles, DECAY, factor, factor_low)
    spread(packed, 1, diag, (2 + kind) * tiles, 1.0, inverse, inverse_low)


def times(high, low, right):
    width = right.shape[1]
    first = right.astype(BF16)
    second = (right - first.astype(F32)).astype(BF16)
    both = jnp.dot(high[...], jnp.concatenate([first, second], axis=1), preferred_element_type=F32)
    return both[:, :width] + both[:, width:] + low * right


def refine(factor, factor_low, inverse, inverse_low, part):
    inner = times(factor, factor_low[:, :1] + DAMPING, part)
    return 2.0 * part - times(inverse, inverse_low[:, :1], inner)


def exact_block(high, low):
    rows = lax.broadcasted_iota(jnp.int32, high.shape, 0)
    columns = lax.broadcasted_iota(jnp.int32, high.shape, 1)
    return high[...].astype(F32) + jnp.where(rows == columns, low[:, :1], 0.0)


def left_columns(mine, other, diag, left, packed, factor, factor_low, inverse, inverse_low):
    facts = Facts()
    core, place = facts.core, facts.place
    unpack(mine, other, core, packed)
    fill_blocks(0, packed, diag, factor, factor_low, inverse, inverse_low)
    start = pl.multiple_of(place * TILE, TILE)
    part = inverse[:, pl.ds(start, TILE)].astype(F32)
    rows = lax.broadcasted_iota(jnp.int32, part.shape, 0) - start
    part = part + jnp.where(
        rows == lax.broadcasted_iota(jnp.int32, part.shape, 1), inverse_low[...], 0.0
    )
    left[...] = refine(factor, factor_low, inverse, inverse_low, part).astype(BF16)


def new_blocks(
    owners, mine, other, far_mine, far_other, diag, right, factor_out, inverse_out,
    packed, factor, factor_low, inverse, inverse_low,
):
    facts = Facts(new_owner=owners)
    core, own_kind = facts.core, facts.own_kind
    first, second = facts.keeps
    blocks = (factor, factor_low, inverse, inverse_low)

    def load_blocks(kind):
        @pl.when(own_kind == kind)
        def _():
            unpack(mine, other, core, packed)

        @pl.when(own_kind != kind)
        def _():
            unpack(far_mine, far_other, core, packed)

        fill_blocks(kind, packed, diag, *blocks)

    load_blocks(1)
    fresh = refine(*blocks, exact_block(inverse, inverse_low))
    right[...] = fresh.astype(BF16)

    @pl.when(second == 1)
    def _():
        factor_out[...] = exact_block(factor, factor_low)
        inverse_out[...] = fresh

    @pl.when(second == 0)
    def _():
        factor_out[...] = jnp.zeros_like(factor_out)
        inverse_out[...] = jnp.zeros_like(inverse_out)

    @pl.when(first == 1)
    def _():
        load_blocks(0)
        factor_out[...] = exact_block(factor, factor_low)
        inverse_out[...] = refine(*blocks, exact_block(inverse, inverse_low))


def precondition(grad, left, right, result, curvature):
    own = Facts().place
    half = sum(
        jnp.dot(grad[p], left[p * TILE : (p + 1) * TILE, :], preferred_element_type=F32)
        for p in range(grad.shape[0])
    )
    product = jnp.dot(half.T.astype(BF16), right[...], preferred_element_type=F32)
    result[...] = product
    curvature[...] = jnp.full(curvature.shape, jnp.sum(product * grad[own].astype(F32).T))


def kernel_call(body, out_shape, in_specs, scratch=(), out_specs=None, aliases=None, flops=0, moved=0):
    if out_specs is None:
        out_specs = (WHOLE,) * len(out_shape) if isinstance(out_shape, tuple) else WHOLE
    return pl.pallas_call(
        body,
        out_shape=out_shape,
        in_specs=in_specs,
        out_specs=out_specs,
        input_output_aliases=aliases or {},
        scratch_shapes=list(scratch),
        compiler_params=PARAMS,
        cost_estimate=pl.CostEstimate(flops=flops, bytes_accessed=moved, transcendentals=0),
        name=body.__name__,
    )


def local(features, out_grads, counts, factor_old, inverse_old, old_owner, new_owner):
    tok_rows, width = out_grads.shape
    feature_count = features.shape[1]
    column = lax.axis_index("mp")
    member = lax.axis_index("dp")
    members = lax.axis_size("dp")
    columns = lax.axis_size("mp")
    chips = members // 2
    ring = chips // 2
    core = member & 1
    core_swap = [(i, i ^ 1) for i in range(members)]
    plane_swap = [(i, (i + chips) % members) for i in range(members)]
    rings = [[y * chips + 2 * z + c for z in range(ring)] for y in range(2) for c in range(2)]
    packed_rows = width * (width + TILE) // 2 // TILE
    share = 2 * packed_rows // members
    lanes = width // TILE
    holders = members // columns
    shape = jax.ShapeDtypeStruct
    megabyte = 2 * width * width * 2

    def along_ring(piece, step):
        return lax.ppermute(piece, "dp", [(i, j) for r in rings for i, j in zip(r, r[step:] + r[:step])])

    def around(pieces):
        return [p if step == 0 else along_ring(p, step) for step, p in enumerate(pieces)]

    def swap_cores(send):
        return lax.ppermute(send, "dp", core_swap)

    def swap_planes(send):
        return lax.ppermute(send, "dp", plane_swap)

    message = shape((chips, share + ROWS, TILE), BF16)
    cov_keep, cov_send, turned = kernel_call(
        covariance_parts,
        (message, message, shape((width, tok_rows), BF16)),
        [SCALARS, ANYWHERE, ANYWHERE],
        [
            pltpu.VMEM((tok_rows, width), BF16),
            pltpu.VMEM((tok_rows, width), BF16),
            pltpu.VMEM((width, tok_rows), BF16),
            pltpu.VMEM((2, packed_rows, TILE), BF16),
            pltpu.SemaphoreType.DMA((2,)),
        ],
        flops=4 * tok_rows * width * width,
        moved=6 * megabyte,
    )(counts, features, out_grads)
    half_shape = (ring,) + message.shape[1:]
    message = shape((chips, 2 * share + 8 * lanes, TILE), BF16)
    keep, send = kernel_call(
        pack_old,
        (message, message),
        [SCALARS, ANYWHERE, ANYWHERE, ANYWHERE],
        [
            pltpu.VMEM((4, width, width), F32),
            pltpu.VMEM((2, 2, packed_rows, TILE), BF16),
            pltpu.VMEM((4 * lanes, TILE), F32),
            pltpu.SemaphoreType.DMA((4,)),
        ],
        moved=6 * megabyte,
    )(old_owner, factor_old[0, 0], inverse_old[0, 0], turned)
    half_message = shape((ring,) + message.shape[1:], BF16)
    near_old, far_old = kernel_call(
        choose_core, (half_message, half_message), [SCALARS, WHOLE, WHOLE], moved=megabyte
    )(old_owner, keep, swap_cores(send))
    arrived_old = swap_planes(far_old)

    near_sum, far_sum = kernel_call(
        add_core, (shape(half_shape, F32), shape(half_shape, BF16)), [WHOLE, WHOLE], moved=megabyte
    )(cov_keep, swap_cores(cov_send))
    arrived_sum = swap_planes(far_sum)

    def gradient(body, tile_at, count, dtype, name, others, passed=()):
        def tile_spec(n):
            return pl.BlockSpec((tok_rows, TILE), lambda i, s: (0, 2 * tile_at(4 * i + n, s) + s[0]))

        message_spec = pl.BlockSpec((4, width, TILE), lambda i, s: (i, 0, 0))
        received_spec = pl.BlockSpec((4, width, TILE), lambda i, s: (tile_at(4 * i, s) // 4, 0, 0))
        other_specs = [received_spec] if len(others) == 1 else [ANYWHERE] * 2
        parity = 1 - core if len(others) == 2 else core
        return pl.pallas_call(
            body,
            out_shape=(shape((count, width, TILE), dtype),) + tuple(shape(p.shape, p.dtype) for p in passed),
            grid_spec=pltpu.PrefetchScalarGridSpec(
                num_scalar_prefetch=1,
                grid=(count // 4,),
                in_specs=[pl.BlockSpec((width, tok_rows), lambda i, s: (0, 0))]
                + [tile_spec(n) for n in range(4)]
                + other_specs
                + [ANYWHERE] * len(passed),
                out_specs=(message_spec,) + (ANYWHERE,) * len(passed),
            ),
            input_output_aliases={6 + len(others) + n: 1 + n for n in range(len(passed))},
            compiler_params=PARAMS,
            cost_estimate=pl.CostEstimate(
                flops=2 * tok_rows * width * TILE * count,
                bytes_accessed=(count // 2) * megabyte,
                transcendentals=0,
            ),
            name=name,
        )(
            jnp.stack([parity, jnp.where(member >= chips, 1, 0)]),
            turned, features, features, features, features, *others, *passed,
        )

    (send,) = gradient(
        gradient_send, lambda q, s: q, chips, BF16, "gradient_send", (far_old, far_sum)
    )
    received = swap_cores(send)
    joined = kernel_call(
        join_planes,
        (shape((near_old.shape[1] + near_sum.shape[1], TILE), BF16),) * ring,
        [SCALARS] + [WHOLE] * 4,
        moved=megabyte,
    )(old_owner, near_old, arrived_old, near_sum, arrived_sum)
    far_grad, *joined = gradient(
        gradient_add,
        lambda q, s: (1 - s[1]) * ring + q,
        ring,
        BF16,
        "gradient_far",
        (received,),
        joined,
    )
    arrived_grad = swap_planes(far_grad)
    (near_grad,) = gradient(
        gradient_add, lambda q, s: s[1] * ring + q, ring, F32, "gradient_near", (received,)
    )

    shares, diag = kernel_call(
        make_shares,
        (shape((2 * share, TILE), BF16), shape((4 * lanes, TILE), F32)),
        [SCALARS] + [WHOLE] * ring,
        [pltpu.VMEM((ring,) + joined[0].shape, BF16)],
        moved=megabyte,
    )(old_owner, *around(joined))

    mine = kernel_call(
        collect, shape((ring, 2 * share, TILE), BF16), [WHOLE] * ring, moved=megabyte
    )(*around([shares] * ring))
    other = swap_cores(mine)
    far_mine = swap_planes(mine)
    far_other = swap_cores(far_mine)
    unpacked = [
        pltpu.VMEM((2, packed_rows, TILE), BF16),
        pltpu.VMEM((width, width), BF16),
        pltpu.VMEM((width, TILE), F32),
        pltpu.VMEM((width, width), BF16),
        pltpu.VMEM((width, TILE), F32),
    ]
    left = kernel_call(
        left_columns,
        shape((width, TILE), BF16),
        [WHOLE] * 3,
        unpacked,
        flops=8 * width * width * TILE,
        moved=2 * megabyte,
    )(mine, other, diag)
    gates = [(i, i // holders) for i in range(members)]
    near = lax.ppermute(
        left, ("dp", "mp"), [(i * columns + g, i * columns + (g ^ 1)) for i, g in gates]
    )
    gate = lax.shift_right_logical(member, holders.bit_length() - 1)
    left = jnp.where(column == gate, left, near)
    left = jnp.where(
        (column ^ gate) <= 1,
        left,
        sum(
            lax.ppermute(
                left,
                ("dp", "mp"),
                [
                    (i * columns + g, i * columns + (g + 2 * step) % columns)
                    for i, at in gates
                    for g in (at, at ^ 1)
                ],
            )
            for step in range(1, columns // 2)
        ),
    )
    square = shape((width, width), F32)
    right, factor_out, inverse_out = kernel_call(
        new_blocks,
        (shape((width, width), BF16), square, square),
        [SCALARS] + [WHOLE] * 5,
        unpacked,
        flops=8 * width * width * width,
        moved=6 * megabyte,
    )(new_owner, mine, other, far_mine, far_other, diag)

    parts = kernel_call(
        add_planes,
        tuple(shape((width, TILE), BF16 if step else F32) for step in range(ring)),
        [WHOLE] * 2,
        moved=4 * megabyte,
    )(near_grad, arrived_grad)
    grad = kernel_call(
        add_ring, shape((width, TILE), BF16), [WHOLE] * ring, moved=megabyte
    )(*around(parts))
    neighbours = [[holders * c + r for r in range(holders)] for c in range(columns)]
    grads = lax.all_gather(grad, "dp", axis=0, axis_index_groups=neighbours)
    result, curvature = kernel_call(
        precondition,
        (shape((TILE, width), F32), shape((8, TILE), F32)),
        [WHOLE] * 3,
        flops=4 * width * width * TILE,
        moved=megabyte,
    )(grads, left, right)

    planes = [[y * chips + i for i in range(chips)] for y in range(2)]
    curvature = lax.all_to_all(
        jnp.broadcast_to(curvature, (chips, 8, TILE)),
        "dp", 0, 0, tiled=True, axis_index_groups=planes,
    )
    curvature = jnp.sum(curvature, axis=0)
    rings = [
        [(y * chips + i) * columns + c for y in range(2) for c in range(columns)] for i in range(chips)
    ]
    curvature = lax.all_to_all(
        jnp.broadcast_to(curvature, (2 * columns, 8, TILE)),
        ("dp", "mp"), 0, 0, tiled=True, axis_index_groups=rings,
    )
    curvature = jnp.sum(curvature, axis=0)[0, 0]
    entries = float(feature_count * width * columns)
    clip_scale = jnp.minimum(1.0, jnp.sqrt(entries / jnp.abs(curvature)))
    return (factor_out[None, None], inverse_out[None, None], clip_scale * result)


def solution(mesh):
    return jax.shard_map(
        local,
        mesh=mesh,
        in_specs=(
            P("dp", None),
            P("dp", "mp"),
            P("dp"),
            P("mp", "dp", None, None, None),
            P("mp", "dp", None, None, None),
            P(),
            P(),
        ),
        out_specs=(P("mp", "dp", None, None), P("mp", "dp", None, None), P("dp", "mp")),
        check_vma=False,
    )
```

```python
import jax
import jax.numpy as jnp
from jax import lax
from jax.experimental import pallas as pl
from jax.experimental.pallas import tpu as pltpu
from jax.sharding import PartitionSpec as P

DECAY = 0.9
DAMPING = 0.01
TILE = 128
ROWS = 16
VMEM_BYTES = 48 * 1024 * 1024
BF16 = jnp.bfloat16
F32 = jnp.float32
PARAMS = pltpu.CompilerParams(vmem_limit_bytes=VMEM_BYTES)
SCALARS = pl.BlockSpec(memory_space=pltpu.SMEM)
WHOLE = pl.BlockSpec(memory_space=pltpu.VMEM)
ANYWHERE = pl.BlockSpec(memory_space=pltpu.HBM)


def upper_pairs(tiles):
    return [(a, b) for a in range(tiles) for b in range(a, tiles)]


def diagonal_mask():
    rows = lax.broadcasted_iota(jnp.int32, (TILE, TILE), 0)
    return rows == lax.broadcasted_iota(jnp.int32, (TILE, TILE), 1)


def tile_of(a, b):
    return (slice(a * TILE, (a + 1) * TILE), slice(b * TILE, (b + 1) * TILE))


class Facts:
    def __init__(self, old_owner=None, new_owner=None):
        member = lax.axis_index("dp")
        self.column = lax.axis_index("mp")
        chips = lax.axis_size("dp") // 2
        self.core = member & 1
        self.plane = jnp.where(member >= chips, 1, 0)
        self.place = member & (lax.axis_size("dp") // lax.axis_size("mp") - 1)
        self.flip = jnp.where(self.column >= lax.axis_size("mp") // 2, 1, 0)
        self.own_kind = self.plane ^ self.flip
        if old_owner is not None:
            owners = [old_owner[self.column, kind] for kind in range(2)]
            self.shared = jnp.where(owners[0] == owners[1], 1, 0)
            self.same_core = [jnp.where((o & 1) == self.core, 1, 0) for o in owners]
            self.same_plane = [
                jnp.where(jnp.where(o >= chips, 1, 0) == self.plane, 1, 0) for o in owners
            ]
            self.ring_at = [lax.shift_right_logical(o & (chips - 1), 1) for o in owners]
        if new_owner is not None:
            self.keeps = [
                jnp.where(new_owner[self.column, kind] == member, 1, 0) for kind in range(2)
            ]


def first_parts(
    owners, counts, features, out_grads, factors, inverses,
    keep, send, turned,
    own, grads, kept, held, packed, diag, arrived,
):
    facts = Facts(owners)
    core, flip, count = facts.core, facts.flip, counts[0]
    rows, width = own.shape
    tiles = width // TILE
    on_diagonal = diagonal_mask()
    start = pl.multiple_of(facts.column * width, width)
    loads = [
        pltpu.make_async_copy(features.at[:, pl.ds(start, width)], own, arrived.at[0]),
        pltpu.make_async_copy(out_grads, grads, arrived.at[1]),
    ] + [
        pltpu.make_async_copy(
            source.at[facts.shared if kind else 0],
            held.at[which * 2 + kind],
            arrived.at[2 + which * 2 + kind],
        )
        for which, source in enumerate((factors, inverses))
        for kind in range(2)
    ]
    for load in loads:
        load.start()
    valid = lax.broadcasted_iota(jnp.int32, (rows, width), 0) < count
    for kind, (block, left) in enumerate(((own, kept), (grads, turned))):
        loads[kind].wait()
        left[...] = jnp.where(valid, block[...].astype(F32), 0.0).T.astype(BF16)
        for a, b in upper_pairs(tiles // 2):
            square = jnp.dot(
                left[2 * a * TILE : 2 * (a + 1) * TILE, :],
                block[:, 2 * b * TILE : 2 * (b + 1) * TILE],
                preferred_element_type=F32,
            ).astype(BF16)
            for i in range(2):
                for j in range(2):
                    if 2 * a + i <= 2 * b + j:
                        at = upper_pairs(tiles).index((2 * a + i, 2 * b + j))
                        packed[kind, 2, at * TILE : (at + 1) * TILE, :] = square[tile_of(i, j)]
    for which in range(2):
        for kind in range(2):
            loads[2 + which * 2 + kind].wait()
            for n, (a, b) in enumerate(upper_pairs(tiles)):
                piece = held[(which * 2 + kind,) + tile_of(a, b)]
                if a == b:
                    row = (which * 2 + kind) * tiles + a
                    diag[row : row + 1, :] = jnp.sum(
                        jnp.where(on_diagonal, piece, 0.0), axis=0, keepdims=True
                    )
                    piece = jnp.where(on_diagonal, 0.0, piece)
                packed[kind, which, n * TILE : (n + 1) * TILE, :] = piece.astype(BF16)
    high = diag[...].astype(BF16)
    low = (diag[...] - high.astype(F32)).astype(BF16)
    words = jnp.concatenate([high, low], axis=0)
    quarter = lax.broadcasted_iota(jnp.int32, (ROWS, TILE), 0) // 4
    digits = lax.shift_right_logical(jnp.full((ROWS, TILE), count), 3 * quarter) & 7
    digits = digits.astype(F32).astype(BF16)
    chips = keep.shape[0]
    share = (keep.shape[1] - words.shape[0] - ROWS) // 3
    sums = 2 * share + words.shape[0]
    for q in range(chips):
        plane, pair = divmod(q, chips // 2)
        kind = flip if plane == 0 else 1 - flip
        for ref, parity in ((keep, core), (send, 1 - core)):
            start = pl.multiple_of((2 * pair + parity) * share, ROWS)
            for which, at in enumerate((0, share, sums)):
                ref[q, at : at + share, :] = packed[kind, which, pl.ds(start, share), :]
            ref[q, 2 * share : sums, :] = words
            ref[q, sums + share :, :] = digits


def merge_words(first_flag, second_flag, one, two):
    lanes = one.shape[0] // 8
    kinds = (lax.broadcasted_iota(jnp.int32, one.shape, 0) // lanes) % 2
    flags = jnp.where(kinds == 0, first_flag, second_flag)
    return jnp.where(flags == 1, one.astype(F32), two.astype(F32))


def choose_core(owners, keep, received, unread, near_old, near_sum, far):
    facts = Facts(owners)
    first, second = facts.same_core
    ring, rows = near_old.shape[0], near_old.shape[1]
    data = rows // 6 * 5
    words = merge_words(first, second, keep[0, data:rows, :], received[0, data:rows, :]).astype(BF16)
    for old, at, kind in (
        (near_old, facts.plane, facts.own_kind),
        (far, 1 - facts.plane, 1 - facts.own_kind),
    ):
        flag = jnp.where(kind == 0, first, second)

        @pl.when(flag == 1)
        def _():
            old[:, :data, :] = keep[pl.ds(at * ring, ring), :data, :]

        @pl.when(flag == 0)
        def _():
            old[:, :data, :] = received[pl.ds(at * ring, ring), :data, :]

        for z in range(ring):
            old[z, data:rows, :] = words
        chips = pl.ds(at * ring, ring)
        total = keep[chips, rows:, :].astype(F32) + received[chips, rows:, :].astype(F32)
        if old is far:
            far[:, rows:, :] = total.astype(BF16)
        else:
            near_sum[...] = total


def join_planes(owners, near_old, near_sum, arrived, unread, other_unread, out):
    facts = Facts(owners)
    first, second = facts.same_plane
    flag = jnp.where(facts.own_kind == 0, first, second)
    ring, rows = near_old.shape[0], near_old.shape[1]
    data = rows // 6 * 5

    @pl.when(flag == 1)
    def _():
        out[:, :data, :] = near_old[:, :data, :]

    @pl.when(flag == 0)
    def _():
        out[:, :data, :] = arrived[:, :data, :]

    words = merge_words(first, second, near_old[0, data:, :], arrived[0, data:rows, :]).astype(BF16)
    for z in range(ring):
        out[z, data:rows, :] = words
    out[:, rows:, :] = (near_sum[...] + arrived[:, rows:, :].astype(F32)).astype(BF16)


def make_shares(owners, arrived, shares, diag):
    facts = Facts(owners)
    own_kind = facts.own_kind
    first, second = facts.ring_at
    ring, rows = shares.shape[0], shares.shape[1]
    share = rows // 2
    words = rows // 5 + rows
    owner = jnp.where(own_kind == 0, first, second)
    both = merge_words(1, 0, arrived[first, rows:words, :], arrived[second, rows:words, :])
    diag[...] = both[: diag.shape[0]] + both[diag.shape[0] :]
    summed = sum(arrived[z, words:, :].astype(F32) for z in range(ring))
    total = sum(summed[share + 4 * d : share + 4 * d + 1, :] * float(8**d) for d in range(4))
    factor = DECAY * arrived[owner, :share, :].astype(F32) + (1.0 - DECAY) * summed[:share] / total
    factor = factor.astype(BF16)
    inverse = arrived[owner, share:rows, :]
    for z in range(ring):
        shares[z, :share, :] = factor
        shares[z, share:, :] = inverse


def gradient_tiles(turned, tiles):
    block = jnp.concatenate([tile[...] for tile in tiles], axis=1)
    return jnp.dot(turned[...], block, preferred_element_type=F32)


def gradient_send(scalars, turned, *refs):
    product = gradient_tiles(turned, refs[:4])
    for n in range(4):
        refs[-1][n] = product[:, n * TILE : (n + 1) * TILE].astype(BF16)


def gradient_add(scalars, turned, *refs):
    received, out = refs[4], refs[-1]
    product = gradient_tiles(turned, refs[:4])
    for n in range(4):
        total = product[:, n * TILE : (n + 1) * TILE] + received[n].astype(F32)
        out[n] = total.astype(out.dtype)


def unpack(mine, other, core, packed):
    share = mine.shape[1] // 2
    for pair in range(mine.shape[0]):
        for ref, parity in ((mine, core), (other, 1 - core)):
            start = pl.multiple_of((2 * pair + parity) * share, ROWS)
            for which in range(2):
                packed[which, pl.ds(start, share), :] = ref[
                    pair, which * share : (which + 1) * share, :
                ]


def spread(packed, which, diag, row, scale, high, low):
    tiles = high.shape[0] // TILE
    on_diagonal = diagonal_mask()
    for n, (a, b) in enumerate(upper_pairs(tiles)):
        piece = packed[which, n * TILE : (n + 1) * TILE, :].astype(F32)
        if a == b:
            exact = piece + jnp.where(on_diagonal, scale * diag[row + a : row + a + 1, :], 0.0)
            rounded = exact.astype(BF16)
            high[tile_of(a, a)] = rounded
            rest = jnp.sum(exact - rounded.astype(F32), axis=1, keepdims=True)
            low[a * TILE : (a + 1) * TILE, :] = jnp.broadcast_to(rest, (TILE, TILE))
        else:
            high[tile_of(a, b)] = packed[which, n * TILE : (n + 1) * TILE, :]
            high[tile_of(b, a)] = piece.T.astype(BF16)


def fill_blocks(kind, packed, diag, factor, factor_low, inverse, inverse_low):
    tiles = factor.shape[0] // TILE
    spread(packed, 0, diag, kind * tiles, DECAY, factor, factor_low)
    spread(packed, 1, diag, (2 + kind) * tiles, 1.0, inverse, inverse_low)


def times(high, low, right):
    width = right.shape[1]
    first = right.astype(BF16)
    second = (right - first.astype(F32)).astype(BF16)
    both = jnp.dot(high[...], jnp.concatenate([first, second], axis=1), preferred_element_type=F32)
    return both[:, :width] + both[:, width:] + low * right


def refine(factor, factor_low, inverse, inverse_low, part):
    inner = times(factor, factor_low[:, :1] + DAMPING, part)
    return 2.0 * part - times(inverse, inverse_low[:, :1], inner)


def exact_block(high, low):
    rows = lax.broadcasted_iota(jnp.int32, high.shape, 0)
    columns = lax.broadcasted_iota(jnp.int32, high.shape, 1)
    return high[...].astype(F32) + jnp.where(rows == columns, low[:, :1], 0.0)


def left_columns(mine, other, diag, left, packed, factor, factor_low, inverse, inverse_low):
    facts = Facts()
    core, place = facts.core, facts.place
    unpack(mine, other, core, packed)
    fill_blocks(0, packed, diag, factor, factor_low, inverse, inverse_low)
    start = pl.multiple_of(place * TILE, TILE)
    part = inverse[:, pl.ds(start, TILE)].astype(F32)
    rows = lax.broadcasted_iota(jnp.int32, part.shape, 0) - start
    part = part + jnp.where(
        rows == lax.broadcasted_iota(jnp.int32, part.shape, 1), inverse_low[...], 0.0
    )
    left[...] = refine(factor, factor_low, inverse, inverse_low, part).astype(BF16)


def new_blocks(
    owners, mine, other, far_mine, far_other, diag, right, factor_out, inverse_out,
    packed, factor, factor_low, inverse, inverse_low,
):
    facts = Facts(new_owner=owners)
    core, own_kind = facts.core, facts.own_kind
    first, second = facts.keeps
    blocks = (factor, factor_low, inverse, inverse_low)

    def load_blocks(kind):
        @pl.when(own_kind == kind)
        def _():
            unpack(mine, other, core, packed)

        @pl.when(own_kind != kind)
        def _():
            unpack(far_mine, far_other, core, packed)

        fill_blocks(kind, packed, diag, *blocks)

    load_blocks(1)
    fresh = refine(*blocks, exact_block(inverse, inverse_low))
    right[...] = fresh.astype(BF16)

    @pl.when(second == 1)
    def _():
        factor_out[...] = exact_block(factor, factor_low)
        inverse_out[...] = fresh

    @pl.when(second == 0)
    def _():
        factor_out[...] = jnp.zeros_like(factor_out)
        inverse_out[...] = jnp.zeros_like(inverse_out)

    @pl.when(first == 1)
    def _():
        load_blocks(0)
        factor_out[...] = exact_block(factor, factor_low)
        inverse_out[...] = refine(*blocks, exact_block(inverse, inverse_low))


def precondition(grad, left, right, result, curvature):
    own = Facts().place
    half = sum(
        jnp.dot(grad[p], left[p * TILE : (p + 1) * TILE, :], preferred_element_type=F32)
        for p in range(grad.shape[0])
    )
    product = jnp.dot(half.T.astype(BF16), right[...], preferred_element_type=F32)
    result[...] = product
    curvature[...] = jnp.full(curvature.shape, jnp.sum(product * grad[own].astype(F32).T))


def kernel_call(body, out_shape, in_specs, scratch=(), out_specs=None, aliases=None, flops=0, moved=0):
    if out_specs is None:
        out_specs = (WHOLE,) * len(out_shape) if isinstance(out_shape, tuple) else WHOLE
    return pl.pallas_call(
        body,
        out_shape=out_shape,
        in_specs=in_specs,
        out_specs=out_specs,
        input_output_aliases=aliases or {},
        scratch_shapes=list(scratch),
        compiler_params=PARAMS,
        cost_estimate=pl.CostEstimate(flops=flops, bytes_accessed=moved, transcendentals=0),
        name=body.__name__,
    )


def local(features, out_grads, counts, factor_old, inverse_old, old_owner, new_owner):
    tok_rows, width = out_grads.shape
    feature_count = features.shape[1]
    column = lax.axis_index("mp")
    member = lax.axis_index("dp")
    members = lax.axis_size("dp")
    columns = lax.axis_size("mp")
    chips = members // 2
    ring = chips // 2
    core = member & 1
    core_swap = [(i, i ^ 1) for i in range(members)]
    plane_swap = [(i, (i + chips) % members) for i in range(members)]
    rings = [[y * chips + 2 * z + c for z in range(ring)] for y in range(2) for c in range(2)]
    packed_rows = width * (width + TILE) // 2 // TILE
    share = 2 * packed_rows // members
    lanes = width // TILE
    holders = members // columns
    shape = jax.ShapeDtypeStruct
    megabyte = 2 * width * width * 2

    def across_ring(parts):
        return lax.all_to_all(parts, "dp", 0, 0, tiled=True, axis_index_groups=rings)

    def swap_cores(send):
        return lax.ppermute(send, "dp", core_swap)

    def swap_planes(send):
        return lax.ppermute(send, "dp", plane_swap)

    message = shape((chips, 3 * share + 8 * lanes + ROWS, TILE), BF16)
    keep, send, turned = kernel_call(
        first_parts,
        (message, message, shape((width, tok_rows), BF16)),
        [SCALARS, SCALARS] + [ANYWHERE] * 4,
        [
            pltpu.VMEM((tok_rows, width), BF16),
            pltpu.VMEM((tok_rows, width), BF16),
            pltpu.VMEM((width, tok_rows), BF16),
            pltpu.VMEM((4, width, width), F32),
            pltpu.VMEM((2, 3, packed_rows, TILE), BF16),
            pltpu.VMEM((4 * lanes, TILE), F32),
            pltpu.SemaphoreType.DMA((6,)),
        ],
        flops=4 * tok_rows * width * width,
        moved=10 * megabyte,
    )(old_owner, counts, features, out_grads, factor_old[0, 0], inverse_old[0, 0])
    old_rows = 2 * share + 8 * lanes
    far_shape = shape((ring,) + message.shape[1:], BF16)
    def gradient(body, parity, which, dtype, name, other):
        def chip_at(i, s):
            return s[1] * ring + 4 * i

        def tile_spec(n):
            return pl.BlockSpec((tok_rows, TILE), lambda i, s: (0, 2 * (chip_at(i, s) + n) + s[0]))

        four_chips = pl.BlockSpec((4, width, TILE), lambda i, s: (i, 0, 0))
        return pl.pallas_call(
            body,
            out_shape=shape((ring, width, TILE), dtype),
            grid_spec=pltpu.PrefetchScalarGridSpec(
                num_scalar_prefetch=1,
                grid=(ring // 4,),
                in_specs=[pl.BlockSpec((width, tok_rows), lambda i, s: (0, 0))]
                + [tile_spec(n) for n in range(4)]
                + [four_chips if body is gradient_add else ANYWHERE],
                out_specs=four_chips,
            ),
            compiler_params=PARAMS,
            cost_estimate=pl.CostEstimate(
                flops=2 * ring * tok_rows * width * TILE,
                bytes_accessed=ring * megabyte // 2,
                transcendentals=0,
            ),
            name=name,
        )(jnp.stack([parity, which]), turned, features, features, features, features, other)

    plane = jnp.where(member >= chips, 1, 0)
    send_far = gradient(gradient_send, 1 - core, 1 - plane, BF16, "send_far", counts)
    received_far = swap_cores(send_far)
    near_old, near_sum, far = kernel_call(
        choose_core,
        (shape((ring, old_rows, TILE), BF16), shape((ring, share + ROWS, TILE), F32), far_shape),
        [SCALARS, WHOLE, WHOLE, ANYWHERE],
        moved=2 * megabyte,
    )(old_owner, keep, swap_cores(send), send_far)
    arrived = swap_planes(far)

    send_near = gradient(gradient_send, 1 - core, plane, BF16, "send_near", far)
    far_grad = gradient(gradient_add, core, 1 - plane, BF16, "gradient_far", received_far)
    arrived_grad = swap_planes(far_grad)
    near_grad = gradient(
        gradient_add, core, plane, F32, "gradient_near", swap_cores(send_near)
    )
    joined = kernel_call(
        join_planes,
        far_shape,
        [SCALARS] + [WHOLE] * 3 + [ANYWHERE] * 2,
        moved=megabyte,
    )(old_owner, near_old, near_sum, arrived, far_grad, send_near)
    shares, diag = kernel_call(
        make_shares,
        (shape((ring, 2 * share, TILE), BF16), shape((4 * lanes, TILE), F32)),
        [SCALARS, WHOLE],
        moved=megabyte,
    )(old_owner, across_ring(joined))

    mine = across_ring(shares)
    other = swap_cores(mine)
    far_mine = swap_planes(mine)
    far_other = swap_cores(far_mine)
    unpacked = [
        pltpu.VMEM((2, packed_rows, TILE), BF16),
        pltpu.VMEM((width, width), BF16),
        pltpu.VMEM((width, TILE), F32),
        pltpu.VMEM((width, width), BF16),
        pltpu.VMEM((width, TILE), F32),
    ]
    left = kernel_call(
        left_columns,
        shape((width, TILE), BF16),
        [WHOLE] * 3,
        unpacked,
        flops=8 * width * width * TILE,
        moved=2 * megabyte,
    )(mine, other, diag)
    gates = [(i, i // holders) for i in range(members)]
    near = lax.ppermute(
        left, ("dp", "mp"), [(i * columns + g, i * columns + (g ^ 1)) for i, g in gates]
    )
    gate = lax.shift_right_logical(member, holders.bit_length() - 1)
    left = jnp.where(column == gate, left, near)
    left = jnp.where(
        (column ^ gate) <= 1,
        left,
        sum(
            lax.ppermute(
                left,
                ("dp", "mp"),
                [
                    (i * columns + g, i * columns + (g + 2 * step) % columns)
                    for i, at in gates
                    for g in (at, at ^ 1)
                ],
            )
            for step in range(1, columns // 2)
        ),
    )
    square = shape((width, width), F32)
    right, factor_out, inverse_out = kernel_call(
        new_blocks,
        (shape((width, width), BF16), square, square),
        [SCALARS] + [WHOLE] * 5,
        unpacked,
        flops=8 * width * width * width,
        moved=6 * megabyte,
    )(new_owner, mine, other, far_mine, far_other, diag)

    grad = across_ring((near_grad + arrived_grad.astype(F32)).astype(BF16))
    grad = jnp.sum(grad.astype(F32), axis=0).astype(BF16)
    neighbours = [[holders * c + r for r in range(holders)] for c in range(columns)]
    grads = lax.all_gather(grad, "dp", axis=0, axis_index_groups=neighbours)
    result, curvature = kernel_call(
        precondition,
        (shape((TILE, width), F32), shape((8, TILE), F32)),
        [WHOLE] * 3,
        flops=4 * width * width * TILE,
        moved=megabyte,
    )(grads, left, right)

    planes = [[y * chips + i for i in range(chips)] for y in range(2)]
    curvature = lax.all_to_all(
        jnp.broadcast_to(curvature, (chips, 8, TILE)),
        "dp", 0, 0, tiled=True, axis_index_groups=planes,
    )
    curvature = jnp.sum(curvature, axis=0)
    rings = [
        [(y * chips + i) * columns + c for y in range(2) for c in range(columns)] for i in range(chips)
    ]
    curvature = lax.all_to_all(
        jnp.broadcast_to(curvature, (2 * columns, 8, TILE)),
        ("dp", "mp"), 0, 0, tiled=True, axis_index_groups=rings,
    )
    curvature = jnp.sum(curvature, axis=0)[0, 0]
    entries = float(feature_count * width * columns)
    clip_scale = jnp.minimum(1.0, jnp.sqrt(entries / jnp.abs(curvature)))
    return (factor_out[None, None], inverse_out[None, None], clip_scale * result)


def solution(mesh):
    return jax.shard_map(
        local,
        mesh=mesh,
        in_specs=(
            P("dp", None),
            P("dp", "mp"),
            P("dp"),
            P("mp", "dp", None, None, None),
            P("mp", "dp", None, None, None),
            P(),
            P(),
        ),
        out_specs=(P("mp", "dp", None, None), P("mp", "dp", None, None), P("dp", "mp")),
        check_vma=False,
    )
```

```python
import jax
import jax.numpy as jnp
from jax import lax
from jax.experimental import pallas as pl
from jax.experimental.pallas import tpu as pltpu
from jax.sharding import PartitionSpec as P

DECAY = 0.9
DAMPING = 0.01
TILE = 128
ROWS = 16
VMEM_BYTES = 48 * 1024 * 1024
BF16 = jnp.bfloat16
F32 = jnp.float32
PARAMS = pltpu.CompilerParams(vmem_limit_bytes=VMEM_BYTES)
SCALARS = pl.BlockSpec(memory_space=pltpu.SMEM)
WHOLE = pl.BlockSpec(memory_space=pltpu.VMEM)
ANYWHERE = pl.BlockSpec(memory_space=pltpu.HBM)


def upper_pairs(tiles):
    return [(a, b) for a in range(tiles) for b in range(a, tiles)]


def diagonal_mask():
    rows = lax.broadcasted_iota(jnp.int32, (TILE, TILE), 0)
    return rows == lax.broadcasted_iota(jnp.int32, (TILE, TILE), 1)


def tile_of(a, b):
    return (slice(a * TILE, (a + 1) * TILE), slice(b * TILE, (b + 1) * TILE))


class Facts:
    def __init__(self, old_owner=None, new_owner=None):
        member = lax.axis_index("dp")
        self.column = lax.axis_index("mp")
        chips = lax.axis_size("dp") // 2
        self.core = member & 1
        self.plane = jnp.where(member >= chips, 1, 0)
        self.ring = lax.shift_right_logical(member & (chips - 1), 1)
        self.place = member & (lax.axis_size("dp") // lax.axis_size("mp") - 1)
        self.flip = jnp.where(self.column >= lax.axis_size("mp") // 2, 1, 0)
        self.own_kind = self.plane ^ self.flip
        if old_owner is not None:
            owners = [old_owner[self.column, kind] for kind in range(2)]
            self.shared = jnp.where(owners[0] == owners[1], 1, 0)
            self.same_core = [jnp.where((o & 1) == self.core, 1, 0) for o in owners]
            self.same_plane = [
                jnp.where(jnp.where(o >= chips, 1, 0) == self.plane, 1, 0) for o in owners
            ]
            self.ring_at = [lax.shift_right_logical(o & (chips - 1), 1) for o in owners]
        if new_owner is not None:
            self.keeps = [
                jnp.where(new_owner[self.column, kind] == member, 1, 0) for kind in range(2)
            ]


def first_parts(
    owners, counts, features, out_grads, factors, inverses,
    keep, send, turned,
    own, grads, kept, held, packed, diag, arrived,
):
    facts = Facts(owners)
    core, flip, count = facts.core, facts.flip, counts[0]
    rows, width = own.shape
    tiles = width // TILE
    on_diagonal = diagonal_mask()
    start = pl.multiple_of(facts.column * width, width)
    loads = [
        pltpu.make_async_copy(features.at[:, pl.ds(start, width)], own, arrived.at[0]),
        pltpu.make_async_copy(out_grads, grads, arrived.at[1]),
    ] + [
        pltpu.make_async_copy(
            source.at[facts.shared if kind else 0],
            held.at[which * 2 + kind],
            arrived.at[2 + which * 2 + kind],
        )
        for which, source in enumerate((factors, inverses))
        for kind in range(2)
    ]
    for load in loads:
        load.start()
    valid = lax.broadcasted_iota(jnp.int32, (rows, width), 0) < count
    for kind, (block, left) in enumerate(((own, kept), (grads, turned))):
        loads[kind].wait()
        left[...] = jnp.where(valid, block[...].astype(F32), 0.0).T.astype(BF16)
        for a, b in upper_pairs(tiles // 2):
            square = jnp.dot(
                left[2 * a * TILE : 2 * (a + 1) * TILE, :],
                block[:, 2 * b * TILE : 2 * (b + 1) * TILE],
                preferred_element_type=F32,
            ).astype(BF16)
            for i in range(2):
                for j in range(2):
                    if 2 * a + i <= 2 * b + j:
                        at = upper_pairs(tiles).index((2 * a + i, 2 * b + j))
                        packed[kind, 2, at * TILE : (at + 1) * TILE, :] = square[tile_of(i, j)]
    for which in range(2):
        for kind in range(2):
            loads[2 + which * 2 + kind].wait()
            for n, (a, b) in enumerate(upper_pairs(tiles)):
                piece = held[(which * 2 + kind,) + tile_of(a, b)]
                if a == b:
                    row = (which * 2 + kind) * tiles + a
                    diag[row : row + 1, :] = jnp.sum(
                        jnp.where(on_diagonal, piece, 0.0), axis=0, keepdims=True
                    )
                    piece = jnp.where(on_diagonal, 0.0, piece)
                packed[kind, which, n * TILE : (n + 1) * TILE, :] = piece.astype(BF16)
    high = diag[...].astype(BF16)
    low = (diag[...] - high.astype(F32)).astype(BF16)
    words = jnp.concatenate([high, low], axis=0)
    quarter = lax.broadcasted_iota(jnp.int32, (ROWS, TILE), 0) // 4
    digits = lax.shift_right_logical(jnp.full((ROWS, TILE), count), 3 * quarter) & 7
    digits = digits.astype(F32).astype(BF16)
    chips = keep.shape[0]
    share = (keep.shape[1] - words.shape[0] - ROWS) // 3
    sums = 2 * share + words.shape[0]
    for q in range(chips):
        plane, pair = divmod(q, chips // 2)
        kind = flip if plane == 0 else 1 - flip
        for ref, parity in ((keep, core), (send, 1 - core)):
            start = pl.multiple_of((2 * pair + parity) * share, ROWS)
            for which, at in enumerate((0, share, sums)):
                ref[q, at : at + share, :] = packed[kind, which, pl.ds(start, share), :]
            ref[q, 2 * share : sums, :] = words
            ref[q, sums + share :, :] = digits


def merge_words(first_flag, second_flag, one, two):
    lanes = one.shape[0] // 8
    kinds = (lax.broadcasted_iota(jnp.int32, one.shape, 0) // lanes) % 2
    flags = jnp.where(kinds == 0, first_flag, second_flag)
    return jnp.where(flags == 1, one.astype(F32), two.astype(F32))


def choose_core(owners, keep, received, unread, near_old, near_sum, far):
    facts = Facts(owners)
    first, second = facts.same_core
    ring, rows = near_old.shape[0], near_old.shape[1]
    data = rows // 6 * 5
    words = merge_words(first, second, keep[0, data:rows, :], received[0, data:rows, :]).astype(BF16)
    for old, at, kind in (
        (near_old, facts.plane, facts.own_kind),
        (far, 1 - facts.plane, 1 - facts.own_kind),
    ):
        flag = jnp.where(kind == 0, first, second)

        @pl.when(flag == 1)
        def _():
            old[:, :data, :] = keep[pl.ds(at * ring, ring), :data, :]

        @pl.when(flag == 0)
        def _():
            old[:, :data, :] = received[pl.ds(at * ring, ring), :data, :]

        for z in range(ring):
            old[z, data:rows, :] = words
        chips = pl.ds(at * ring, ring)
        total = keep[chips, rows:, :].astype(F32) + received[chips, rows:, :].astype(F32)
        if old is far:
            far[:, rows:, :] = total.astype(BF16)
        else:
            near_sum[...] = total


def join_planes(owners, near_old, near_sum, arrived, unread, other_unread, out):
    facts = Facts(owners)
    first, second = facts.same_plane
    flag = jnp.where(facts.own_kind == 0, first, second)
    ring, rows = near_old.shape[0], near_old.shape[1]
    data = rows // 6 * 5

    @pl.when(flag == 1)
    def _():
        out[:, :data, :] = near_old[:, :data, :]

    @pl.when(flag == 0)
    def _():
        out[:, :data, :] = arrived[:, :data, :]

    words = merge_words(first, second, near_old[0, data:, :], arrived[0, data:rows, :]).astype(BF16)
    for z in range(ring):
        out[z, data:rows, :] = words
    out[:, rows:, :] = (near_sum[...] + arrived[:, rows:, :].astype(F32)).astype(BF16)


def make_shares(owners, arrived, shares, diag):
    facts = Facts(owners)
    own_kind = facts.own_kind
    first, second = facts.ring_at
    ring, rows = shares.shape[0], shares.shape[1]
    share = rows // 2
    words = rows // 5 + rows
    owner = jnp.where(own_kind == 0, first, second)
    both = merge_words(1, 0, arrived[first, rows:words, :], arrived[second, rows:words, :])
    diag[...] = both[: diag.shape[0]] + both[diag.shape[0] :]
    summed = sum(arrived[z, words:, :].astype(F32) for z in range(ring))
    total = sum(summed[share + 4 * d : share + 4 * d + 1, :] * float(8**d) for d in range(4))
    factor = DECAY * arrived[owner, :share, :].astype(F32) + (1.0 - DECAY) * summed[:share] / total
    factor = factor.astype(BF16)
    inverse = arrived[owner, share:rows, :]
    for z in range(ring):
        shares[z, :share, :] = factor
        shares[z, share:, :] = inverse


def gradient_tiles(turned, tiles):
    block = jnp.concatenate([tile[...] for tile in tiles], axis=1)
    return jnp.dot(turned[...], block, preferred_element_type=F32)


def gradient_send(scalars, turned, *refs):
    product = gradient_tiles(turned, refs[:4])
    for n in range(4):
        refs[-1][n] = product[:, n * TILE : (n + 1) * TILE].astype(BF16)


def gradient_add(scalars, turned, *refs):
    received, out = refs[4], refs[-1]
    product = gradient_tiles(turned, refs[:4])
    for n in range(4):
        total = product[:, n * TILE : (n + 1) * TILE] + received[n].astype(F32)
        out[n] = total.astype(out.dtype)


def add_planes(near, arrived, keep, send):
    parity = Facts().ring & 1
    for pair in range(keep.shape[0]):
        for out, which in ((keep, parity), (send, 1 - parity)):
            at = 2 * pair + which
            out[pair] = (near[at] + arrived[at].astype(F32)).astype(out.dtype)


def add_pair(keep, received, out):
    out[...] = (keep[...] + received[...].astype(F32)).astype(BF16)


def unpack(mine, other, core, packed):
    share = mine.shape[1] // 2
    for pair in range(mine.shape[0]):
        for ref, parity in ((mine, core), (other, 1 - core)):
            start = pl.multiple_of((2 * pair + parity) * share, ROWS)
            for which in range(2):
                packed[which, pl.ds(start, share), :] = ref[
                    pair, which * share : (which + 1) * share, :
                ]


def spread(packed, which, diag, row, scale, high, low):
    tiles = high.shape[0] // TILE
    on_diagonal = diagonal_mask()
    for n, (a, b) in enumerate(upper_pairs(tiles)):
        piece = packed[which, n * TILE : (n + 1) * TILE, :].astype(F32)
        if a == b:
            exact = piece + jnp.where(on_diagonal, scale * diag[row + a : row + a + 1, :], 0.0)
            rounded = exact.astype(BF16)
            high[tile_of(a, a)] = rounded
            rest = jnp.sum(exact - rounded.astype(F32), axis=1, keepdims=True)
            low[a * TILE : (a + 1) * TILE, :] = jnp.broadcast_to(rest, (TILE, TILE))
        else:
            high[tile_of(a, b)] = packed[which, n * TILE : (n + 1) * TILE, :]
            high[tile_of(b, a)] = piece.T.astype(BF16)


def fill_blocks(kind, packed, diag, factor, factor_low, inverse, inverse_low):
    tiles = factor.shape[0] // TILE
    spread(packed, 0, diag, kind * tiles, DECAY, factor, factor_low)
    spread(packed, 1, diag, (2 + kind) * tiles, 1.0, inverse, inverse_low)


def times(high, low, right):
    width = right.shape[1]
    first = right.astype(BF16)
    second = (right - first.astype(F32)).astype(BF16)
    both = jnp.dot(high[...], jnp.concatenate([first, second], axis=1), preferred_element_type=F32)
    return both[:, :width] + both[:, width:] + low * right


def refine(factor, factor_low, inverse, inverse_low, part):
    inner = times(factor, factor_low[:, :1] + DAMPING, part)
    return 2.0 * part - times(inverse, inverse_low[:, :1], inner)


def exact_block(high, low):
    rows = lax.broadcasted_iota(jnp.int32, high.shape, 0)
    columns = lax.broadcasted_iota(jnp.int32, high.shape, 1)
    return high[...].astype(F32) + jnp.where(rows == columns, low[:, :1], 0.0)


def left_columns(mine, other, diag, left, packed, factor, factor_low, inverse, inverse_low):
    facts = Facts()
    core, place = facts.core, facts.place
    unpack(mine, other, core, packed)
    fill_blocks(0, packed, diag, factor, factor_low, inverse, inverse_low)
    start = pl.multiple_of(place * TILE, TILE)
    part = inverse[:, pl.ds(start, TILE)].astype(F32)
    rows = lax.broadcasted_iota(jnp.int32, part.shape, 0) - start
    part = part + jnp.where(
        rows == lax.broadcasted_iota(jnp.int32, part.shape, 1), inverse_low[...], 0.0
    )
    left[...] = refine(factor, factor_low, inverse, inverse_low, part).astype(BF16)


def new_blocks(
    owners, mine, other, far_mine, far_other, diag, right, factor_out, inverse_out,
    packed, factor, factor_low, inverse, inverse_low,
):
    facts = Facts(new_owner=owners)
    core, own_kind = facts.core, facts.own_kind
    first, second = facts.keeps
    blocks = (factor, factor_low, inverse, inverse_low)

    def load_blocks(kind):
        @pl.when(own_kind == kind)
        def _():
            unpack(mine, other, core, packed)

        @pl.when(own_kind != kind)
        def _():
            unpack(far_mine, far_other, core, packed)

        fill_blocks(kind, packed, diag, *blocks)

    load_blocks(1)
    fresh = refine(*blocks, exact_block(inverse, inverse_low))
    right[...] = fresh.astype(BF16)

    @pl.when(second == 1)
    def _():
        factor_out[...] = exact_block(factor, factor_low)
        inverse_out[...] = fresh

    @pl.when(second == 0)
    def _():
        factor_out[...] = jnp.zeros_like(factor_out)
        inverse_out[...] = jnp.zeros_like(inverse_out)

    @pl.when(first == 1)
    def _():
        load_blocks(0)
        factor_out[...] = exact_block(factor, factor_low)
        inverse_out[...] = refine(*blocks, exact_block(inverse, inverse_low))


def precondition(grad, left, right, result, curvature):
    own = Facts().place
    half = sum(
        jnp.dot(grad[p], left[p * TILE : (p + 1) * TILE, :], preferred_element_type=F32)
        for p in range(grad.shape[0])
    )
    product = jnp.dot(half.T.astype(BF16), right[...], preferred_element_type=F32)
    result[...] = product
    curvature[...] = jnp.full(curvature.shape, jnp.sum(product * grad[own].astype(F32).T))


def kernel_call(body, out_shape, in_specs, scratch=(), out_specs=None, aliases=None, flops=0, moved=0):
    if out_specs is None:
        out_specs = (WHOLE,) * len(out_shape) if isinstance(out_shape, tuple) else WHOLE
    return pl.pallas_call(
        body,
        out_shape=out_shape,
        in_specs=in_specs,
        out_specs=out_specs,
        input_output_aliases=aliases or {},
        scratch_shapes=list(scratch),
        compiler_params=PARAMS,
        cost_estimate=pl.CostEstimate(flops=flops, bytes_accessed=moved, transcendentals=0),
        name=body.__name__,
    )


def local(features, out_grads, counts, factor_old, inverse_old, old_owner, new_owner):
    tok_rows, width = out_grads.shape
    feature_count = features.shape[1]
    column = lax.axis_index("mp")
    member = lax.axis_index("dp")
    members = lax.axis_size("dp")
    columns = lax.axis_size("mp")
    chips = members // 2
    ring = chips // 2
    core = member & 1
    core_swap = [(i, i ^ 1) for i in range(members)]
    plane_swap = [(i, (i + chips) % members) for i in range(members)]
    rings = [[y * chips + 2 * z + c for z in range(ring)] for y in range(2) for c in range(2)]
    packed_rows = width * (width + TILE) // 2 // TILE
    share = 2 * packed_rows // members
    lanes = width // TILE
    holders = members // columns
    shape = jax.ShapeDtypeStruct
    megabyte = 2 * width * width * 2

    def across_ring(parts):
        return lax.all_to_all(parts, "dp", 0, 0, tiled=True, axis_index_groups=rings)

    def swap_cores(send):
        return lax.ppermute(send, "dp", core_swap)

    def swap_planes(send):
        return lax.ppermute(send, "dp", plane_swap)

    message = shape((chips, 3 * share + 8 * lanes + ROWS, TILE), BF16)
    keep, send, turned = kernel_call(
        first_parts,
        (message, message, shape((width, tok_rows), BF16)),
        [SCALARS, SCALARS] + [ANYWHERE] * 4,
        [
            pltpu.VMEM((tok_rows, width), BF16),
            pltpu.VMEM((tok_rows, width), BF16),
            pltpu.VMEM((width, tok_rows), BF16),
            pltpu.VMEM((4, width, width), F32),
            pltpu.VMEM((2, 3, packed_rows, TILE), BF16),
            pltpu.VMEM((4 * lanes, TILE), F32),
            pltpu.SemaphoreType.DMA((6,)),
        ],
        flops=4 * tok_rows * width * width,
        moved=10 * megabyte,
    )(old_owner, counts, features, out_grads, factor_old[0, 0], inverse_old[0, 0])
    old_rows = 2 * share + 8 * lanes
    far_shape = shape((ring,) + message.shape[1:], BF16)
    def gradient(body, parity, which, dtype, name, other):
        def chip_at(i, s):
            return s[1] * ring + 4 * i

        def tile_spec(n):
            return pl.BlockSpec((tok_rows, TILE), lambda i, s: (0, 2 * (chip_at(i, s) + n) + s[0]))

        four_chips = pl.BlockSpec((4, width, TILE), lambda i, s: (i, 0, 0))
        return pl.pallas_call(
            body,
            out_shape=shape((ring, width, TILE), dtype),
            grid_spec=pltpu.PrefetchScalarGridSpec(
                num_scalar_prefetch=1,
                grid=(ring // 4,),
                in_specs=[pl.BlockSpec((width, tok_rows), lambda i, s: (0, 0))]
                + [tile_spec(n) for n in range(4)]
                + [four_chips if body is gradient_add else ANYWHERE],
                out_specs=four_chips,
            ),
            compiler_params=PARAMS,
            cost_estimate=pl.CostEstimate(
                flops=2 * ring * tok_rows * width * TILE,
                bytes_accessed=ring * megabyte // 2,
                transcendentals=0,
            ),
            name=name,
        )(jnp.stack([parity, which]), turned, features, features, features, features, other)

    def plane_shape(count, dtype):
        return shape((count, width, TILE), dtype)

    plane = jnp.where(member >= chips, 1, 0)
    send_far = gradient(gradient_send, 1 - core, 1 - plane, BF16, "send_far", counts)
    received_far = swap_cores(send_far)
    near_old, near_sum, far = kernel_call(
        choose_core,
        (shape((ring, old_rows, TILE), BF16), shape((ring, share + ROWS, TILE), F32), far_shape),
        [SCALARS, WHOLE, WHOLE, ANYWHERE],
        moved=2 * megabyte,
    )(old_owner, keep, swap_cores(send), send_far)
    arrived = swap_planes(far)

    send_near = gradient(gradient_send, 1 - core, plane, BF16, "send_near", far)
    far_grad = gradient(gradient_add, core, 1 - plane, BF16, "gradient_far", received_far)
    arrived_grad = swap_planes(far_grad)
    near_grad = gradient(
        gradient_add, core, plane, F32, "gradient_near", swap_cores(send_near)
    )
    joined = kernel_call(
        join_planes,
        far_shape,
        [SCALARS] + [WHOLE] * 3 + [ANYWHERE] * 2,
        moved=megabyte,
    )(old_owner, near_old, near_sum, arrived, far_grad, send_near)
    shares, diag = kernel_call(
        make_shares,
        (shape((ring, 2 * share, TILE), BF16), shape((4 * lanes, TILE), F32)),
        [SCALARS, WHOLE],
        moved=megabyte,
    )(old_owner, across_ring(joined))

    mine = across_ring(shares)
    other = swap_cores(mine)
    far_mine = swap_planes(mine)
    far_other = swap_cores(far_mine)
    unpacked = [
        pltpu.VMEM((2, packed_rows, TILE), BF16),
        pltpu.VMEM((width, width), BF16),
        pltpu.VMEM((width, TILE), F32),
        pltpu.VMEM((width, width), BF16),
        pltpu.VMEM((width, TILE), F32),
    ]
    left = kernel_call(
        left_columns,
        shape((width, TILE), BF16),
        [WHOLE] * 3,
        unpacked,
        flops=8 * width * width * TILE,
        moved=2 * megabyte,
    )(mine, other, diag)
    gates = [(i, i // holders) for i in range(members)]
    near = lax.ppermute(
        left, ("dp", "mp"), [(i * columns + g, i * columns + (g ^ 1)) for i, g in gates]
    )
    gate = lax.shift_right_logical(member, holders.bit_length() - 1)
    left = jnp.where(column == gate, left, near)
    left = jnp.where(
        (column ^ gate) <= 1,
        left,
        sum(
            lax.ppermute(
                left,
                ("dp", "mp"),
                [
                    (i * columns + g, i * columns + (g + 2 * step) % columns)
                    for i, at in gates
                    for g in (at, at ^ 1)
                ],
            )
            for step in range(1, columns // 2)
        ),
    )
    square = shape((width, width), F32)
    right, factor_out, inverse_out = kernel_call(
        new_blocks,
        (shape((width, width), BF16), square, square),
        [SCALARS] + [WHOLE] * 5,
        unpacked,
        flops=8 * width * width * width,
        moved=6 * megabyte,
    )(new_owner, mine, other, far_mine, far_other, diag)

    pairs = ring // 2
    keep, send = kernel_call(
        add_planes,
        (plane_shape(pairs, F32), plane_shape(pairs, BF16)),
        [WHOLE] * 2,
        moved=4 * megabyte,
    )(near_grad, arrived_grad)
    received = lax.ppermute(send, "dp", [(i, i ^ 2) for i in range(members)])
    grad = kernel_call(add_pair, plane_shape(pairs, BF16), [WHOLE] * 2, moved=2 * megabyte)(
        keep, received
    )
    halves = [[r[z] for z in range(parity, ring, 2)] for r in rings for parity in range(2)]
    grad = lax.all_to_all(grad, "dp", 0, 0, tiled=True, axis_index_groups=halves)
    grad = jnp.sum(grad.astype(F32), axis=0).astype(BF16)
    neighbours = [[holders * c + r for r in range(holders)] for c in range(columns)]
    grads = lax.all_gather(grad, "dp", axis=0, axis_index_groups=neighbours)
    result, curvature = kernel_call(
        precondition,
        (shape((TILE, width), F32), shape((8, TILE), F32)),
        [WHOLE] * 3,
        flops=4 * width * width * TILE,
        moved=megabyte,
    )(grads, left, right)

    planes = [[y * chips + i for i in range(chips)] for y in range(2)]
    curvature = lax.all_to_all(
        jnp.broadcast_to(curvature, (chips, 8, TILE)),
        "dp", 0, 0, tiled=True, axis_index_groups=planes,
    )
    curvature = jnp.sum(curvature, axis=0)
    across = [
        [(y * chips + i) * columns + c for y in range(2) for c in range(columns)] for i in range(chips)
    ]
    curvature = lax.all_to_all(
        jnp.broadcast_to(curvature, (2 * columns, 8, TILE)),
        ("dp", "mp"), 0, 0, tiled=True, axis_index_groups=across,
    )
    curvature = jnp.sum(curvature, axis=0)[0, 0]
    entries = float(feature_count * width * columns)
    clip_scale = jnp.minimum(1.0, jnp.sqrt(entries / jnp.abs(curvature)))
    return (factor_out[None, None], inverse_out[None, None], clip_scale * result)


def solution(mesh):
    return jax.shard_map(
        local,
        mesh=mesh,
        in_specs=(
            P("dp", None),
            P("dp", "mp"),
            P("dp"),
            P("mp", "dp", None, None, None),
            P("mp", "dp", None, None, None),
            P(),
            P(),
        ),
        out_specs=(P("mp", "dp", None, None), P("mp", "dp", None, None), P("dp", "mp")),
        check_vma=False,
    )
```

```python
import jax
import jax.numpy as jnp
from jax import lax
from jax.experimental import pallas as pl
from jax.experimental.pallas import tpu as pltpu
from jax.sharding import PartitionSpec as P

DECAY = 0.9
DAMPING = 0.01
TILE = 128
ROWS = 16
VMEM_BYTES = 48 * 1024 * 1024
BF16 = jnp.bfloat16
F32 = jnp.float32
PARAMS = pltpu.CompilerParams(vmem_limit_bytes=VMEM_BYTES)
SCALARS = pl.BlockSpec(memory_space=pltpu.SMEM)
WHOLE = pl.BlockSpec(memory_space=pltpu.VMEM)
ANYWHERE = pl.BlockSpec(memory_space=pltpu.HBM)


def upper_pairs(tiles):
    return [(a, b) for a in range(tiles) for b in range(a, tiles)]


def diagonal_mask():
    rows = lax.broadcasted_iota(jnp.int32, (TILE, TILE), 0)
    return rows == lax.broadcasted_iota(jnp.int32, (TILE, TILE), 1)


def tile_of(a, b):
    return (slice(a * TILE, (a + 1) * TILE), slice(b * TILE, (b + 1) * TILE))


def turn_of(core):
    return core * (lax.axis_size("dp") // 8)


class Facts:
    def __init__(self, old_owner=None, new_owner=None):
        member = lax.axis_index("dp")
        self.column = lax.axis_index("mp")
        chips = lax.axis_size("dp") // 2
        self.core = member & 1
        self.plane = jnp.where(member >= chips, 1, 0)
        self.turn = turn_of(self.core)
        self.place = member & (lax.axis_size("dp") // lax.axis_size("mp") - 1)
        self.flip = jnp.where(self.column >= lax.axis_size("mp") // 2, 1, 0)
        self.own_kind = self.plane ^ self.flip
        if old_owner is not None:
            owners = [old_owner[self.column, kind] for kind in range(2)]
            self.shared = jnp.where(owners[0] == owners[1], 1, 0)
            self.same_core = [jnp.where((o & 1) == self.core, 1, 0) for o in owners]
            self.same_plane = [
                jnp.where(jnp.where(o >= chips, 1, 0) == self.plane, 1, 0) for o in owners
            ]
            self.slots = [lax.shift_right_logical(o & (chips - 1), 1) ^ self.turn for o in owners]
        if new_owner is not None:
            self.keeps = [
                jnp.where(new_owner[self.column, kind] == member, 1, 0) for kind in range(2)
            ]


def first_parts(
    owners, counts, features, out_grads, factors, inverses,
    keep, send, turned,
    own, grads, kept, held, packed, diag, arrived,
):
    facts = Facts(owners)
    core, flip, count = facts.core, facts.flip, counts[0]
    rows, width = own.shape
    tiles = width // TILE
    on_diagonal = diagonal_mask()
    start = pl.multiple_of(facts.column * width, width)
    loads = [
        pltpu.make_async_copy(features.at[:, pl.ds(start, width)], own, arrived.at[0]),
        pltpu.make_async_copy(out_grads, grads, arrived.at[1]),
    ] + [
        pltpu.make_async_copy(
            source.at[facts.shared if kind else 0],
            held.at[which * 2 + kind],
            arrived.at[2 + which * 2 + kind],
        )
        for which, source in enumerate((factors, inverses))
        for kind in range(2)
    ]
    for load in loads:
        load.start()
    valid = lax.broadcasted_iota(jnp.int32, (rows, width), 0) < count
    for kind, (block, left) in enumerate(((own, kept), (grads, turned))):
        loads[kind].wait()
        left[...] = jnp.where(valid, block[...].astype(F32), 0.0).T.astype(BF16)
        for a, b in upper_pairs(tiles // 2):
            square = jnp.dot(
                left[2 * a * TILE : 2 * (a + 1) * TILE, :],
                block[:, 2 * b * TILE : 2 * (b + 1) * TILE],
                preferred_element_type=F32,
            ).astype(BF16)
            for i in range(2):
                for j in range(2):
                    if 2 * a + i <= 2 * b + j:
                        at = upper_pairs(tiles).index((2 * a + i, 2 * b + j))
                        packed[kind, 2, at * TILE : (at + 1) * TILE, :] = square[tile_of(i, j)]
    for which in range(2):
        for kind in range(2):
            loads[2 + which * 2 + kind].wait()
            for n, (a, b) in enumerate(upper_pairs(tiles)):
                piece = held[(which * 2 + kind,) + tile_of(a, b)]
                if a == b:
                    row = (which * 2 + kind) * tiles + a
                    diag[row : row + 1, :] = jnp.sum(
                        jnp.where(on_diagonal, piece, 0.0), axis=0, keepdims=True
                    )
                    piece = jnp.where(on_diagonal, 0.0, piece)
                packed[kind, which, n * TILE : (n + 1) * TILE, :] = piece.astype(BF16)
    high = diag[...].astype(BF16)
    low = (diag[...] - high.astype(F32)).astype(BF16)
    words = jnp.concatenate([high, low], axis=0)
    quarter = lax.broadcasted_iota(jnp.int32, (ROWS, TILE), 0) // 4
    digits = lax.shift_right_logical(jnp.full((ROWS, TILE), count), 3 * quarter) & 7
    digits = digits.astype(F32).astype(BF16)
    chips = keep.shape[0]
    share = (keep.shape[1] - words.shape[0] - ROWS) // 3
    sums = 2 * share + words.shape[0]
    for q in range(chips):
        plane, pair = divmod(q, chips // 2)
        kind = flip if plane == 0 else 1 - flip
        for ref, parity in ((keep, core), (send, 1 - core)):
            start = pl.multiple_of((2 * pair + parity) * share, ROWS)
            for which, at in enumerate((0, share, sums)):
                ref[q, at : at + share, :] = packed[kind, which, pl.ds(start, share), :]
            ref[q, 2 * share : sums, :] = words
            ref[q, sums + share :, :] = digits


def merge_words(first_flag, second_flag, one, two):
    lanes = one.shape[0] // 8
    kinds = (lax.broadcasted_iota(jnp.int32, one.shape, 0) // lanes) % 2
    flags = jnp.where(kinds == 0, first_flag, second_flag)
    return jnp.where(flags == 1, one.astype(F32), two.astype(F32))


def choose_core(owners, keep, received, unread, near_old, near_sum, far):
    facts = Facts(owners)
    first, second = facts.same_core
    ring, rows = near_old.shape[0], near_old.shape[1]
    data = rows // 6 * 5
    words = merge_words(first, second, keep[0, data:rows, :], received[0, data:rows, :]).astype(BF16)
    for old, at, kind in (
        (near_old, facts.plane, facts.own_kind),
        (far, 1 - facts.plane, 1 - facts.own_kind),
    ):
        flag = jnp.where(kind == 0, first, second)

        @pl.when(flag == 1)
        def _():
            old[:, :data, :] = keep[pl.ds(at * ring, ring), :data, :]

        @pl.when(flag == 0)
        def _():
            old[:, :data, :] = received[pl.ds(at * ring, ring), :data, :]

        for z in range(ring):
            old[z, data:rows, :] = words
        chips = pl.ds(at * ring, ring)
        total = keep[chips, rows:, :].astype(F32) + received[chips, rows:, :].astype(F32)
        if old is far:
            far[:, rows:, :] = total.astype(BF16)
        else:
            near_sum[...] = total


def join_planes(owners, near_old, near_sum, arrived, unread, other_unread, out):
    facts = Facts(owners)
    first, second = facts.same_plane
    flag = jnp.where(facts.own_kind == 0, first, second)
    ring, rows = near_old.shape[0], near_old.shape[1]
    data = rows // 6 * 5

    words = merge_words(first, second, near_old[0, data:, :], arrived[0, data:rows, :]).astype(BF16)
    for slot in range(ring):
        z = slot ^ facts.turn

        @pl.when(flag == 1)
        def _():
            out[slot, :data, :] = near_old[z, :data, :]

        @pl.when(flag == 0)
        def _():
            out[slot, :data, :] = arrived[z, :data, :]

        out[slot, data:rows, :] = words
        out[slot, rows:, :] = (near_sum[z] + arrived[z, rows:, :].astype(F32)).astype(BF16)


def make_shares(owners, arrived, shares, diag):
    facts = Facts(owners)
    own_kind = facts.own_kind
    first, second = facts.slots
    ring, rows = shares.shape[0], shares.shape[1]
    share = rows // 2
    words = rows // 5 + rows
    owner = jnp.where(own_kind == 0, first, second)
    both = merge_words(1, 0, arrived[first, rows:words, :], arrived[second, rows:words, :])
    diag[...] = both[: diag.shape[0]] + both[diag.shape[0] :]
    summed = sum(arrived[z, words:, :].astype(F32) for z in range(ring))
    total = sum(summed[share + 4 * d : share + 4 * d + 1, :] * float(8**d) for d in range(4))
    factor = DECAY * arrived[owner, :share, :].astype(F32) + (1.0 - DECAY) * summed[:share] / total
    factor = factor.astype(BF16)
    inverse = arrived[owner, share:rows, :]
    for z in range(ring):
        shares[z, :share, :] = factor
        shares[z, share:, :] = inverse


def gradient_tiles(turned, tiles):
    block = jnp.concatenate([tile[...] for tile in tiles], axis=1)
    return jnp.dot(turned[...], block, preferred_element_type=F32)


def gradient_send(scalars, turned, *refs):
    product = gradient_tiles(turned, refs[:4])
    for n in range(4):
        refs[-1][n] = product[:, n * TILE : (n + 1) * TILE].astype(BF16)


def gradient_add(scalars, turned, *refs):
    received, out = refs[4], refs[-1]
    product = gradient_tiles(turned, refs[:4])
    for n in range(4):
        total = product[:, n * TILE : (n + 1) * TILE] + received[n].astype(F32)
        out[n] = total.astype(out.dtype)


def add_planes(near, arrived, out):
    turn = Facts().turn
    for slot in range(out.shape[0]):
        z = slot ^ turn
        out[slot] = (near[z] + arrived[z].astype(F32)).astype(BF16)


def unpack(mine, other, core, packed):
    share = mine.shape[1] // 2
    for slot in range(mine.shape[0]):
        for ref, parity in ((mine, core), (other, 1 - core)):
            pair = slot ^ turn_of(parity)
            start = pl.multiple_of((2 * pair + parity) * share, ROWS)
            for which in range(2):
                packed[which, pl.ds(start, share), :] = ref[
                    slot, which * share : (which + 1) * share, :
                ]


def spread(packed, which, diag, row, scale, high, low):
    tiles = high.shape[0] // TILE
    on_diagonal = diagonal_mask()
    for n, (a, b) in enumerate(upper_pairs(tiles)):
        piece = packed[which, n * TILE : (n + 1) * TILE, :].astype(F32)
        if a == b:
            exact = piece + jnp.where(on_diagonal, scale * diag[row + a : row + a + 1, :], 0.0)
            rounded = exact.astype(BF16)
            high[tile_of(a, a)] = rounded
            rest = jnp.sum(exact - rounded.astype(F32), axis=1, keepdims=True)
            low[a * TILE : (a + 1) * TILE, :] = jnp.broadcast_to(rest, (TILE, TILE))
        else:
            high[tile_of(a, b)] = packed[which, n * TILE : (n + 1) * TILE, :]
            high[tile_of(b, a)] = piece.T.astype(BF16)


def fill_blocks(kind, packed, diag, factor, factor_low, inverse, inverse_low):
    tiles = factor.shape[0] // TILE
    spread(packed, 0, diag, kind * tiles, DECAY, factor, factor_low)
    spread(packed, 1, diag, (2 + kind) * tiles, 1.0, inverse, inverse_low)


def times(high, low, right):
    width = right.shape[1]
    first = right.astype(BF16)
    second = (right - first.astype(F32)).astype(BF16)
    both = jnp.dot(high[...], jnp.concatenate([first, second], axis=1), preferred_element_type=F32)
    return both[:, :width] + both[:, width:] + low * right


def refine(factor, factor_low, inverse, inverse_low, part):
    inner = times(factor, factor_low[:, :1] + DAMPING, part)
    return 2.0 * part - times(inverse, inverse_low[:, :1], inner)


def exact_block(high, low):
    rows = lax.broadcasted_iota(jnp.int32, high.shape, 0)
    columns = lax.broadcasted_iota(jnp.int32, high.shape, 1)
    return high[...].astype(F32) + jnp.where(rows == columns, low[:, :1], 0.0)


def left_columns(mine, other, diag, left, packed, factor, factor_low, inverse, inverse_low):
    facts = Facts()
    core, place = facts.core, facts.place
    unpack(mine, other, core, packed)
    fill_blocks(0, packed, diag, factor, factor_low, inverse, inverse_low)
    start = pl.multiple_of(place * TILE, TILE)
    part = inverse[:, pl.ds(start, TILE)].astype(F32)
    rows = lax.broadcasted_iota(jnp.int32, part.shape, 0) - start
    part = part + jnp.where(
        rows == lax.broadcasted_iota(jnp.int32, part.shape, 1), inverse_low[...], 0.0
    )
    left[...] = refine(factor, factor_low, inverse, inverse_low, part).astype(BF16)


def new_blocks(
    owners, mine, other, far_mine, far_other, diag, right, factor_out, inverse_out,
    packed, factor, factor_low, inverse, inverse_low,
):
    facts = Facts(new_owner=owners)
    core, own_kind = facts.core, facts.own_kind
    first, second = facts.keeps
    blocks = (factor, factor_low, inverse, inverse_low)

    def load_blocks(kind):
        @pl.when(own_kind == kind)
        def _():
            unpack(mine, other, core, packed)

        @pl.when(own_kind != kind)
        def _():
            unpack(far_mine, far_other, core, packed)

        fill_blocks(kind, packed, diag, *blocks)

    load_blocks(1)
    fresh = refine(*blocks, exact_block(inverse, inverse_low))
    right[...] = fresh.astype(BF16)

    @pl.when(second == 1)
    def _():
        factor_out[...] = exact_block(factor, factor_low)
        inverse_out[...] = fresh

    @pl.when(second == 0)
    def _():
        factor_out[...] = jnp.zeros_like(factor_out)
        inverse_out[...] = jnp.zeros_like(inverse_out)

    @pl.when(first == 1)
    def _():
        load_blocks(0)
        factor_out[...] = exact_block(factor, factor_low)
        inverse_out[...] = refine(*blocks, exact_block(inverse, inverse_low))


def precondition(grad, left, right, result, curvature):
    own = Facts().place
    half = sum(
        jnp.dot(grad[p], left[p * TILE : (p + 1) * TILE, :], preferred_element_type=F32)
        for p in range(grad.shape[0])
    )
    product = jnp.dot(half.T.astype(BF16), right[...], preferred_element_type=F32)
    result[...] = product
    curvature[...] = jnp.full(curvature.shape, jnp.sum(product * grad[own].astype(F32).T))


def kernel_call(body, out_shape, in_specs, scratch=(), out_specs=None, aliases=None, flops=0, moved=0):
    if out_specs is None:
        out_specs = (WHOLE,) * len(out_shape) if isinstance(out_shape, tuple) else WHOLE
    return pl.pallas_call(
        body,
        out_shape=out_shape,
        in_specs=in_specs,
        out_specs=out_specs,
        input_output_aliases=aliases or {},
        scratch_shapes=list(scratch),
        compiler_params=PARAMS,
        cost_estimate=pl.CostEstimate(flops=flops, bytes_accessed=moved, transcendentals=0),
        name=body.__name__,
    )


def local(features, out_grads, counts, factor_old, inverse_old, old_owner, new_owner):
    tok_rows, width = out_grads.shape
    feature_count = features.shape[1]
    column = lax.axis_index("mp")
    member = lax.axis_index("dp")
    members = lax.axis_size("dp")
    columns = lax.axis_size("mp")
    chips = members // 2
    ring = chips // 2
    core = member & 1
    core_swap = [(i, i ^ 1) for i in range(members)]
    plane_swap = [(i, (i + chips) % members) for i in range(members)]
    rings = [
        [y * chips + 2 * (z ^ turn_of(c)) + c for z in range(ring)] for y in range(2) for c in range(2)
    ]
    packed_rows = width * (width + TILE) // 2 // TILE
    share = 2 * packed_rows // members
    lanes = width // TILE
    holders = members // columns
    shape = jax.ShapeDtypeStruct
    megabyte = 2 * width * width * 2

    def across_ring(parts):
        return lax.all_to_all(parts, "dp", 0, 0, tiled=True, axis_index_groups=rings)

    def swap_cores(send):
        return lax.ppermute(send, "dp", core_swap)

    def swap_planes(send):
        return lax.ppermute(send, "dp", plane_swap)

    message = shape((chips, 3 * share + 8 * lanes + ROWS, TILE), BF16)
    keep, send, turned = kernel_call(
        first_parts,
        (message, message, shape((width, tok_rows), BF16)),
        [SCALARS, SCALARS] + [ANYWHERE] * 4,
        [
            pltpu.VMEM((tok_rows, width), BF16),
            pltpu.VMEM((tok_rows, width), BF16),
            pltpu.VMEM((width, tok_rows), BF16),
            pltpu.VMEM((4, width, width), F32),
            pltpu.VMEM((2, 3, packed_rows, TILE), BF16),
            pltpu.VMEM((4 * lanes, TILE), F32),
            pltpu.SemaphoreType.DMA((6,)),
        ],
        flops=4 * tok_rows * width * width,
        moved=10 * megabyte,
    )(old_owner, counts, features, out_grads, factor_old[0, 0], inverse_old[0, 0])
    old_rows = 2 * share + 8 * lanes
    far_shape = shape((ring,) + message.shape[1:], BF16)
    def gradient(body, parity, which, dtype, name, other):
        def chip_at(i, s):
            return s[1] * ring + 4 * i

        def tile_spec(n):
            return pl.BlockSpec((tok_rows, TILE), lambda i, s: (0, 2 * (chip_at(i, s) + n) + s[0]))

        four_chips = pl.BlockSpec((4, width, TILE), lambda i, s: (i, 0, 0))
        return pl.pallas_call(
            body,
            out_shape=shape((ring, width, TILE), dtype),
            grid_spec=pltpu.PrefetchScalarGridSpec(
                num_scalar_prefetch=1,
                grid=(ring // 4,),
                in_specs=[pl.BlockSpec((width, tok_rows), lambda i, s: (0, 0))]
                + [tile_spec(n) for n in range(4)]
                + [four_chips if body is gradient_add else ANYWHERE],
                out_specs=four_chips,
            ),
            compiler_params=PARAMS,
            cost_estimate=pl.CostEstimate(
                flops=2 * ring * tok_rows * width * TILE,
                bytes_accessed=ring * megabyte // 2,
                transcendentals=0,
            ),
            name=name,
        )(jnp.stack([parity, which]), turned, features, features, features, features, other)

    plane = jnp.where(member >= chips, 1, 0)
    send_far = gradient(gradient_send, 1 - core, 1 - plane, BF16, "send_far", counts)
    received_far = swap_cores(send_far)
    near_old, near_sum, far = kernel_call(
        choose_core,
        (shape((ring, old_rows, TILE), BF16), shape((ring, share + ROWS, TILE), F32), far_shape),
        [SCALARS, WHOLE, WHOLE, ANYWHERE],
        moved=2 * megabyte,
    )(old_owner, keep, swap_cores(send), send_far)
    arrived = swap_planes(far)

    send_near = gradient(gradient_send, 1 - core, plane, BF16, "send_near", far)
    far_grad = gradient(gradient_add, core, 1 - plane, BF16, "gradient_far", received_far)
    arrived_grad = swap_planes(far_grad)
    near_grad = gradient(
        gradient_add, core, plane, F32, "gradient_near", swap_cores(send_near)
    )
    joined = kernel_call(
        join_planes,
        far_shape,
        [SCALARS] + [WHOLE] * 3 + [ANYWHERE] * 2,
        moved=megabyte,
    )(old_owner, near_old, near_sum, arrived, far_grad, send_near)
    shares, diag = kernel_call(
        make_shares,
        (shape((ring, 2 * share, TILE), BF16), shape((4 * lanes, TILE), F32)),
        [SCALARS, WHOLE],
        moved=megabyte,
    )(old_owner, across_ring(joined))

    mine = across_ring(shares)
    other = swap_cores(mine)
    far_mine = swap_planes(mine)
    far_other = swap_cores(far_mine)
    unpacked = [
        pltpu.VMEM((2, packed_rows, TILE), BF16),
        pltpu.VMEM((width, width), BF16),
        pltpu.VMEM((width, TILE), F32),
        pltpu.VMEM((width, width), BF16),
        pltpu.VMEM((width, TILE), F32),
    ]
    left = kernel_call(
        left_columns,
        shape((width, TILE), BF16),
        [WHOLE] * 3,
        unpacked,
        flops=8 * width * width * TILE,
        moved=2 * megabyte,
    )(mine, other, diag)
    gates = [(i, i // holders) for i in range(members)]
    near = lax.ppermute(
        left, ("dp", "mp"), [(i * columns + g, i * columns + (g ^ 1)) for i, g in gates]
    )
    gate = lax.shift_right_logical(member, holders.bit_length() - 1)
    left = jnp.where(column == gate, left, near)
    left = jnp.where(
        (column ^ gate) <= 1,
        left,
        sum(
            lax.ppermute(
                left,
                ("dp", "mp"),
                [
                    (i * columns + g, i * columns + (g + 2 * step) % columns)
                    for i, at in gates
                    for g in (at, at ^ 1)
                ],
            )
            for step in range(1, columns // 2)
        ),
    )
    square = shape((width, width), F32)
    right, factor_out, inverse_out = kernel_call(
        new_blocks,
        (shape((width, width), BF16), square, square),
        [SCALARS] + [WHOLE] * 5,
        unpacked,
        flops=8 * width * width * width,
        moved=6 * megabyte,
    )(new_owner, mine, other, far_mine, far_other, diag)

    grad = across_ring(
        kernel_call(add_planes, shape(far_grad.shape, BF16), [WHOLE] * 2, moved=4 * megabyte)(
            near_grad, arrived_grad
        )
    )
    grad = jnp.sum(grad.astype(F32), axis=0).astype(BF16)
    neighbours = [[holders * c + r for r in range(holders)] for c in range(columns)]
    grads = lax.all_gather(grad, "dp", axis=0, axis_index_groups=neighbours)
    result, curvature = kernel_call(
        precondition,
        (shape((TILE, width), F32), shape((8, TILE), F32)),
        [WHOLE] * 3,
        flops=4 * width * width * TILE,
        moved=megabyte,
    )(grads, left, right)

    planes = [[y * chips + i for i in range(chips)] for y in range(2)]
    curvature = lax.all_to_all(
        jnp.broadcast_to(curvature, (chips, 8, TILE)),
        "dp", 0, 0, tiled=True, axis_index_groups=planes,
    )
    curvature = jnp.sum(curvature, axis=0)
    rings = [
        [(y * chips + i) * columns + c for y in range(2) for c in range(columns)] for i in range(chips)
    ]
    curvature = lax.all_to_all(
        jnp.broadcast_to(curvature, (2 * columns, 8, TILE)),
        ("dp", "mp"), 0, 0, tiled=True, axis_index_groups=rings,
    )
    curvature = jnp.sum(curvature, axis=0)[0, 0]
    entries = float(feature_count * width * columns)
    clip_scale = jnp.minimum(1.0, jnp.sqrt(entries / jnp.abs(curvature)))
    return (factor_out[None, None], inverse_out[None, None], clip_scale * result)


def solution(mesh):
    return jax.shard_map(
        local,
        mesh=mesh,
        in_specs=(
            P("dp", None),
            P("dp", "mp"),
            P("dp"),
            P("mp", "dp", None, None, None),
            P("mp", "dp", None, None, None),
            P(),
            P(),
        ),
        out_specs=(P("mp", "dp", None, None), P("mp", "dp", None, None), P("dp", "mp")),
        check_vma=False,
    )
```

```python
import functools

import jax
import jax.numpy as jnp
from jax import lax
from jax.experimental import pallas as pl
from jax.experimental.pallas import tpu as pltpu
from jax.sharding import PartitionSpec as P

DECAY = 0.9
DAMPING = 0.01
TILE = 128
ROWS = 16
VMEM_BYTES = 48 * 1024 * 1024
BF16 = jnp.bfloat16
F32 = jnp.float32
PARAMS = pltpu.CompilerParams(vmem_limit_bytes=VMEM_BYTES)
SCALARS = pl.BlockSpec(memory_space=pltpu.SMEM)
WHOLE = pl.BlockSpec(memory_space=pltpu.VMEM)
ANYWHERE = pl.BlockSpec(memory_space=pltpu.HBM)


def upper_pairs(tiles):
    return [(a, b) for a in range(tiles) for b in range(a, tiles)]


def diagonal_mask():
    rows = lax.broadcasted_iota(jnp.int32, (TILE, TILE), 0)
    return rows == lax.broadcasted_iota(jnp.int32, (TILE, TILE), 1)


def tile_of(a, b):
    return (slice(a * TILE, (a + 1) * TILE), slice(b * TILE, (b + 1) * TILE))


def clip(entries, result, partials, update):
    curvature = jnp.sum(partials[...], axis=0)[:1, :1]
    scale = jnp.minimum(1.0, jnp.sqrt(entries / jnp.abs(curvature)))
    update[...] = scale * result[...]


class Facts:
    def __init__(self, old_owner=None, new_owner=None):
        member = lax.axis_index("dp")
        self.column = lax.axis_index("mp")
        chips = lax.axis_size("dp") // 2
        self.core = member & 1
        self.plane = jnp.where(member >= chips, 1, 0)
        self.place = member & (lax.axis_size("dp") // lax.axis_size("mp") - 1)
        self.flip = jnp.where(self.column >= lax.axis_size("mp") // 2, 1, 0)
        self.own_kind = self.plane ^ self.flip
        if old_owner is not None:
            owners = [old_owner[self.column, kind] for kind in range(2)]
            self.shared = jnp.where(owners[0] == owners[1], 1, 0)
            self.same_core = [jnp.where((o & 1) == self.core, 1, 0) for o in owners]
            self.same_plane = [
                jnp.where(jnp.where(o >= chips, 1, 0) == self.plane, 1, 0) for o in owners
            ]
            self.ring_at = [lax.shift_right_logical(o & (chips - 1), 1) for o in owners]
        if new_owner is not None:
            self.keeps = [
                jnp.where(new_owner[self.column, kind] == member, 1, 0) for kind in range(2)
            ]


def first_parts(
    owners, counts, features, out_grads, factors, inverses,
    keep, send, turned,
    own, grads, kept, held, packed, diag, arrived,
):
    facts = Facts(owners)
    core, flip, count = facts.core, facts.flip, counts[0]
    rows, width = own.shape
    tiles = width // TILE
    on_diagonal = diagonal_mask()
    start = pl.multiple_of(facts.column * width, width)
    loads = [
        pltpu.make_async_copy(features.at[:, pl.ds(start, width)], own, arrived.at[0]),
        pltpu.make_async_copy(out_grads, grads, arrived.at[1]),
    ] + [
        pltpu.make_async_copy(
            source.at[facts.shared if kind else 0],
            held.at[which * 2 + kind],
            arrived.at[2 + which * 2 + kind],
        )
        for which, source in enumerate((factors, inverses))
        for kind in range(2)
    ]
    for load in loads:
        load.start()
    valid = lax.broadcasted_iota(jnp.int32, (rows, width), 0) < count
    for kind, (block, left) in enumerate(((own, kept), (grads, turned))):
        loads[kind].wait()
        left[...] = jnp.where(valid, block[...].astype(F32), 0.0).T.astype(BF16)
        for a, b in upper_pairs(tiles // 2):
            square = jnp.dot(
                left[2 * a * TILE : 2 * (a + 1) * TILE, :],
                block[:, 2 * b * TILE : 2 * (b + 1) * TILE],
                preferred_element_type=F32,
            ).astype(BF16)
            for i in range(2):
                for j in range(2):
                    if 2 * a + i <= 2 * b + j:
                        at = upper_pairs(tiles).index((2 * a + i, 2 * b + j))
                        packed[kind, 2, at * TILE : (at + 1) * TILE, :] = square[tile_of(i, j)]
    for which in range(2):
        for kind in range(2):
            loads[2 + which * 2 + kind].wait()
            for n, (a, b) in enumerate(upper_pairs(tiles)):
                piece = held[(which * 2 + kind,) + tile_of(a, b)]
                if a == b:
                    row = (which * 2 + kind) * tiles + a
                    diag[row : row + 1, :] = jnp.sum(
                        jnp.where(on_diagonal, piece, 0.0), axis=0, keepdims=True
                    )
                    piece = jnp.where(on_diagonal, 0.0, piece)
                packed[kind, which, n * TILE : (n + 1) * TILE, :] = piece.astype(BF16)
    high = diag[...].astype(BF16)
    low = (diag[...] - high.astype(F32)).astype(BF16)
    words = []
    for kind in range(2):
        ends = [((which * 2 + kind) * tiles, (which * 2 + kind + 1) * tiles) for which in range(2)]
        words.append(jnp.concatenate([w[a:b].astype(F32) for w in (high, low) for a, b in ends], axis=0))
    quarter = lax.broadcasted_iota(jnp.int32, (ROWS, TILE), 0) // 4
    digits = lax.shift_right_logical(jnp.full((ROWS, TILE), count), 3 * quarter) & 7
    digits = digits.astype(F32).astype(BF16)
    chips = keep.shape[0]
    share = (keep.shape[1] - 4 * tiles - ROWS) // 3
    sums = 2 * share + 4 * tiles
    of_plane = [
        jnp.where(flip == first, words[0], words[1]).astype(BF16) for first in range(2)
    ]
    for q in range(chips):
        plane, pair = divmod(q, chips // 2)
        kind = flip if plane == 0 else 1 - flip
        for ref, parity in ((keep, core), (send, 1 - core)):
            start = pl.multiple_of((2 * pair + parity) * share, ROWS)
            for which, at in enumerate((0, share, sums)):
                ref[q, at : at + share, :] = packed[kind, which, pl.ds(start, share), :]
            ref[q, 2 * share : sums, :] = of_plane[plane]
            ref[q, sums + share :, :] = digits


def choose_core(owners, keep, received, unread, near_old, near_sum, far):
    facts = Facts(owners)
    first, second = facts.same_core
    ring, rows = near_old.shape[0], near_old.shape[1]
    for old, at, kind in (
        (near_old, facts.plane, facts.own_kind),
        (far, 1 - facts.plane, 1 - facts.own_kind),
    ):
        flag = jnp.where(kind == 0, first, second)
        chips = pl.ds(at * ring, ring)

        @pl.when(flag == 1)
        def _():
            old[:, :rows, :] = keep[chips, :rows, :]

        @pl.when(flag == 0)
        def _():
            old[:, :rows, :] = received[chips, :rows, :]

        total = keep[chips, rows:, :].astype(F32) + received[chips, rows:, :].astype(F32)
        if old is far:
            far[:, rows:, :] = total.astype(BF16)
        else:
            near_sum[...] = total


def join_planes(owners, near_old, near_sum, arrived, unread, other_unread, out):
    facts = Facts(owners)
    first, second = facts.same_plane
    flag = jnp.where(facts.own_kind == 0, first, second)
    rows = near_old.shape[1]

    @pl.when(flag == 1)
    def _():
        out[:, :rows, :] = near_old[...]

    @pl.when(flag == 0)
    def _():
        out[:, :rows, :] = arrived[:, :rows, :]

    out[:, rows:, :] = (near_sum[...] + arrived[:, rows:, :].astype(F32)).astype(BF16)


def make_shares(owners, arrived, shares, diag):
    facts = Facts(owners)
    ring, rows = shares.shape[0], shares.shape[1]
    share, lanes = rows // 2, diag.shape[0]
    sums = rows + 2 * lanes
    owner = jnp.where(facts.own_kind == 0, facts.ring_at[0], facts.ring_at[1])
    words = arrived[owner, rows:sums, :].astype(F32)
    diag[...] = words[:lanes] + words[lanes:]
    summed = sum(arrived[z, sums:, :].astype(F32) for z in range(ring))
    total = sum(summed[share + 4 * d : share + 4 * d + 1, :] * float(8**d) for d in range(4))
    factor = DECAY * arrived[owner, :share, :].astype(F32) + (1.0 - DECAY) * summed[:share] / total
    factor = factor.astype(BF16)
    inverse = arrived[owner, share:rows, :]
    for z in range(ring):
        shares[z, :share, :] = factor
        shares[z, share:, :] = inverse


def gradient_tiles(turned, tiles):
    block = jnp.concatenate([tile[...] for tile in tiles], axis=1)
    return jnp.dot(turned[...], block, preferred_element_type=F32)


def gradient_send(scalars, turned, *refs):
    product = gradient_tiles(turned, refs[:4])
    for n in range(4):
        refs[-1][n] = product[:, n * TILE : (n + 1) * TILE].astype(BF16)


def gradient_add(scalars, turned, *refs):
    received, out = refs[4], refs[-1]
    product = gradient_tiles(turned, refs[:4])
    for n in range(4):
        total = product[:, n * TILE : (n + 1) * TILE] + received[n].astype(F32)
        out[n] = total.astype(out.dtype)


def unpack(mine, other, core, packed):
    share = mine.shape[1] // 2
    for pair in range(mine.shape[0]):
        for ref, parity in ((mine, core), (other, 1 - core)):
            start = pl.multiple_of((2 * pair + parity) * share, ROWS)
            for which in range(2):
                packed[which, pl.ds(start, share), :] = ref[
                    pair, which * share : (which + 1) * share, :
                ]


def spread(packed, which, diag, row, scale, high, low):
    tiles = high.shape[0] // TILE
    on_diagonal = diagonal_mask()
    for n, (a, b) in enumerate(upper_pairs(tiles)):
        piece = packed[which, n * TILE : (n + 1) * TILE, :].astype(F32)
        if a == b:
            exact = piece + jnp.where(on_diagonal, scale * diag[row + a : row + a + 1, :], 0.0)
            rounded = exact.astype(BF16)
            high[tile_of(a, a)] = rounded
            rest = jnp.sum(exact - rounded.astype(F32), axis=1, keepdims=True)
            low[a * TILE : (a + 1) * TILE, :] = jnp.broadcast_to(rest, (TILE, TILE))
        else:
            high[tile_of(a, b)] = packed[which, n * TILE : (n + 1) * TILE, :]
            high[tile_of(b, a)] = piece.T.astype(BF16)


def fill_blocks(packed, diag, factor, factor_low, inverse, inverse_low):
    spread(packed, 0, diag, 0, DECAY, factor, factor_low)
    spread(packed, 1, diag, factor.shape[0] // TILE, 1.0, inverse, inverse_low)


def times(high, low, right):
    width = right.shape[1]
    first = right.astype(BF16)
    second = (right - first.astype(F32)).astype(BF16)
    both = jnp.dot(high[...], jnp.concatenate([first, second], axis=1), preferred_element_type=F32)
    return both[:, :width] + both[:, width:] + low * right


def refine(factor, factor_low, inverse, inverse_low, part):
    inner = times(factor, factor_low[:, :1] + DAMPING, part)
    return 2.0 * part - times(inverse, inverse_low[:, :1], inner)


def exact_block(high, low):
    rows = lax.broadcasted_iota(jnp.int32, high.shape, 0)
    columns = lax.broadcasted_iota(jnp.int32, high.shape, 1)
    return high[...].astype(F32) + jnp.where(rows == columns, low[:, :1], 0.0)


def left_columns(mine, other, diag, left, packed, factor, factor_low, inverse, inverse_low):
    facts = Facts()
    core, place = facts.core, facts.place
    unpack(mine, other, core, packed)
    fill_blocks(packed, diag, factor, factor_low, inverse, inverse_low)
    start = pl.multiple_of(place * TILE, TILE)
    part = inverse[:, pl.ds(start, TILE)].astype(F32)
    rows = lax.broadcasted_iota(jnp.int32, part.shape, 0) - start
    part = part + jnp.where(
        rows == lax.broadcasted_iota(jnp.int32, part.shape, 1), inverse_low[...], 0.0
    )
    left[...] = refine(factor, factor_low, inverse, inverse_low, part).astype(BF16)


def new_blocks(
    owners, mine, other, far_mine, far_other, diag, far_diag, right, factor_out, inverse_out,
    packed, factor, factor_low, inverse, inverse_low, lanes,
):
    facts = Facts(new_owner=owners)
    core, own_kind = facts.core, facts.own_kind
    first, second = facts.keeps
    blocks = (factor, factor_low, inverse, inverse_low)

    def load_blocks(kind):
        @pl.when(own_kind == kind)
        def _():
            unpack(mine, other, core, packed)
            lanes[...] = diag[...]

        @pl.when(own_kind != kind)
        def _():
            unpack(far_mine, far_other, core, packed)
            lanes[...] = far_diag[...]

        fill_blocks(packed, lanes, *blocks)

    load_blocks(1)
    fresh = refine(*blocks, exact_block(inverse, inverse_low))
    right[...] = fresh.astype(BF16)

    @pl.when(second == 1)
    def _():
        factor_out[...] = exact_block(factor, factor_low)
        inverse_out[...] = fresh

    @pl.when(second == 0)
    def _():
        factor_out[...] = jnp.zeros_like(factor_out)
        inverse_out[...] = jnp.zeros_like(inverse_out)

    @pl.when(first == 1)
    def _():
        load_blocks(0)
        factor_out[...] = exact_block(factor, factor_low)
        inverse_out[...] = refine(*blocks, exact_block(inverse, inverse_low))


def precondition(grad, left, right, result, curvature):
    own = Facts().place
    half = sum(
        jnp.dot(grad[p], left[p * TILE : (p + 1) * TILE, :], preferred_element_type=F32)
        for p in range(grad.shape[0])
    )
    product = jnp.dot(half.T.astype(BF16), right[...], preferred_element_type=F32)
    result[...] = product
    curvature[...] = jnp.full(curvature.shape, jnp.sum(product * grad[own].astype(F32).T))


def kernel_call(body, out_shape, in_specs, scratch=(), out_specs=None, aliases=None, flops=0, moved=0, name=None):
    if out_specs is None:
        out_specs = (WHOLE,) * len(out_shape) if isinstance(out_shape, tuple) else WHOLE
    return pl.pallas_call(
        body,
        out_shape=out_shape,
        in_specs=in_specs,
        out_specs=out_specs,
        input_output_aliases=aliases or {},
        scratch_shapes=list(scratch),
        compiler_params=PARAMS,
        cost_estimate=pl.CostEstimate(flops=flops, bytes_accessed=moved, transcendentals=0),
        name=name or body.__name__,
    )


def local(features, out_grads, counts, factor_old, inverse_old, old_owner, new_owner):
    tok_rows, width = out_grads.shape
    feature_count = features.shape[1]
    column = lax.axis_index("mp")
    member = lax.axis_index("dp")
    members = lax.axis_size("dp")
    columns = lax.axis_size("mp")
    chips = members // 2
    ring = chips // 2
    core = member & 1
    core_swap = [(i, i ^ 1) for i in range(members)]
    plane_swap = [(i, (i + chips) % members) for i in range(members)]
    rings = [[y * chips + 2 * z + c for z in range(ring)] for y in range(2) for c in range(2)]
    packed_rows = width * (width + TILE) // 2 // TILE
    share = 2 * packed_rows // members
    lanes = width // TILE
    holders = members // columns
    shape = jax.ShapeDtypeStruct
    megabyte = 2 * width * width * 2

    def across_ring(parts):
        return lax.all_to_all(parts, "dp", 0, 0, tiled=True, axis_index_groups=rings)

    def swap_cores(send):
        return lax.ppermute(send, "dp", core_swap)

    def swap_planes(send):
        return lax.ppermute(send, "dp", plane_swap)

    message = shape((chips, 3 * share + 4 * lanes + ROWS, TILE), BF16)
    keep, send, turned = kernel_call(
        first_parts,
        (message, message, shape((width, tok_rows), BF16)),
        [SCALARS, SCALARS] + [ANYWHERE] * 4,
        [
            pltpu.VMEM((tok_rows, width), BF16),
            pltpu.VMEM((tok_rows, width), BF16),
            pltpu.VMEM((width, tok_rows), BF16),
            pltpu.VMEM((4, width, width), F32),
            pltpu.VMEM((2, 3, packed_rows, TILE), BF16),
            pltpu.VMEM((4 * lanes, TILE), F32),
            pltpu.SemaphoreType.DMA((6,)),
        ],
        flops=4 * tok_rows * width * width,
        moved=10 * megabyte,
    )(old_owner, counts, features, out_grads, factor_old[0, 0], inverse_old[0, 0])
    old_rows = 2 * share + 4 * lanes
    far_shape = shape((ring,) + message.shape[1:], BF16)
    def gradient(body, parity, which, dtype, name, other):
        def chip_at(i, s):
            return s[1] * ring + 4 * i

        def tile_spec(n):
            return pl.BlockSpec((tok_rows, TILE), lambda i, s: (0, 2 * (chip_at(i, s) + n) + s[0]))

        four_chips = pl.BlockSpec((4, width, TILE), lambda i, s: (i, 0, 0))
        return pl.pallas_call(
            body,
            out_shape=shape((ring, width, TILE), dtype),
            grid_spec=pltpu.PrefetchScalarGridSpec(
                num_scalar_prefetch=1,
                grid=(ring // 4,),
                in_specs=[pl.BlockSpec((width, tok_rows), lambda i, s: (0, 0))]
                + [tile_spec(n) for n in range(4)]
                + [four_chips if body is gradient_add else ANYWHERE],
                out_specs=four_chips,
            ),
            compiler_params=PARAMS,
            cost_estimate=pl.CostEstimate(
                flops=2 * ring * tok_rows * width * TILE,
                bytes_accessed=ring * megabyte // 2,
                transcendentals=0,
            ),
            name=name,
        )(jnp.stack([parity, which]), turned, features, features, features, features, other)

    plane = jnp.where(member >= chips, 1, 0)
    send_far = gradient(gradient_send, 1 - core, 1 - plane, BF16, "send_far", counts)
    received_far = swap_cores(send_far)
    near_old, near_sum, far = kernel_call(
        choose_core,
        (shape((ring, old_rows, TILE), BF16), shape((ring, share + ROWS, TILE), F32), far_shape),
        [SCALARS, WHOLE, WHOLE, ANYWHERE],
        moved=2 * megabyte,
    )(old_owner, keep, swap_cores(send), send_far)
    arrived = swap_planes(far)

    send_near = gradient(gradient_send, 1 - core, plane, BF16, "send_near", far)
    far_grad = gradient(gradient_add, core, 1 - plane, BF16, "gradient_far", received_far)
    arrived_grad = swap_planes(far_grad)
    near_grad = gradient(
        gradient_add, core, plane, F32, "gradient_near", swap_cores(send_near)
    )
    joined = kernel_call(
        join_planes,
        far_shape,
        [SCALARS] + [WHOLE] * 3 + [ANYWHERE] * 2,
        moved=megabyte,
    )(old_owner, near_old, near_sum, arrived, far_grad, send_near)
    shares, diag = kernel_call(
        make_shares,
        (shape((ring, 2 * share, TILE), BF16), shape((2 * lanes, TILE), F32)),
        [SCALARS, WHOLE],
        moved=megabyte,
    )(old_owner, across_ring(joined))

    mine = across_ring(shares)
    other = swap_cores(mine)
    far_mine = swap_planes(mine)
    far_other = swap_cores(far_mine)
    unpacked = [
        pltpu.VMEM((2, packed_rows, TILE), BF16),
        pltpu.VMEM((width, width), BF16),
        pltpu.VMEM((width, TILE), F32),
        pltpu.VMEM((width, width), BF16),
        pltpu.VMEM((width, TILE), F32),
    ]
    left = kernel_call(
        left_columns,
        shape((width, TILE), BF16),
        [WHOLE] * 3,
        unpacked,
        flops=8 * width * width * TILE,
        moved=2 * megabyte,
    )(mine, other, diag)
    gates = [(i, i // holders) for i in range(members)]
    near = lax.ppermute(
        left, ("dp", "mp"), [(i * columns + g, i * columns + (g ^ 1)) for i, g in gates]
    )
    gate = lax.shift_right_logical(member, holders.bit_length() - 1)
    left = jnp.where(column == gate, left, near)
    left = jnp.where(
        (column ^ gate) <= 1,
        left,
        sum(
            lax.ppermute(
                left,
                ("dp", "mp"),
                [
                    (i * columns + g, i * columns + (g + 2 * step) % columns)
                    for i, at in gates
                    for g in (at, at ^ 1)
                ],
            )
            for step in range(1, columns // 2)
        ),
    )
    square = shape((width, width), F32)
    right, factor_out, inverse_out = kernel_call(
        new_blocks,
        (shape((width, width), BF16), square, square),
        [SCALARS] + [WHOLE] * 6,
        unpacked + [pltpu.VMEM((2 * lanes, TILE), F32)],
        flops=8 * width * width * width,
        moved=6 * megabyte,
    )(new_owner, mine, other, far_mine, far_other, diag, swap_planes(diag))

    grad = across_ring((near_grad + arrived_grad.astype(F32)).astype(BF16))
    grad = jnp.sum(grad.astype(F32), axis=0).astype(BF16)
    neighbours = [[holders * c + r for r in range(holders)] for c in range(columns)]
    grads = lax.all_gather(grad, "dp", axis=0, axis_index_groups=neighbours)
    result, curvature = kernel_call(
        precondition,
        (shape((TILE, width), F32), shape((8, TILE), F32)),
        [WHOLE] * 3,
        flops=4 * width * width * TILE,
        moved=megabyte,
    )(grads, left, right)

    planes = [[y * chips + i for i in range(chips)] for y in range(2)]
    curvature = lax.all_to_all(
        jnp.broadcast_to(curvature, (chips, 8, TILE)),
        "dp", 0, 0, tiled=True, axis_index_groups=planes,
    )
    curvature = jnp.sum(curvature, axis=0)
    rings = [
        [(y * chips + i) * columns + c for y in range(2) for c in range(columns)] for i in range(chips)
    ]
    curvature = lax.all_to_all(
        jnp.broadcast_to(curvature, (2 * columns, 8, TILE)),
        ("dp", "mp"), 0, 0, tiled=True, axis_index_groups=rings,
    )
    entries = float(feature_count * width * columns)
    update = kernel_call(
        functools.partial(clip, entries), shape((TILE, width), F32), [WHOLE] * 2, name="clip"
    )(result, curvature)
    return (factor_out[None, None], inverse_out[None, None], update)


def solution(mesh):
    return jax.shard_map(
        local,
        mesh=mesh,
        in_specs=(
            P("dp", None),
            P("dp", "mp"),
            P("dp"),
            P("mp", "dp", None, None, None),
            P("mp", "dp", None, None, None),
            P(),
            P(),
        ),
        out_specs=(P("mp", "dp", None, None), P("mp", "dp", None, None), P("dp", "mp")),
        check_vma=False,
    )
```

```python
import functools

import jax
import jax.numpy as jnp
from jax import lax
from jax.experimental import pallas as pl
from jax.experimental.pallas import tpu as pltpu
from jax.sharding import PartitionSpec as P

DECAY = 0.9
DAMPING = 0.01
TILE = 128
ROWS = 16
VMEM_BYTES = 48 * 1024 * 1024
BF16 = jnp.bfloat16
F32 = jnp.float32
PARAMS = pltpu.CompilerParams(vmem_limit_bytes=VMEM_BYTES)
SCALARS = pl.BlockSpec(memory_space=pltpu.SMEM)
WHOLE = pl.BlockSpec(memory_space=pltpu.VMEM)
ANYWHERE = pl.BlockSpec(memory_space=pltpu.HBM)


def upper_pairs(tiles):
    return [(a, b) for a in range(tiles) for b in range(a, tiles)]


def diagonal_mask():
    rows = lax.broadcasted_iota(jnp.int32, (TILE, TILE), 0)
    return rows == lax.broadcasted_iota(jnp.int32, (TILE, TILE), 1)


def tile_of(a, b):
    return (slice(a * TILE, (a + 1) * TILE), slice(b * TILE, (b + 1) * TILE))


def clip(entries, result, partials, update):
    curvature = jnp.sum(partials[...], axis=0)[:1, :1]
    scale = jnp.minimum(1.0, jnp.sqrt(entries / jnp.abs(curvature)))
    update[...] = scale * result[...]


class Facts:
    def __init__(self, old_owner=None, new_owner=None):
        member = lax.axis_index("dp")
        self.column = lax.axis_index("mp")
        chips = lax.axis_size("dp") // 2
        self.core = member & 1
        self.plane = jnp.where(member >= chips, 1, 0)
        self.place = member & (lax.axis_size("dp") // lax.axis_size("mp") - 1)
        self.flip = jnp.where(self.column >= lax.axis_size("mp") // 2, 1, 0)
        self.own_kind = self.plane ^ self.flip
        if old_owner is not None:
            owners = [old_owner[self.column, kind] for kind in range(2)]
            self.shared = jnp.where(owners[0] == owners[1], 1, 0)
            self.same_core = [jnp.where((o & 1) == self.core, 1, 0) for o in owners]
            self.same_plane = [
                jnp.where(jnp.where(o >= chips, 1, 0) == self.plane, 1, 0) for o in owners
            ]
            self.ring_at = [lax.shift_right_logical(o & (chips - 1), 1) for o in owners]
        if new_owner is not None:
            self.keeps = [
                jnp.where(new_owner[self.column, kind] == member, 1, 0) for kind in range(2)
            ]


def first_parts(
    owners, counts, features, out_grads, factors, inverses,
    keep, send, turned,
    own, grads, kept, held, packed, diag, arrived,
):
    facts = Facts(owners)
    core, flip, count = facts.core, facts.flip, counts[0]
    rows, width = own.shape
    tiles = width // TILE
    on_diagonal = diagonal_mask()
    start = pl.multiple_of(facts.column * width, width)
    loads = [
        pltpu.make_async_copy(features.at[:, pl.ds(start, width)], own, arrived.at[0]),
        pltpu.make_async_copy(out_grads, grads, arrived.at[1]),
    ] + [
        pltpu.make_async_copy(
            source.at[facts.shared if kind else 0],
            held.at[which * 2 + kind],
            arrived.at[2 + which * 2 + kind],
        )
        for which, source in enumerate((factors, inverses))
        for kind in range(2)
    ]
    for load in loads:
        load.start()
    valid = lax.broadcasted_iota(jnp.int32, (rows, width), 0) < count
    for kind, (block, left) in enumerate(((own, kept), (grads, turned))):
        loads[kind].wait()
        left[...] = jnp.where(valid, block[...].astype(F32), 0.0).T.astype(BF16)
        for a, b in upper_pairs(tiles // 2):
            square = jnp.dot(
                left[2 * a * TILE : 2 * (a + 1) * TILE, :],
                block[:, 2 * b * TILE : 2 * (b + 1) * TILE],
                preferred_element_type=F32,
            ).astype(BF16)
            for i in range(2):
                for j in range(2):
                    if 2 * a + i <= 2 * b + j:
                        at = upper_pairs(tiles).index((2 * a + i, 2 * b + j))
                        packed[kind, 2, at * TILE : (at + 1) * TILE, :] = square[tile_of(i, j)]
    for which in range(2):
        for kind in range(2):
            loads[2 + which * 2 + kind].wait()
            for n, (a, b) in enumerate(upper_pairs(tiles)):
                piece = held[(which * 2 + kind,) + tile_of(a, b)]
                if a == b:
                    row = (which * 2 + kind) * tiles + a
                    diag[row : row + 1, :] = jnp.sum(
                        jnp.where(on_diagonal, piece, 0.0), axis=0, keepdims=True
                    )
                    piece = jnp.where(on_diagonal, 0.0, piece)
                packed[kind, which, n * TILE : (n + 1) * TILE, :] = piece.astype(BF16)
    high = diag[...].astype(BF16)
    low = (diag[...] - high.astype(F32)).astype(BF16)
    words = jnp.concatenate([high, low], axis=0)
    quarter = lax.broadcasted_iota(jnp.int32, (ROWS, TILE), 0) // 4
    digits = lax.shift_right_logical(jnp.full((ROWS, TILE), count), 3 * quarter) & 7
    digits = digits.astype(F32).astype(BF16)
    chips = keep.shape[0]
    share = (keep.shape[1] - words.shape[0] - ROWS) // 3
    sums = 2 * share + words.shape[0]
    for q in range(chips):
        plane, pair = divmod(q, chips // 2)
        kind = flip if plane == 0 else 1 - flip
        for ref, parity in ((keep, core), (send, 1 - core)):
            start = pl.multiple_of((2 * pair + parity) * share, ROWS)
            for which, at in enumerate((0, share, sums)):
                ref[q, at : at + share, :] = packed[kind, which, pl.ds(start, share), :]
            ref[q, 2 * share : sums, :] = words
            ref[q, sums + share :, :] = digits


def merge_words(first_flag, second_flag, one, two):
    lanes = one.shape[0] // 8
    kinds = (lax.broadcasted_iota(jnp.int32, one.shape, 0) // lanes) % 2
    flags = jnp.where(kinds == 0, first_flag, second_flag)
    return jnp.where(flags == 1, one.astype(F32), two.astype(F32))


def choose_core(owners, keep, received, unread, near_old, near_sum, far):
    facts = Facts(owners)
    first, second = facts.same_core
    ring, rows = near_old.shape[0], near_old.shape[1]
    data = rows // 6 * 5
    words = merge_words(first, second, keep[0, data:rows, :], received[0, data:rows, :]).astype(BF16)
    for old, at, kind in (
        (near_old, facts.plane, facts.own_kind),
        (far, 1 - facts.plane, 1 - facts.own_kind),
    ):
        flag = jnp.where(kind == 0, first, second)

        @pl.when(flag == 1)
        def _():
            old[:, :data, :] = keep[pl.ds(at * ring, ring), :data, :]

        @pl.when(flag == 0)
        def _():
            old[:, :data, :] = received[pl.ds(at * ring, ring), :data, :]

        for z in range(ring):
            old[z, data:rows, :] = words
        chips = pl.ds(at * ring, ring)
        total = keep[chips, rows:, :].astype(F32) + received[chips, rows:, :].astype(F32)
        if old is far:
            far[:, rows:, :] = total.astype(BF16)
        else:
            near_sum[...] = total


def join_planes(owners, near_old, near_sum, arrived, unread, other_unread, out):
    facts = Facts(owners)
    first, second = facts.same_plane
    flag = jnp.where(facts.own_kind == 0, first, second)
    ring, rows = near_old.shape[0], near_old.shape[1]
    data = rows // 6 * 5

    @pl.when(flag == 1)
    def _():
        out[:, :data, :] = near_old[:, :data, :]

    @pl.when(flag == 0)
    def _():
        out[:, :data, :] = arrived[:, :data, :]

    words = merge_words(first, second, near_old[0, data:, :], arrived[0, data:rows, :]).astype(BF16)
    for z in range(ring):
        out[z, data:rows, :] = words
    out[:, rows:, :] = (near_sum[...] + arrived[:, rows:, :].astype(F32)).astype(BF16)


def make_shares(owners, arrived, shares, diag):
    facts = Facts(owners)
    own_kind = facts.own_kind
    first, second = facts.ring_at
    ring, rows = shares.shape[0], shares.shape[1]
    share = rows // 2
    words = rows // 5 + rows
    owner = jnp.where(own_kind == 0, first, second)
    both = merge_words(1, 0, arrived[first, rows:words, :], arrived[second, rows:words, :])
    diag[...] = both[: diag.shape[0]] + both[diag.shape[0] :]
    summed = sum(arrived[z, words:, :].astype(F32) for z in range(ring))
    total = sum(summed[share + 4 * d : share + 4 * d + 1, :] * float(8**d) for d in range(4))
    factor = DECAY * arrived[owner, :share, :].astype(F32) + (1.0 - DECAY) * summed[:share] / total
    factor = factor.astype(BF16)
    inverse = arrived[owner, share:rows, :]
    for z in range(ring):
        shares[z, :share, :] = factor
        shares[z, share:, :] = inverse


def gradient_tiles(turned, tiles):
    block = jnp.concatenate([tile[...] for tile in tiles], axis=1)
    return jnp.dot(turned[...], block, preferred_element_type=F32)


def gradient_send(scalars, turned, *refs):
    product = gradient_tiles(turned, refs[:4])
    for n in range(4):
        refs[-1][n] = product[:, n * TILE : (n + 1) * TILE].astype(BF16)


def gradient_add(scalars, turned, *refs):
    received, out = refs[4], refs[-1]
    product = gradient_tiles(turned, refs[:4])
    for n in range(4):
        total = product[:, n * TILE : (n + 1) * TILE] + received[n].astype(F32)
        out[n] = total.astype(out.dtype)


def unpack(mine, other, core, packed):
    share = mine.shape[1] // 2
    for pair in range(mine.shape[0]):
        for ref, parity in ((mine, core), (other, 1 - core)):
            start = pl.multiple_of((2 * pair + parity) * share, ROWS)
            for which in range(2):
                packed[which, pl.ds(start, share), :] = ref[
                    pair, which * share : (which + 1) * share, :
                ]


def spread(packed, which, diag, row, scale, high, low):
    tiles = high.shape[0] // TILE
    on_diagonal = diagonal_mask()
    for n, (a, b) in enumerate(upper_pairs(tiles)):
        piece = packed[which, n * TILE : (n + 1) * TILE, :].astype(F32)
        if a == b:
            exact = piece + jnp.where(on_diagonal, scale * diag[row + a : row + a + 1, :], 0.0)
            rounded = exact.astype(BF16)
            high[tile_of(a, a)] = rounded
            rest = jnp.sum(exact - rounded.astype(F32), axis=1, keepdims=True)
            low[a * TILE : (a + 1) * TILE, :] = jnp.broadcast_to(rest, (TILE, TILE))
        else:
            high[tile_of(a, b)] = packed[which, n * TILE : (n + 1) * TILE, :]
            high[tile_of(b, a)] = piece.T.astype(BF16)


def fill_blocks(kind, packed, diag, factor, factor_low, inverse, inverse_low):
    tiles = factor.shape[0] // TILE
    spread(packed, 0, diag, kind * tiles, DECAY, factor, factor_low)
    spread(packed, 1, diag, (2 + kind) * tiles, 1.0, inverse, inverse_low)


def times(high, low, right):
    width = right.shape[1]
    first = right.astype(BF16)
    second = (right - first.astype(F32)).astype(BF16)
    both = jnp.dot(high[...], jnp.concatenate([first, second], axis=1), preferred_element_type=F32)
    return both[:, :width] + both[:, width:] + low * right


def refine(factor, factor_low, inverse, inverse_low, part):
    inner = times(factor, factor_low[:, :1] + DAMPING, part)
    return 2.0 * part - times(inverse, inverse_low[:, :1], inner)


def exact_block(high, low):
    rows = lax.broadcasted_iota(jnp.int32, high.shape, 0)
    columns = lax.broadcasted_iota(jnp.int32, high.shape, 1)
    return high[...].astype(F32) + jnp.where(rows == columns, low[:, :1], 0.0)


def left_columns(mine, other, diag, left, packed, factor, factor_low, inverse, inverse_low):
    facts = Facts()
    core, place = facts.core, facts.place
    unpack(mine, other, core, packed)
    fill_blocks(0, packed, diag, factor, factor_low, inverse, inverse_low)
    start = pl.multiple_of(place * TILE, TILE)
    part = inverse[:, pl.ds(start, TILE)].astype(F32)
    rows = lax.broadcasted_iota(jnp.int32, part.shape, 0) - start
    part = part + jnp.where(
        rows == lax.broadcasted_iota(jnp.int32, part.shape, 1), inverse_low[...], 0.0
    )
    left[...] = refine(factor, factor_low, inverse, inverse_low, part).astype(BF16)


def new_blocks(
    owners, mine, other, far_mine, far_other, diag, right, factor_out, inverse_out,
    packed, factor, factor_low, inverse, inverse_low,
):
    facts = Facts(new_owner=owners)
    core, own_kind = facts.core, facts.own_kind
    first, second = facts.keeps
    blocks = (factor, factor_low, inverse, inverse_low)

    def load_blocks(kind):
        @pl.when(own_kind == kind)
        def _():
            unpack(mine, other, core, packed)

        @pl.when(own_kind != kind)
        def _():
            unpack(far_mine, far_other, core, packed)

        fill_blocks(kind, packed, diag, *blocks)

    load_blocks(1)
    fresh = refine(*blocks, exact_block(inverse, inverse_low))
    right[...] = fresh.astype(BF16)

    @pl.when(second == 1)
    def _():
        factor_out[...] = exact_block(factor, factor_low)
        inverse_out[...] = fresh

    @pl.when(second == 0)
    def _():
        factor_out[...] = jnp.zeros_like(factor_out)
        inverse_out[...] = jnp.zeros_like(inverse_out)

    @pl.when(first == 1)
    def _():
        load_blocks(0)
        factor_out[...] = exact_block(factor, factor_low)
        inverse_out[...] = refine(*blocks, exact_block(inverse, inverse_low))


def precondition(grad, left, right, result, curvature):
    own = Facts().place
    half = sum(
        jnp.dot(grad[p], left[p * TILE : (p + 1) * TILE, :], preferred_element_type=F32)
        for p in range(grad.shape[0])
    )
    product = jnp.dot(half.T.astype(BF16), right[...], preferred_element_type=F32)
    result[...] = product
    curvature[...] = jnp.full(curvature.shape, jnp.sum(product * grad[own].astype(F32).T))


def kernel_call(body, out_shape, in_specs, scratch=(), out_specs=None, aliases=None, flops=0, moved=0, name=None):
    if out_specs is None:
        out_specs = (WHOLE,) * len(out_shape) if isinstance(out_shape, tuple) else WHOLE
    return pl.pallas_call(
        body,
        out_shape=out_shape,
        in_specs=in_specs,
        out_specs=out_specs,
        input_output_aliases=aliases or {},
        scratch_shapes=list(scratch),
        compiler_params=PARAMS,
        cost_estimate=pl.CostEstimate(flops=flops, bytes_accessed=moved, transcendentals=0),
        name=name or body.__name__,
    )


def local(features, out_grads, counts, factor_old, inverse_old, old_owner, new_owner):
    tok_rows, width = out_grads.shape
    feature_count = features.shape[1]
    column = lax.axis_index("mp")
    member = lax.axis_index("dp")
    members = lax.axis_size("dp")
    columns = lax.axis_size("mp")
    chips = members // 2
    ring = chips // 2
    core = member & 1
    core_swap = [(i, i ^ 1) for i in range(members)]
    plane_swap = [(i, (i + chips) % members) for i in range(members)]
    rings = [[y * chips + 2 * z + c for z in range(ring)] for y in range(2) for c in range(2)]
    packed_rows = width * (width + TILE) // 2 // TILE
    share = 2 * packed_rows // members
    lanes = width // TILE
    holders = members // columns
    shape = jax.ShapeDtypeStruct
    megabyte = 2 * width * width * 2

    def across_ring(parts):
        return lax.all_to_all(parts, "dp", 0, 0, tiled=True, axis_index_groups=rings)

    def swap_cores(send):
        return lax.ppermute(send, "dp", core_swap)

    def swap_planes(send):
        return lax.ppermute(send, "dp", plane_swap)

    message = shape((chips, 3 * share + 8 * lanes + ROWS, TILE), BF16)
    keep, send, turned = kernel_call(
        first_parts,
        (message, message, shape((width, tok_rows), BF16)),
        [SCALARS, SCALARS] + [ANYWHERE] * 4,
        [
            pltpu.VMEM((tok_rows, width), BF16),
            pltpu.VMEM((tok_rows, width), BF16),
            pltpu.VMEM((width, tok_rows), BF16),
            pltpu.VMEM((4, width, width), F32),
            pltpu.VMEM((2, 3, packed_rows, TILE), BF16),
            pltpu.VMEM((4 * lanes, TILE), F32),
            pltpu.SemaphoreType.DMA((6,)),
        ],
        flops=4 * tok_rows * width * width,
        moved=10 * megabyte,
    )(old_owner, counts, features, out_grads, factor_old[0, 0], inverse_old[0, 0])
    old_rows = 2 * share + 8 * lanes
    far_shape = shape((ring,) + message.shape[1:], BF16)
    def gradient(body, parity, which, dtype, name, other):
        def chip_at(i, s):
            return s[1] * ring + 4 * i

        def tile_spec(n):
            return pl.BlockSpec((tok_rows, TILE), lambda i, s: (0, 2 * (chip_at(i, s) + n) + s[0]))

        four_chips = pl.BlockSpec((4, width, TILE), lambda i, s: (i, 0, 0))
        return pl.pallas_call(
            body,
            out_shape=shape((ring, width, TILE), dtype),
            grid_spec=pltpu.PrefetchScalarGridSpec(
                num_scalar_prefetch=1,
                grid=(ring // 4,),
                in_specs=[pl.BlockSpec((width, tok_rows), lambda i, s: (0, 0))]
                + [tile_spec(n) for n in range(4)]
                + [four_chips if body is gradient_add else ANYWHERE],
                out_specs=four_chips,
            ),
            compiler_params=PARAMS,
            cost_estimate=pl.CostEstimate(
                flops=2 * ring * tok_rows * width * TILE,
                bytes_accessed=ring * megabyte // 2,
                transcendentals=0,
            ),
            name=name,
        )(jnp.stack([parity, which]), turned, features, features, features, features, other)

    plane = jnp.where(member >= chips, 1, 0)
    send_far = gradient(gradient_send, 1 - core, 1 - plane, BF16, "send_far", counts)
    received_far = swap_cores(send_far)
    near_old, near_sum, far = kernel_call(
        choose_core,
        (shape((ring, old_rows, TILE), BF16), shape((ring, share + ROWS, TILE), F32), far_shape),
        [SCALARS, WHOLE, WHOLE, ANYWHERE],
        moved=2 * megabyte,
    )(old_owner, keep, swap_cores(send), send_far)
    arrived = swap_planes(far)

    send_near = gradient(gradient_send, 1 - core, plane, BF16, "send_near", far)
    far_grad = gradient(gradient_add, core, 1 - plane, BF16, "gradient_far", received_far)
    arrived_grad = swap_planes(far_grad)
    near_grad = gradient(
        gradient_add, core, plane, F32, "gradient_near", swap_cores(send_near)
    )
    joined = kernel_call(
        join_planes,
        far_shape,
        [SCALARS] + [WHOLE] * 3 + [ANYWHERE] * 2,
        moved=megabyte,
    )(old_owner, near_old, near_sum, arrived, far_grad, send_near)
    shares, diag = kernel_call(
        make_shares,
        (shape((ring, 2 * share, TILE), BF16), shape((4 * lanes, TILE), F32)),
        [SCALARS, WHOLE],
        moved=megabyte,
    )(old_owner, across_ring(joined))

    mine = across_ring(shares)
    other = swap_cores(mine)
    far_mine = swap_planes(mine)
    far_other = swap_cores(far_mine)
    unpacked = [
        pltpu.VMEM((2, packed_rows, TILE), BF16),
        pltpu.VMEM((width, width), BF16),
        pltpu.VMEM((width, TILE), F32),
        pltpu.VMEM((width, width), BF16),
        pltpu.VMEM((width, TILE), F32),
    ]
    left = kernel_call(
        left_columns,
        shape((width, TILE), BF16),
        [WHOLE] * 3,
        unpacked,
        flops=8 * width * width * TILE,
        moved=2 * megabyte,
    )(mine, other, diag)
    gates = [(i, i // holders) for i in range(members)]
    near = lax.ppermute(
        left, ("dp", "mp"), [(i * columns + g, i * columns + (g ^ 1)) for i, g in gates]
    )
    gate = lax.shift_right_logical(member, holders.bit_length() - 1)
    left = jnp.where(column == gate, left, near)
    left = jnp.where(
        (column ^ gate) <= 1,
        left,
        sum(
            lax.ppermute(
                left,
                ("dp", "mp"),
                [
                    (i * columns + g, i * columns + (g + 2 * step) % columns)
                    for i, at in gates
                    for g in (at, at ^ 1)
                ],
            )
            for step in range(1, columns // 2)
        ),
    )
    square = shape((width, width), F32)
    right, factor_out, inverse_out = kernel_call(
        new_blocks,
        (shape((width, width), BF16), square, square),
        [SCALARS] + [WHOLE] * 5,
        unpacked,
        flops=8 * width * width * width,
        moved=6 * megabyte,
    )(new_owner, mine, other, far_mine, far_other, diag)

    grad = across_ring((near_grad + arrived_grad.astype(F32)).astype(BF16))
    grad = jnp.sum(grad.astype(F32), axis=0).astype(BF16)
    neighbours = [[holders * c + r for r in range(holders)] for c in range(columns)]
    grads = lax.all_gather(grad, "dp", axis=0, axis_index_groups=neighbours)
    result, curvature = kernel_call(
        precondition,
        (shape((TILE, width), F32), shape((8, TILE), F32)),
        [WHOLE] * 3,
        flops=4 * width * width * TILE,
        moved=megabyte,
    )(grads, left, right)

    planes = [[y * chips + i for i in range(chips)] for y in range(2)]
    curvature = lax.all_to_all(
        jnp.broadcast_to(curvature, (chips, 8, TILE)),
        "dp", 0, 0, tiled=True, axis_index_groups=planes,
    )
    curvature = jnp.sum(curvature, axis=0)
    rings = [
        [(y * chips + i) * columns + c for y in range(2) for c in range(columns)] for i in range(chips)
    ]
    curvature = lax.all_to_all(
        jnp.broadcast_to(curvature, (2 * columns, 8, TILE)),
        ("dp", "mp"), 0, 0, tiled=True, axis_index_groups=rings,
    )
    entries = float(feature_count * width * columns)
    update = kernel_call(
        functools.partial(clip, entries), shape((TILE, width), F32), [WHOLE] * 2, name="clip"
    )(result, curvature)
    return (factor_out[None, None], inverse_out[None, None], update)


def solution(mesh):
    return jax.shard_map(
        local,
        mesh=mesh,
        in_specs=(
            P("dp", None),
            P("dp", "mp"),
            P("dp"),
            P("mp", "dp", None, None, None),
            P("mp", "dp", None, None, None),
            P(),
            P(),
        ),
        out_specs=(P("mp", "dp", None, None), P("mp", "dp", None, None), P("dp", "mp")),
        check_vma=False,
    )
```

```python
import functools

import jax
import jax.numpy as jnp
from jax import lax
from jax.experimental import pallas as pl
from jax.experimental.pallas import tpu as pltpu
from jax.sharding import PartitionSpec as P

DECAY = 0.9
DAMPING = 0.01
TILE = 128
ROWS = 16
VMEM_BYTES = 48 * 1024 * 1024
BF16 = jnp.bfloat16
F32 = jnp.float32
PARAMS = pltpu.CompilerParams(vmem_limit_bytes=VMEM_BYTES)
SCALARS = pl.BlockSpec(memory_space=pltpu.SMEM)
WHOLE = pl.BlockSpec(memory_space=pltpu.VMEM)
ANYWHERE = pl.BlockSpec(memory_space=pltpu.HBM)


def upper_pairs(tiles):
    return [(a, b) for a in range(tiles) for b in range(a, tiles)]


def diagonal_mask():
    rows = lax.broadcasted_iota(jnp.int32, (TILE, TILE), 0)
    return rows == lax.broadcasted_iota(jnp.int32, (TILE, TILE), 1)


def tile_of(a, b):
    return (slice(a * TILE, (a + 1) * TILE), slice(b * TILE, (b + 1) * TILE))


def clip(entries, result, partials, update):
    curvature = jnp.sum(partials[...], axis=0)[:1, :1]
    scale = jnp.minimum(1.0, jnp.sqrt(entries / jnp.abs(curvature)))
    update[...] = scale * result[...]


class Facts:
    def __init__(self, old_owner=None, new_owner=None):
        member = lax.axis_index("dp")
        self.column = lax.axis_index("mp")
        chips = lax.axis_size("dp") // 2
        self.core = member & 1
        self.plane = jnp.where(member >= chips, 1, 0)
        self.place = member & (lax.axis_size("dp") // lax.axis_size("mp") - 1)
        self.flip = jnp.where(self.column >= lax.axis_size("mp") // 2, 1, 0)
        self.own_kind = self.plane ^ self.flip
        if old_owner is not None:
            owners = [old_owner[self.column, kind] for kind in range(2)]
            self.shared = jnp.where(owners[0] == owners[1], 1, 0)
            self.same_core = [jnp.where((o & 1) == self.core, 1, 0) for o in owners]
            self.same_plane = [
                jnp.where(jnp.where(o >= chips, 1, 0) == self.plane, 1, 0) for o in owners
            ]
            self.ring_at = [lax.shift_right_logical(o & (chips - 1), 1) for o in owners]
        if new_owner is not None:
            self.keeps = [
                jnp.where(new_owner[self.column, kind] == member, 1, 0) for kind in range(2)
            ]


def first_parts(
    owners, counts, features, out_grads, factors, inverses,
    keep, send, turned,
    own, grads, kept, held, packed, diag, arrived,
):
    facts = Facts(owners)
    core, flip, count = facts.core, facts.flip, counts[0]
    rows, width = own.shape
    tiles = width // TILE
    on_diagonal = diagonal_mask()
    start = pl.multiple_of(facts.column * width, width)
    loads = [
        pltpu.make_async_copy(features.at[:, pl.ds(start, width)], own, arrived.at[0]),
        pltpu.make_async_copy(out_grads, grads, arrived.at[1]),
    ] + [
        pltpu.make_async_copy(
            source.at[facts.shared if kind else 0],
            held.at[which * 2 + kind],
            arrived.at[2 + which * 2 + kind],
        )
        for which, source in enumerate((factors, inverses))
        for kind in range(2)
    ]
    for load in loads:
        load.start()
    valid = lax.broadcasted_iota(jnp.int32, (rows, width), 0) < count
    for kind, (block, left) in enumerate(((own, kept), (grads, turned))):
        loads[kind].wait()
        left[...] = jnp.where(valid, block[...].astype(F32), 0.0).T.astype(BF16)
        for a, b in upper_pairs(tiles // 2):
            square = jnp.dot(
                left[2 * a * TILE : 2 * (a + 1) * TILE, :],
                block[:, 2 * b * TILE : 2 * (b + 1) * TILE],
                preferred_element_type=F32,
            ).astype(BF16)
            for i in range(2):
                for j in range(2):
                    if 2 * a + i <= 2 * b + j:
                        at = upper_pairs(tiles).index((2 * a + i, 2 * b + j))
                        packed[kind, 2, at * TILE : (at + 1) * TILE, :] = square[tile_of(i, j)]
    for which in range(2):
        for kind in range(2):
            loads[2 + which * 2 + kind].wait()
            for n, (a, b) in enumerate(upper_pairs(tiles)):
                piece = held[(which * 2 + kind,) + tile_of(a, b)]
                if a == b:
                    row = (which * 2 + kind) * tiles + a
                    diag[row : row + 1, :] = jnp.sum(
                        jnp.where(on_diagonal, piece, 0.0), axis=0, keepdims=True
                    )
                    piece = jnp.where(on_diagonal, 0.0, piece)
                packed[kind, which, n * TILE : (n + 1) * TILE, :] = piece.astype(BF16)
    high = diag[...].astype(BF16)
    low = (diag[...] - high.astype(F32)).astype(BF16)
    words = jnp.concatenate([high, low], axis=0)
    quarter = lax.broadcasted_iota(jnp.int32, (ROWS, TILE), 0) // 4
    digits = lax.shift_right_logical(jnp.full((ROWS, TILE), count), 3 * quarter) & 7
    digits = digits.astype(F32).astype(BF16)
    chips = keep.shape[0]
    share = (keep.shape[1] - words.shape[0] - ROWS) // 3
    sums = 2 * share + words.shape[0]
    for q in range(chips):
        plane, pair = divmod(q, chips // 2)
        kind = flip if plane == 0 else 1 - flip
        for ref, parity in ((keep, core), (send, 1 - core)):
            start = pl.multiple_of((2 * pair + parity) * share, ROWS)
            for which, at in enumerate((0, share, sums)):
                ref[q, at : at + share, :] = packed[kind, which, pl.ds(start, share), :]
            ref[q, 2 * share : sums, :] = words
            ref[q, sums + share :, :] = digits


def merge_words(first_flag, second_flag, one, two):
    lanes = one.shape[0] // 8
    kinds = (lax.broadcasted_iota(jnp.int32, one.shape, 0) // lanes) % 2
    flags = jnp.where(kinds == 0, first_flag, second_flag)
    return jnp.where(flags == 1, one.astype(F32), two.astype(F32))


def choose_core(owners, keep, received, unread, near_old, near_sum, far):
    facts = Facts(owners)
    first, second = facts.same_core
    ring, rows = near_old.shape[0], near_old.shape[1]
    data = rows // 6 * 5
    words = merge_words(first, second, keep[0, data:rows, :], received[0, data:rows, :]).astype(BF16)
    for old, at, kind in (
        (near_old, facts.plane, facts.own_kind),
        (far, 1 - facts.plane, 1 - facts.own_kind),
    ):
        flag = jnp.where(kind == 0, first, second)

        @pl.when(flag == 1)
        def _():
            old[:, :data, :] = keep[pl.ds(at * ring, ring), :data, :]

        @pl.when(flag == 0)
        def _():
            old[:, :data, :] = received[pl.ds(at * ring, ring), :data, :]

        for z in range(ring):
            old[z, data:rows, :] = words
        chips = pl.ds(at * ring, ring)
        total = keep[chips, rows:, :].astype(F32) + received[chips, rows:, :].astype(F32)
        if old is far:
            far[:, rows:, :] = total.astype(BF16)
        else:
            near_sum[...] = total


def join_planes(owners, near_old, near_sum, arrived, *refs):
    out = refs[-1]
    facts = Facts(owners)
    first, second = facts.same_plane
    flag = jnp.where(facts.own_kind == 0, first, second)
    ring, rows = near_old.shape[0], near_old.shape[1]
    data = rows // 6 * 5

    @pl.when(flag == 1)
    def _():
        out[:, :data, :] = near_old[:, :data, :]

    @pl.when(flag == 0)
    def _():
        out[:, :data, :] = arrived[:, :data, :]

    words = merge_words(first, second, near_old[0, data:, :], arrived[0, data:rows, :]).astype(BF16)
    for z in range(ring):
        out[z, data:rows, :] = words
    out[:, rows:, :] = (near_sum[...] + arrived[:, rows:, :].astype(F32)).astype(BF16)


def make_shares(owners, arrived, shares, diag):
    facts = Facts(owners)
    own_kind = facts.own_kind
    first, second = facts.ring_at
    ring, rows = shares.shape[0], shares.shape[1]
    share = rows // 2
    words = rows // 5 + rows
    owner = jnp.where(own_kind == 0, first, second)
    both = merge_words(1, 0, arrived[first, rows:words, :], arrived[second, rows:words, :])
    diag[...] = both[: diag.shape[0]] + both[diag.shape[0] :]
    summed = sum(arrived[z, words:, :].astype(F32) for z in range(ring))
    total = sum(summed[share + 4 * d : share + 4 * d + 1, :] * float(8**d) for d in range(4))
    factor = DECAY * arrived[owner, :share, :].astype(F32) + (1.0 - DECAY) * summed[:share] / total
    factor = factor.astype(BF16)
    inverse = arrived[owner, share:rows, :]
    for z in range(ring):
        shares[z, :share, :] = factor
        shares[z, share:, :] = inverse


def gradient_tiles(turned, tiles):
    block = jnp.concatenate([tile[...] for tile in tiles], axis=1)
    return jnp.dot(turned[...], block, preferred_element_type=F32)


def gradient_send(scalars, turned, *refs):
    product = gradient_tiles(turned, refs[:4])
    for n in range(4):
        refs[-1][n] = product[:, n * TILE : (n + 1) * TILE].astype(BF16)


def gradient_add(scalars, turned, *refs):
    received, out = refs[4], refs[-1]
    product = gradient_tiles(turned, refs[:4])
    for n in range(4):
        total = product[:, n * TILE : (n + 1) * TILE] + received[n].astype(F32)
        out[n] = total.astype(out.dtype)


def unpack(mine, other, core, packed):
    share = mine.shape[1] // 2
    for pair in range(mine.shape[0]):
        for ref, parity in ((mine, core), (other, 1 - core)):
            start = pl.multiple_of((2 * pair + parity) * share, ROWS)
            for which in range(2):
                packed[which, pl.ds(start, share), :] = ref[
                    pair, which * share : (which + 1) * share, :
                ]


def spread(packed, which, diag, row, scale, high, low):
    tiles = high.shape[0] // TILE
    on_diagonal = diagonal_mask()
    for n, (a, b) in enumerate(upper_pairs(tiles)):
        piece = packed[which, n * TILE : (n + 1) * TILE, :].astype(F32)
        if a == b:
            exact = piece + jnp.where(on_diagonal, scale * diag[row + a : row + a + 1, :], 0.0)
            rounded = exact.astype(BF16)
            high[tile_of(a, a)] = rounded
            rest = jnp.sum(exact - rounded.astype(F32), axis=1, keepdims=True)
            low[a * TILE : (a + 1) * TILE, :] = jnp.broadcast_to(rest, (TILE, TILE))
        else:
            high[tile_of(a, b)] = packed[which, n * TILE : (n + 1) * TILE, :]
            high[tile_of(b, a)] = piece.T.astype(BF16)


def fill_blocks(kind, packed, diag, factor, factor_low, inverse, inverse_low):
    tiles = factor.shape[0] // TILE
    spread(packed, 0, diag, kind * tiles, DECAY, factor, factor_low)
    spread(packed, 1, diag, (2 + kind) * tiles, 1.0, inverse, inverse_low)


def times(high, low, right):
    width = right.shape[1]
    first = right.astype(BF16)
    second = (right - first.astype(F32)).astype(BF16)
    both = jnp.dot(high[...], jnp.concatenate([first, second], axis=1), preferred_element_type=F32)
    return both[:, :width] + both[:, width:] + low * right


def refine(factor, factor_low, inverse, inverse_low, part):
    inner = times(factor, factor_low[:, :1] + DAMPING, part)
    return 2.0 * part - times(inverse, inverse_low[:, :1], inner)


def exact_block(high, low):
    rows = lax.broadcasted_iota(jnp.int32, high.shape, 0)
    columns = lax.broadcasted_iota(jnp.int32, high.shape, 1)
    return high[...].astype(F32) + jnp.where(rows == columns, low[:, :1], 0.0)


def left_columns(mine, other, diag, left, packed, factor, factor_low, inverse, inverse_low):
    facts = Facts()
    core, place = facts.core, facts.place
    unpack(mine, other, core, packed)
    fill_blocks(0, packed, diag, factor, factor_low, inverse, inverse_low)
    start = pl.multiple_of(place * TILE, TILE)
    part = inverse[:, pl.ds(start, TILE)].astype(F32)
    rows = lax.broadcasted_iota(jnp.int32, part.shape, 0) - start
    part = part + jnp.where(
        rows == lax.broadcasted_iota(jnp.int32, part.shape, 1), inverse_low[...], 0.0
    )
    left[...] = refine(factor, factor_low, inverse, inverse_low, part).astype(BF16)


def blank(unread, first, second, zeros, sent):
    zeros[...] = jnp.zeros_like(zeros)
    copies = [pltpu.make_async_copy(zeros, out, sent.at[n]) for n, out in enumerate((first, second))]
    for copy in copies:
        copy.start()
    for copy in copies:
        copy.wait()


def new_blocks(
    owners, mine, other, far_mine, far_other, diag, blank_factor, blank_inverse,
    right, factor_out, inverse_out,
    packed, factor, factor_low, inverse, inverse_low, new_factor, new_inverse, sent,
):
    facts = Facts(new_owner=owners)
    core, own_kind = facts.core, facts.own_kind
    first, second = facts.keeps
    blocks = (factor, factor_low, inverse, inverse_low)

    def load_blocks(kind):
        @pl.when(own_kind == kind)
        def _():
            unpack(mine, other, core, packed)

        @pl.when(own_kind != kind)
        def _():
            unpack(far_mine, far_other, core, packed)

        fill_blocks(kind, packed, diag, *blocks)

    load_blocks(1)
    fresh = refine(*blocks, exact_block(inverse, inverse_low))
    right[...] = fresh.astype(BF16)

    @pl.when(second == 1)
    def _():
        new_factor[...] = exact_block(factor, factor_low)
        new_inverse[...] = fresh

    @pl.when(first == 1)
    def _():
        load_blocks(0)
        new_factor[...] = exact_block(factor, factor_low)
        new_inverse[...] = refine(*blocks, exact_block(inverse, inverse_low))

    @pl.when(first + second > 0)
    def _():
        copies = [
            pltpu.make_async_copy(new_factor, factor_out, sent.at[0]),
            pltpu.make_async_copy(new_inverse, inverse_out, sent.at[1]),
        ]
        for copy in copies:
            copy.start()
        for copy in copies:
            copy.wait()


def precondition(grad, left, right, result, curvature):
    own = Facts().place
    half = sum(
        jnp.dot(grad[p], left[p * TILE : (p + 1) * TILE, :], preferred_element_type=F32)
        for p in range(grad.shape[0])
    )
    product = jnp.dot(half.T.astype(BF16), right[...], preferred_element_type=F32)
    result[...] = product
    curvature[...] = jnp.full(curvature.shape, jnp.sum(product * grad[own].astype(F32).T))


def kernel_call(body, out_shape, in_specs, scratch=(), out_specs=None, aliases=None, flops=0, moved=0, name=None):
    if out_specs is None:
        out_specs = (WHOLE,) * len(out_shape) if isinstance(out_shape, tuple) else WHOLE
    return pl.pallas_call(
        body,
        out_shape=out_shape,
        in_specs=in_specs,
        out_specs=out_specs,
        input_output_aliases=aliases or {},
        scratch_shapes=list(scratch),
        compiler_params=PARAMS,
        cost_estimate=pl.CostEstimate(flops=flops, bytes_accessed=moved, transcendentals=0),
        name=name or body.__name__,
    )


def local(features, out_grads, counts, factor_old, inverse_old, old_owner, new_owner):
    tok_rows, width = out_grads.shape
    feature_count = features.shape[1]
    column = lax.axis_index("mp")
    member = lax.axis_index("dp")
    members = lax.axis_size("dp")
    columns = lax.axis_size("mp")
    chips = members // 2
    ring = chips // 2
    core = member & 1
    core_swap = [(i, i ^ 1) for i in range(members)]
    plane_swap = [(i, (i + chips) % members) for i in range(members)]
    rings = [[y * chips + 2 * z + c for z in range(ring)] for y in range(2) for c in range(2)]
    packed_rows = width * (width + TILE) // 2 // TILE
    share = 2 * packed_rows // members
    lanes = width // TILE
    holders = members // columns
    shape = jax.ShapeDtypeStruct
    megabyte = 2 * width * width * 2

    def across_ring(parts):
        return lax.all_to_all(parts, "dp", 0, 0, tiled=True, axis_index_groups=rings)

    def swap_cores(send):
        return lax.ppermute(send, "dp", core_swap)

    def swap_planes(send):
        return lax.ppermute(send, "dp", plane_swap)

    message = shape((chips, 3 * share + 8 * lanes + ROWS, TILE), BF16)
    keep, send, turned = kernel_call(
        first_parts,
        (message, message, shape((width, tok_rows), BF16)),
        [SCALARS, SCALARS] + [ANYWHERE] * 4,
        [
            pltpu.VMEM((tok_rows, width), BF16),
            pltpu.VMEM((tok_rows, width), BF16),
            pltpu.VMEM((width, tok_rows), BF16),
            pltpu.VMEM((4, width, width), F32),
            pltpu.VMEM((2, 3, packed_rows, TILE), BF16),
            pltpu.VMEM((4 * lanes, TILE), F32),
            pltpu.SemaphoreType.DMA((6,)),
        ],
        flops=4 * tok_rows * width * width,
        moved=10 * megabyte,
    )(old_owner, counts, features, out_grads, factor_old[0, 0], inverse_old[0, 0])
    old_rows = 2 * share + 8 * lanes
    far_shape = shape((ring,) + message.shape[1:], BF16)
    def gradient(body, parity, which, dtype, name, other):
        def chip_at(i, s):
            return s[1] * ring + 4 * i

        def tile_spec(n):
            return pl.BlockSpec((tok_rows, TILE), lambda i, s: (0, 2 * (chip_at(i, s) + n) + s[0]))

        four_chips = pl.BlockSpec((4, width, TILE), lambda i, s: (i, 0, 0))
        return pl.pallas_call(
            body,
            out_shape=shape((ring, width, TILE), dtype),
            grid_spec=pltpu.PrefetchScalarGridSpec(
                num_scalar_prefetch=1,
                grid=(ring // 4,),
                in_specs=[pl.BlockSpec((width, tok_rows), lambda i, s: (0, 0))]
                + [tile_spec(n) for n in range(4)]
                + [four_chips if body is gradient_add else ANYWHERE],
                out_specs=four_chips,
            ),
            compiler_params=PARAMS,
            cost_estimate=pl.CostEstimate(
                flops=2 * ring * tok_rows * width * TILE,
                bytes_accessed=ring * megabyte // 2,
                transcendentals=0,
            ),
            name=name,
        )(jnp.stack([parity, which]), turned, features, features, features, features, other)

    plane = jnp.where(member >= chips, 1, 0)
    send_far = gradient(gradient_send, 1 - core, 1 - plane, BF16, "send_far", counts)
    received_far = swap_cores(send_far)
    near_old, near_sum, far = kernel_call(
        choose_core,
        (shape((ring, old_rows, TILE), BF16), shape((ring, share + ROWS, TILE), F32), far_shape),
        [SCALARS, WHOLE, WHOLE, ANYWHERE],
        moved=2 * megabyte,
    )(old_owner, keep, swap_cores(send), send_far)
    arrived = swap_planes(far)

    send_near = gradient(gradient_send, 1 - core, plane, BF16, "send_near", far)
    far_grad = gradient(gradient_add, core, 1 - plane, BF16, "gradient_far", received_far)
    arrived_grad = swap_planes(far_grad)
    near_grad = gradient(
        gradient_add, core, plane, F32, "gradient_near", swap_cores(send_near)
    )
    square = shape((width, width), F32)
    blanks = kernel_call(
        blank,
        (square, square),
        [ANYWHERE],
        [pltpu.VMEM((width, width), F32), pltpu.SemaphoreType.DMA((2,))],
        out_specs=(ANYWHERE, ANYWHERE),
        moved=2 * megabyte,
    )(far)
    joined = kernel_call(
        join_planes,
        far_shape,
        [SCALARS] + [WHOLE] * 3 + [ANYWHERE] * 4,
        moved=megabyte,
    )(old_owner, near_old, near_sum, arrived, far_grad, send_near, *blanks)
    shares, diag = kernel_call(
        make_shares,
        (shape((ring, 2 * share, TILE), BF16), shape((4 * lanes, TILE), F32)),
        [SCALARS, WHOLE],
        moved=megabyte,
    )(old_owner, across_ring(joined))

    mine = across_ring(shares)
    other = swap_cores(mine)
    far_mine = swap_planes(mine)
    far_other = swap_cores(far_mine)
    unpacked = [
        pltpu.VMEM((2, packed_rows, TILE), BF16),
        pltpu.VMEM((width, width), BF16),
        pltpu.VMEM((width, TILE), F32),
        pltpu.VMEM((width, width), BF16),
        pltpu.VMEM((width, TILE), F32),
    ]
    left = kernel_call(
        left_columns,
        shape((width, TILE), BF16),
        [WHOLE] * 3,
        unpacked,
        flops=8 * width * width * TILE,
        moved=2 * megabyte,
    )(mine, other, diag)
    gates = [(i, i // holders) for i in range(members)]
    near = lax.ppermute(
        left, ("dp", "mp"), [(i * columns + g, i * columns + (g ^ 1)) for i, g in gates]
    )
    gate = lax.shift_right_logical(member, holders.bit_length() - 1)
    left = jnp.where(column == gate, left, near)
    left = jnp.where(
        (column ^ gate) <= 1,
        left,
        sum(
            lax.ppermute(
                left,
                ("dp", "mp"),
                [
                    (i * columns + g, i * columns + (g + 2 * step) % columns)
                    for i, at in gates
                    for g in (at, at ^ 1)
                ],
            )
            for step in range(1, columns // 2)
        ),
    )
    right, factor_out, inverse_out = kernel_call(
        new_blocks,
        (shape((width, width), BF16), square, square),
        [SCALARS] + [WHOLE] * 5 + [ANYWHERE] * 2,
        unpacked
        + [pltpu.VMEM((width, width), F32)] * 2
        + [pltpu.SemaphoreType.DMA((2,))],
        out_specs=(WHOLE, ANYWHERE, ANYWHERE),
        aliases={6: 1, 7: 2},
        flops=8 * width * width * width,
        moved=6 * megabyte,
    )(new_owner, mine, other, far_mine, far_other, diag, *blanks)

    grad = across_ring((near_grad + arrived_grad.astype(F32)).astype(BF16))
    grad = jnp.sum(grad.astype(F32), axis=0).astype(BF16)
    neighbours = [[holders * c + r for r in range(holders)] for c in range(columns)]
    grads = lax.all_gather(grad, "dp", axis=0, axis_index_groups=neighbours)
    result, curvature = kernel_call(
        precondition,
        (shape((TILE, width), F32), shape((8, TILE), F32)),
        [WHOLE] * 3,
        flops=4 * width * width * TILE,
        moved=megabyte,
    )(grads, left, right)

    planes = [[y * chips + i for i in range(chips)] for y in range(2)]
    curvature = lax.all_to_all(
        jnp.broadcast_to(curvature, (chips, 8, TILE)),
        "dp", 0, 0, tiled=True, axis_index_groups=planes,
    )
    curvature = jnp.sum(curvature, axis=0)
    rings = [
        [(y * chips + i) * columns + c for y in range(2) for c in range(columns)] for i in range(chips)
    ]
    curvature = lax.all_to_all(
        jnp.broadcast_to(curvature, (2 * columns, 8, TILE)),
        ("dp", "mp"), 0, 0, tiled=True, axis_index_groups=rings,
    )
    entries = float(feature_count * width * columns)
    update = kernel_call(
        functools.partial(clip, entries), shape((TILE, width), F32), [WHOLE] * 2, name="clip"
    )(result, curvature)
    return (factor_out[None, None], inverse_out[None, None], update)


def solution(mesh):
    return jax.shard_map(
        local,
        mesh=mesh,
        in_specs=(
            P("dp", None),
            P("dp", "mp"),
            P("dp"),
            P("mp", "dp", None, None, None),
            P("mp", "dp", None, None, None),
            P(),
            P(),
        ),
        out_specs=(P("mp", "dp", None, None), P("mp", "dp", None, None), P("dp", "mp")),
        check_vma=False,
    )
```
